128 devices in a mesh: ctx: 8 (over z, y_hi), exp: 16 (over x, y_lo, core).
Axes of the slice: x: 4, y: 4 (y_hi: 2, y_lo: 2; y = y_hi * 2 + y_lo), z: 4, core: 2. Of those that a mesh axis runs over, the one named last changes fastest.
Arguments:
- queries: bfloat16 [2048, 96, 576], P('ctx', 'exp'), may hold values from -20 to 20
- latent: bfloat16 [2048, 576], P('ctx'), may hold values from -4 to 4
- block_order: int32 [16], replicated, may hold values from 0 to 15, each once
- w_uv: bfloat16 [96, 512, 128], P('exp'), may hold values from -0.75 to 0.75
- w_out: bfloat16 [12288, 7168], P('exp'), may hold values from -0.0546875 to 0.0546875
- resid: bfloat16 [2048, 7168], P(('ctx', 'exp')), may hold values from -3 to 3
- norm_gain: float32 [7168], replicated, may hold values from 0.5 to 1.5
- expert_ids: int32 [2048, 8], P(('ctx', 'exp')), may hold values from 0 to 31, all different within a row; in each aligned block of 16 rows (0 to 15, 16 to 31, ...) at most 6 rows name the same one
- route_weights: float32 [2048, 8], P(('ctx', 'exp')), may hold values from 0.1 to 0.6
- w_gate_up: bfloat16 [32, 7168, 2048], P('exp', 'ctx'), may hold values from -0.0625 to 0.0625
- w_down: bfloat16 [32, 1024, 7168], P('exp', None, 'ctx'), may hold values from -0.1875 to 0.1875
Outputs:
- layer_out: bfloat16 [2048, 7168], P(('ctx', 'exp'))
The draws below stay inside these ranges and needn't reach their ends.
Inputs may be any that keep to these rules, and one draw needn't show every extreme that they name: `block_order`: A permutation of the 16 stored blocks. `expert_ids`: A token names 8 distinct experts. Among the tokens of one device (aligned blocks of 16 stored rows), no expert is named by more than 6 of them.
All inputs are finite; a program needn't handle non-finite values.
Results may differ from the reference program's by a relative error of at most 0.029.
Values may be sent and summed in bfloat16 or wider, within the bound.
A program may use at most 128 MiB of HBM per device.

```python
import math
import jax
import jax.numpy as jnp
import numpy as np
from jax import lax

D = 7168
HEADS = 96
LAT = 512
ROPE = 64
VHEAD = 128
HID = 1024
TOPK = 8
TOK = 16
BLK = 128
SEQ = 2048
EXPERTS = 32
CAP = 6
N_CTX = 8


def draw_latent(key, part):
    key = jax.random.fold_in(key, 5)
    base_draw = jax.random.normal(key, (SEQ, LAT + ROPE), jnp.float32)
    return jnp.clip(base_draw, -4.0, 4.0).astype(jnp.bfloat16)


def draw_queries(key, part):
    key = jax.random.fold_in(key, 9)
    base_draw = jax.random.normal(key, (SEQ, HEADS, LAT + ROPE), jnp.float32)
    return jnp.clip(base_draw, -6.0, 6.0).astype(jnp.bfloat16)


def shard_levels(stream_key, shape, cuts, low, largest):
    level = 1.0
    for dim, blocks in cuts:
        steps = jax.random.uniform(jax.random.fold_in(jax.random.fold_in(stream_key, 6), dim), (blocks,), jnp.float32, low / len(cuts), largest / len(cuts))
        level = level * jnp.repeat(jnp.exp(steps), shape[dim] // blocks).reshape((-1,) + (1,) * (len(shape) - 1 - dim))
    return level


def shared_out(rng, own, number, rows, number_of, top, bound, lean):
    order = jax.random.permutation(rng, number_of)
    packed, common = load_shares(number_of, rows * top, bound, lean, True), load_shares(number_of, rows * top, bound, lean, False)
    places = jnp.arange(number_of)

    def named(sizes, turn):
        used = int((sizes > 0).sum())
        fixed = max(1, used // 4)
        moved = fixed + (places - fixed + turn * (used - fixed)) % max(1, number_of - fixed)
        return jnp.zeros((number_of,), jnp.int32).at[order[jnp.where(places < fixed, places, moved)]].set(jnp.asarray(sizes, jnp.int32))

    sizes = jnp.where(number % 4 == 0, named(packed, number // 4), named(common, number - number // 4 - 1))
    mixed = jax.random.permutation(jax.random.fold_in(own, 3), number_of)
    giver, sink = mixed[0:number_of // 2 * 2:2], mixed[1:number_of // 2 * 2:2]
    margin = jnp.minimum(sizes[giver] - 1, bound - sizes[sink]) // 2
    margin = jnp.where((giver == order[0]) | (sink == order[0]) | (sizes[sink] == 0), 0, jnp.maximum(margin, 0))
    moved = jax.random.randint(jax.random.fold_in(own, 4), (number_of // 2,), 0, 1 << 20) % (margin + 1)
    sizes = sizes.at[giver].add(-moved).at[sink].add(moved)
    members = jnp.searchsorted(jnp.cumsum(sizes), jnp.arange(rows * top), side="right").astype(jnp.int32)
    table = members.reshape(top, rows).T
    table = table[jax.random.permutation(jax.random.fold_in(own, 1), rows)]
    turn = jax.random.randint(jax.random.fold_in(own, 2), (rows, 1), 0, top)
    return jnp.take_along_axis(table, (jnp.arange(top)[None, :] + turn) % top, axis=1)


def load_shares(number_of, total, bound, lean, full):
    loads = [(1 << 20) // math.isqrt(grade ** lean) + 1 for grade in range(1, number_of + 1)]
    largest = bound if full else min(bound, max(-(-total // number_of), total * loads[0] // sum(loads)))
    least = 1 if total - largest >= number_of - 1 else 0
    given, rest = [largest] + [least] * (number_of - 1), total - largest - least * (number_of - 1)
    while rest > 0:
        movable = [i for i in range(1, number_of) if given[i] < largest] or [i for i in range(1, number_of) if given[i] < bound]
        pool, remaining = sum([loads[i] for i in movable]), rest
        for i in movable:
            more = min(bound - given[i], max(1, remaining * loads[i] // pool), rest)
            given[i] = given[i] + more
            rest = rest - more
    return np.array(given)


def bell_draw(key, dims, deviation, limit, shards=(), kind=jnp.bfloat16):
    array = deviation * jax.random.normal(key, dims, jnp.float32)
    if shards:
        array = array * shard_levels(key, dims, shards, -0.22, 0.18)
    return jnp.clip(array, -limit, limit).astype(kind)


def setup_inputs(seed: int = 0) -> dict:
    key_of = jax.random.split(jax.random.key(seed), 12)
    queries = draw_queries(jax.random.fold_in(key_of[11], 71), 0)
    latent = draw_latent(jax.random.fold_in(key_of[11], 71), 0)
    block_order = jax.random.permutation(key_of[2], 2 * N_CTX).astype(jnp.int32)
    w_uv = bell_draw(key_of[3], (HEADS, LAT, VHEAD), (LAT // 8) ** -0.5, 0.75, ((0, 16),))
    w_out = bell_draw(key_of[4], (HEADS * VHEAD, D), (HEADS * VHEAD) ** -0.5, 0.0546875, ((0, 16),))
    resid = bell_draw(key_of[5], (SEQ, D), 0.5, 3.0, ((0, 128),))
    norm_gain = jnp.clip(1.0 + 0.1 * jax.random.normal(key_of[6], (D,), jnp.float32), 0.5, 1.5)
    expert_ids_keys = jax.random.split(jax.random.fold_in(key_of[7], 1), SEQ // TOK)
    expert_ids_turns = jax.random.permutation(jax.random.fold_in(key_of[7], 3), SEQ // TOK)
    expert_ids = jax.vmap(lambda own, number: shared_out(jax.random.fold_in(key_of[7], 2), own, number, TOK, EXPERTS, TOPK, CAP, 2))(expert_ids_keys, expert_ids_turns).reshape((SEQ, TOPK))
    route_weights = jnp.clip(jnp.exp(math.log(0.6) - 1.7917595 * jax.random.uniform(key_of[8], (SEQ, TOPK), jnp.float32) ** shard_levels(key_of[8], (SEQ, TOPK), ((0, 128),), -0.2, 0.2)), 0.1, 0.6)
    w_gate_up = bell_draw(key_of[9], (EXPERTS, D, 2 * HID), D ** -0.5, 0.0625, ((0, 16), (1, 8)))
    w_down = bell_draw(key_of[10], (EXPERTS, HID, D), HID ** -0.5, 0.1875, ((0, 16), (2, 8)))
    return {"queries": queries, "latent": latent, "block_order": block_order, "w_uv": w_uv, "w_out": w_out, "resid": resid, "norm_gain": norm_gain, "expert_ids": expert_ids, "route_weights": route_weights, "w_gate_up": w_gate_up, "w_down": w_down}


def stored_positions(block_order):
    row_index = jnp.arange(SEQ, dtype=jnp.int32)
    return block_order[row_index // BLK] * BLK + row_index % BLK

def reference(queries, latent, block_order, w_uv, w_out, resid, norm_gain, expert_ids, route_weights, w_gate_up, w_down):
    positions = stored_positions(block_order)
    score_scale = (VHEAD + ROPE) ** (-0.5)
    values = latent[:, :LAT]
    block_count = SEQ // BLK

    def one_head(head_item):
        query_head, value_w = head_item

        def one_block(block_item):
            query_block, pos_block = block_item
            scores = jnp.dot(query_block, latent.T, preferred_element_type=jnp.float32) * score_scale
            visible = positions[None, :] <= pos_block[:, None]
            scores = jnp.where(visible, scores, -jnp.inf)
            row_max = lax.optimization_barrier(jnp.max(scores, axis=1))
            weights = jnp.exp(scores - row_max[:, None])
            weight_sum = lax.optimization_barrier(jnp.sum(weights, axis=1))
            context = jnp.dot(weights.astype(jnp.bfloat16), values, preferred_element_type=jnp.float32)
            context = (context / weight_sum[:, None]).astype(jnp.bfloat16)
            return jnp.dot(context, value_w, preferred_element_type=jnp.float32).astype(jnp.bfloat16)
        outputs = lax.map(one_block, (query_head.reshape(block_count, BLK, LAT + ROPE), positions.reshape(block_count, BLK)))
        return outputs.reshape(SEQ, VHEAD)
    heads_out = lax.map(one_head, (jnp.transpose(queries, (1, 0, 2)), w_uv))
    flat_heads = jnp.transpose(heads_out, (1, 0, 2)).reshape(SEQ, HEADS * VHEAD)
    attention = jnp.dot(flat_heads, w_out, preferred_element_type=jnp.float32)
    layer_state = resid.astype(jnp.float32) + attention
    normed = (layer_state * lax.rsqrt(lax.optimization_barrier(jnp.mean(layer_state * layer_state, axis=1, keepdims=True)) + 1e-06) * norm_gain).astype(jnp.bfloat16)
    dev_blocks = SEQ // TOK
    ids_blocks = expert_ids.reshape(dev_blocks, TOK * TOPK)
    one_hot = (ids_blocks[:, :, None] == jnp.arange(EXPERTS, dtype=jnp.int32)[None, None, :]).astype(jnp.int32)
    slot_ids = lax.optimization_barrier(jnp.sum((jnp.cumsum(one_hot, axis=1) - one_hot) * one_hot, axis=2))
    token_ids = (jnp.arange(SEQ * TOPK, dtype=jnp.int32) // TOPK).reshape(dev_blocks, TOK * TOPK)
    block_ids = jnp.broadcast_to(jnp.arange(dev_blocks, dtype=jnp.int32)[:, None], (dev_blocks, TOK * TOPK))
    slot_table = jnp.full((EXPERTS, dev_blocks, CAP), SEQ, jnp.int32).at[ids_blocks, block_ids, slot_ids].set(token_ids)
    weight_table = jnp.zeros((EXPERTS, dev_blocks, CAP), jnp.float32).at[ids_blocks, block_ids, slot_ids].set(route_weights.reshape(dev_blocks, TOK * TOPK))
    padded = jnp.concatenate([normed, jnp.zeros((1, D), jnp.bfloat16)], axis=0)
    slice_width = D // N_CTX

    def expert_step(moe_sum, expert_item):
        token_slots, slot_weights, gate_up_w, down_w = expert_item
        flat_slots = token_slots.reshape(-1)
        gathered = padded[flat_slots]
        gate_up = jnp.zeros((gathered.shape[0], 2 * HID), jnp.float32)
        for slice_idx in range(N_CTX):
            lower = slice_idx * slice_width
            partial_value = jnp.dot(gathered[:, lower:lower + slice_width], gate_up_w[lower:lower + slice_width], preferred_element_type=jnp.float32)
            partial_value = lax.optimization_barrier(partial_value.astype(jnp.bfloat16)).astype(jnp.float32)
            gate_up = gate_up + partial_value
        activated = (jax.nn.silu(gate_up[:, :HID]) * gate_up[:, HID:]).astype(jnp.bfloat16)
        expert_out = jnp.dot(activated, down_w, preferred_element_type=jnp.float32).astype(jnp.bfloat16)
        expert_out = lax.optimization_barrier(expert_out).astype(jnp.float32)
        moe_sum = moe_sum.at[flat_slots].add(slot_weights.reshape(-1)[:, None] * expert_out)
        return (moe_sum, None)
    moe_sum, unused = lax.scan(expert_step, jnp.zeros((SEQ + 1, D), jnp.float32), (slot_table, weight_table, w_gate_up, w_down))
    return (layer_state + moe_sum[:SEQ]).astype(jnp.bfloat16)
```

```python
import functools

import jax
import jax.numpy as jnp
from jax import lax
from jax.experimental import pallas as pl
from jax.experimental.pallas import tpu as pltpu
from jax.sharding import PartitionSpec as P

BF = jnp.bfloat16
F32 = jnp.float32
DMA = pltpu.SemaphoreType.DMA
W = 896


def place():
    c = lax.axis_index("ctx")
    e = lax.axis_index("exp")
    return c // 2, c % 2, e // 4, (e // 2) % 2, e % 2


def dev(z, yh, x, yl, co):
    return (z * 2 + yh, x * 4 + yl * 2 + co)


def put(src, dst, ss, rs, device):
    return pltpu.make_async_remote_copy(
        src_ref=src,
        dst_ref=dst,
        send_sem=ss,
        recv_sem=rs,
        device_id=device,
        device_id_type=pl.DeviceIdType.MESH,
    )


def greet(devices):
    barrier = pltpu.get_barrier_semaphore()
    for d in devices:
        pl.semaphore_signal(barrier, inc=1, device_id=d, device_id_type=pl.DeviceIdType.MESH)
    pl.semaphore_wait(barrier, len(devices))


def exp_peers(pos):
    z, yh, x, yl, co = pos
    core = dev(z, yh, x, yl, (co + 1) % 2)
    ylp = dev(z, yh, x, (yl + 1) % 2, co)
    xs = [dev(z, yh, (x + d) % 4, yl, co) for d in (1, 2, 3)]
    return core, ylp, xs


REDUCE_SCRATCH = [
    pltpu.VMEM((8, 4, 2, 16, W), F32),
    pltpu.VMEM((8, 4, 2, 16, W), BF),
    pltpu.VMEM((8, 4, 2, 16, W), BF),
    pltpu.VMEM((8, 4, 2, 16, W), BF),
    pltpu.VMEM((4, 3, 2, 16, W), BF),
    pltpu.VMEM((4, 4, 16, W), BF),
    pltpu.VMEM((4, 16, W), BF),
    pltpu.VMEM((4, 3, 16, W), BF),
    pltpu.VMEM((4, 16, W), BF),
    pltpu.VMEM((4, 3, 16, W), BF),
    pltpu.VMEM((8, 16, W), F32),
    DMA((8,)),
    DMA((8,)),
    DMA((4, 3)),
    DMA((4, 3)),
    DMA((4,)),
    DMA((4,)),
    DMA((4,)),
    DMA((4,)),
    DMA((4, 3)),
    DMA((4, 3)),
]


class Reduce:
    def __init__(self, refs, pos):
        (self.own, self.cs, self.cl, self.s1, self.x1, self.y1, self.y2s, self.x2s, self.y2,
         self.x2, self.acc, *self.sems) = refs
        self.pos = pos
        self.core, self.ylp, self.xs = exp_peers(pos)

    def c_core(self, n):
        return put(self.cs.at[n], self.cl.at[n], self.sems[0].at[n], self.sems[1].at[n], self.core)

    def c_x1(self, i, d):
        xx = (self.pos[2] + d) % 4
        return put(self.s1.at[2 * i, xx], self.x1.at[i, d - 1], self.sems[2].at[i, d - 1],
                   self.sems[3].at[i, d - 1], self.xs[d - 1])

    def c_y1(self, i):
        return put(self.s1.at[2 * i + 1, :, (self.pos[3] + 1) % 2], self.y1.at[i], self.sems[4].at[i],
                   self.sems[5].at[i], self.ylp)

    def c_y2(self, i):
        return put(self.y2s.at[i], self.y2.at[i], self.sems[6].at[i], self.sems[7].at[i], self.ylp)

    def c_x2(self, i, d):
        return put(self.x2s.at[i, d - 1], self.x2.at[i, d - 1], self.sems[8].at[i, d - 1],
                   self.sems[9].at[i, d - 1], self.xs[d - 1])

    def chip_sum(self, n):
        self.c_core(n).wait_recv()
        self.s1[n] = (self.own[n] + self.cl[n].astype(F32)).astype(BF)

    def first(self, i):
        self.chip_sum(2 * i)
        for d in (1, 2, 3):
            self.c_x1(i, d).start()
        self.chip_sum(2 * i + 1)
        self.c_y1(i).start()

    def second(self, i):
        x, yl = self.pos[2], self.pos[3]
        yo = (yl + 1) % 2
        for d in (1, 2, 3):
            self.c_x1(i, d).wait_recv()

        def over_x(which):
            t = self.s1[2 * i, x, which].astype(F32)
            for d in (0, 1, 2):
                t = t + self.x1[i, d, which].astype(F32)
            return t

        self.y2s[i] = over_x(yo).astype(BF)
        self.c_y2(i).start()
        self.acc[2 * i] = over_x(yl)
        self.c_y1(i).wait_recv()
        for d in (1, 2, 3):
            xx = (x + d) % 4
            t = self.s1[2 * i + 1, xx, yl].astype(F32) + self.y1[i, xx].astype(F32)
            self.x2s[i, d - 1] = t.astype(BF)
            self.c_x2(i, d).start()
        self.acc[2 * i + 1] = self.s1[2 * i + 1, x, yl].astype(F32) + self.y1[i, x].astype(F32)

    def third(self, i):
        self.c_y2(i).wait_recv()
        self.acc[2 * i] = self.acc[2 * i] + self.y2[i].astype(F32)
        t = self.acc[2 * i + 1]
        for d in (1, 2, 3):
            self.c_x2(i, d).wait_recv()
            t = t + self.x2[i, d - 1].astype(F32)
        self.acc[2 * i + 1] = t

    def drain(self, i):
        self.c_core(2 * i).wait_send()
        self.c_core(2 * i + 1).wait_send()
        self.c_y1(i).wait_send()
        self.c_y2(i).wait_send()
        for d in (1, 2, 3):
            self.c_x1(i, d).wait_send()
            self.c_x2(i, d).wait_send()


def loop(count, step):
    def body(k, carry):
        step(k)
        return carry

    lax.fori_loop(0, count, body, 0)


def when(cond):
    return pl.when(cond)


def project_kernel(heads, w_hbm, resid, gain, state, normed, w, wsem, *reduce_refs):
    pos = place()
    core, ylp, xs = exp_peers(pos)

    def load(n):
        return pltpu.make_async_copy(
            w_hbm.at[:, pl.ds(pl.multiple_of(n * W, W), W)], w.at[n], wsem.at[n]
        )

    loop(8, lambda n: load(n).start())
    greet([core, ylp] + xs)
    red = Reduce(reduce_refs, pos)

    def multiply(n):
        load(n).wait()
        t = jnp.dot(heads[...], w[n], preferred_element_type=F32)
        red.cs[n] = t[:128].astype(BF).reshape(4, 2, 16, W)
        red.c_core(n).start()
        red.own[n] = t[128:].reshape(4, 2, 16, W)

    def step(k):
        @when(k < 4)
        def _():
            multiply(2 * k)
            multiply(2 * k + 1)

        @when((k >= 1) & (k < 5))
        def _():
            red.first(k - 1)

        @when((k >= 2) & (k < 6))
        def _():
            red.second(k - 2)

        @when(k >= 3)
        def _():
            red.third(k - 3)

    loop(7, step)
    square = jnp.zeros((16, 1), F32)
    for n in range(8):
        t = resid[:, n * W:(n + 1) * W].astype(F32) + red.acc[n]
        state[n] = t
        square = square + jnp.sum(t * t, axis=1, keepdims=True)
    scale = lax.rsqrt(square / (8 * W) + 1e-06)
    for n in range(8):
        normed[n] = (state[n] * scale * gain[:, n * W:(n + 1) * W]).astype(BF)
    loop(4, red.drain)


def experts_kernel(normed, slots, weights, state, wg_hbm, wd_hbm, out,
                   wg, wd, wsem, xb, rows, abuf, la, bbuf, bown, lb1, b2, lb2, a2, la2, suma,
                   acta, actb, yrow, tbuf, fin, ret, sems, *reduce_refs):
    pos = place()
    z, yh, x, yl, co = pos
    me = z * 2 + yh
    core, ylp, xs = exp_peers(pos)
    yo = (yl + 1) % 2
    yp = dev(z, (yh + 1) % 2, x, yl, co)
    zs = [dev((z + d) % 4, yh, x, yl, co) for d in (1, 2, 3)]
    red = Reduce(reduce_refs, pos)
    (s_in, r_in, s_g1x, r_g1x, s_g1y, r_g1y, s_g2y, r_g2y, s_g2x, r_g2x, s_gc, r_gc,
     s_a1, r_a1, s_b1, r_b1, s_b2, r_b2, s_a2, r_a2, s_ay, r_ay, s_az, r_az, s_bz, r_bz, s_by, r_by,
     s_f, r_f) = sems

    loads = [
        pltpu.make_async_copy(wg_hbm.at[0], wg.at[0], wsem.at[0]),
        pltpu.make_async_copy(wg_hbm.at[1], wg.at[1], wsem.at[1]),
        pltpu.make_async_copy(wd_hbm, wd, wsem.at[2]),
    ]
    for cp in loads:
        cp.start()
    ctx = [dev((z + dz) % 4, (yh + dy) % 2, x, yl, co) for dz in range(4) for dy in range(2) if dz or dy]
    greet([core, ylp] + xs + ctx)

    def chunk(dz, dy):
        return ((z + 4 - dz) % 4) * 2 + (yh + dy) % 2

    def c_in(dz, dy):
        zz, yy = (z + dz) % 4, (yh + dy) % 2
        r = dz * 2 + dy
        return put(normed.at[zz * 2 + yy], xb.at[me, co, x, yl], s_in.at[r], r_in.at[r],
                   dev(zz, yy, x, yl, co))

    for dz in (1, 2, 3, 0):
        for dy in range(2):
            if dz or dy:
                c_in(dz, dy).start()
    xb[me, co, x, yl] = normed[me]

    def c_g1x(dz, d):
        c = chunk(dz, 0)
        return put(xb.at[c, co, x, yl], xb.at[c, co, x, yl], s_g1x.at[dz, d - 1], r_g1x.at[dz, d - 1], xs[d - 1])

    def c_g2y(dz):
        c = chunk(dz, 0)
        return put(xb.at[c, co, :, yl], xb.at[c, co, :, yl], s_g2y.at[dz], r_g2y.at[dz], ylp)

    def c_g1y(dz):
        c = chunk(dz, 1)
        return put(xb.at[c, co, x, yl], xb.at[c, co, x, yl], s_g1y.at[dz], r_g1y.at[dz], ylp)

    def c_g2x(dz, d):
        c = chunk(dz, 1)
        return put(xb.at[c, co, x], xb.at[c, co, x], s_g2x.at[dz, d - 1], r_g2x.at[dz, d - 1], xs[d - 1])

    def c_gc(dz, dy):
        c = chunk(dz, dy)
        return put(xb.at[c, co], xb.at[c, co], s_gc.at[dz, dy], r_gc.at[dz, dy], core)

    def gather1(dz):
        @when(dz > 0)
        def _():
            c_in(dz, 0).wait_recv()
        for d in (1, 2, 3):
            c_g1x(dz, d).start()
        c_in(dz, 1).wait_recv()
        c_g1y(dz).start()

    def gather2(dz):
        for d in (1, 2, 3):
            c_g1x(dz, d).wait_recv()
        c_g2y(dz).start()
        c_g1y(dz).wait_recv()
        for d in (1, 2, 3):
            c_g2x(dz, d).start()

    def gather3(dz):
        c_g2y(dz).wait_recv()
        c_gc(dz, 0).start()
        for d in (1, 2, 3):
            c_g2x(dz, d).wait_recv()
        c_gc(dz, 1).start()

    def c_a1(dz, d):
        return put(abuf.at[dz], la.at[d - 1], s_a1.at[d - 1], r_a1.at[d - 1],
                   dev((z + 4 - d) % 4, yh, x, yl, co))

    def c_b1(dz):
        return put(bbuf.at[dz], lb1.at[dz], s_b1.at[dz], r_b1.at[dz], yp)

    def c_b2(dz):
        return put(b2.at[dz], lb2.at[dz], s_b2.at[dz], r_b2.at[dz], dev((z + 4 - dz) % 4, yh, x, yl, co))

    row_id = lax.broadcasted_iota(jnp.int32, (96, 256), 0)

    def gate_up(dz):
        for dy in range(2):
            c_gc(dz, dy).wait_recv()
            c = chunk(dz, dy)
            tokens = xb[c].reshape(256, W)
            for i in range(2):
                pick = (row_id == slots[c, i:i + 1, :]).astype(BF)
                rows[i, dy * 96:(dy + 1) * 96] = jnp.dot(pick, tokens, preferred_element_type=F32).astype(BF)

        def cols(t):
            sl = pl.ds(pl.multiple_of(t * 512, 512), 512)
            r = jnp.dot(rows[0], wg[0, :, sl], preferred_element_type=F32).astype(BF)
            abuf[dz, :, :, sl] = r.reshape(2, 96, 512)

        loop(4, cols)

        for d in (1, 2, 3):
            @when(dz == d)
            def _():
                c_a1(d, d).start()

        def cols(t):
            sl = pl.ds(pl.multiple_of(t * 512, 512), 512)
            r = jnp.dot(rows[1], wg[1, :, sl], preferred_element_type=F32).astype(BF)
            bown[dz, :, sl] = r[:96]
            bbuf[dz, :, sl] = r[96:]

        loop(4, cols)
        c_b1(dz).start()

    def forward_b(dz):
        c_b1(dz).wait_recv()

        def cols(t):
            sl = pl.ds(pl.multiple_of(t * 512, 512), 512)
            b2[dz, :, sl] = (bown[dz, :, sl].astype(F32) + lb1[dz, :, sl].astype(F32)).astype(BF)

        loop(4, cols)

        @when(dz > 0)
        def _():
            c_b2(dz).start()

    def order(k):
        return (k + 1) % 4

    def step(k):
        @when(k < 4)
        def _():
            gather1(order(k))

        @when((k >= 1) & (k < 5))
        def _():
            gather2(order(k - 1))

        @when((k >= 2) & (k < 6))
        def _():
            gather3(order(k - 2))

        @when(k == 3)
        def _():
            loads[0].wait()
            loads[1].wait()

        @when((k >= 3) & (k < 7))
        def _():
            gate_up(order(k - 3))

        @when(k >= 5)
        def _():
            forward_b(order(k - 5))

    loop(9, step)

    for d in (1, 2, 3):
        c_a1(d, d).wait_recv()

    def cols(t):
        sl = pl.ds(pl.multiple_of(t * 256, 256), 256)

        def total(dy):
            r = abuf[0, dy, :, sl].astype(F32)
            for d in range(3):
                r = r + la[d, dy, :, sl].astype(F32)
            return r

        a2[:, sl] = total(1).astype(BF)
        suma[:, sl] = total(0)

    loop(8, cols)
    c_a2 = put(a2, la2, s_a2, r_a2, yp)
    c_a2.start()

    def activate(gate, up):
        return (gate / (1.0 + jnp.exp(-gate)) * up).astype(BF)

    c_a2.wait_recv()

    def cols(t):
        lo = pl.ds(pl.multiple_of(t * 256, 256), 256)
        hi = pl.ds(pl.multiple_of(t * 256 + 1024, 256), 256)
        acta[z, yh, :, lo] = activate(suma[:, lo] + la2[:, lo].astype(F32), suma[:, hi] + la2[:, hi].astype(F32))

    loop(4, cols)
    c_ay = put(acta.at[z, yh], acta.at[z, yh], s_ay, r_ay, yp)
    c_ay.start()

    def c_az(d):
        return put(acta.at[z], acta.at[z], s_az.at[d - 1], r_az.at[d - 1], zs[d - 1])

    def c_bz(d):
        return put(actb.at[z, yh], actb.at[z, yh], s_bz.at[d - 1], r_bz.at[d - 1], zs[d - 1])

    def c_by(dz):
        zz = (z + 4 - dz) % 4
        return put(actb.at[zz, yh], actb.at[zz, yh], s_by.at[dz], r_by.at[dz], yp)

    c_ay.wait_recv()
    for d in (1, 2, 3):
        c_az(d).start()

    for d in (1, 2, 3):
        c_b2(d).wait_recv()

    def cols(t):
        lo = pl.ds(pl.multiple_of(t * 256, 256), 256)
        hi = pl.ds(pl.multiple_of(t * 256 + 1024, 256), 256)

        def total(sl):
            r = b2[0, :, sl].astype(F32)
            for d in (1, 2, 3):
                r = r + lb2[d, :, sl].astype(F32)
            return r

        actb[z, yh, :, lo] = activate(total(lo), total(hi))

    loop(4, cols)
    for d in (1, 2, 3):
        c_bz(d).start()
    loads[2].wait()

    def pass_on(dz):
        for d in (1, 2, 3):
            @when(dz == d)
            def _():
                c_bz(d).wait_recv()
        c_by(dz).start()

    def down(dz):
        zz = (z + 4 - dz) % 4
        for d in (1, 2, 3):
            @when(dz == d)
            def _():
                c_az(d).wait_recv()
        c_by(dz).wait_recv()
        yrow[0] = jnp.dot(acta[zz].reshape(192, 1024), wd[0], preferred_element_type=F32).astype(BF)
        yrow[1] = jnp.dot(actb[zz].reshape(192, 1024), wd[1], preferred_element_type=F32).astype(BF)
        for dy in range(2):
            yy = (yh + dy) % 2
            c = zz * 2 + yy
            t = jnp.zeros((256, W), F32)
            for i in range(2):
                pick = jnp.where(row_id == slots[c, i:i + 1, :], weights[c, i:i + 1, :], 0.0).astype(BF)
                t = t + lax.dot_general(
                    pick, yrow[i, pl.ds(pl.multiple_of(yy * 96, 96), 96)], (((0,), (0,)), ((), ())),
                    preferred_element_type=F32)
            tbuf[...] = t.reshape(2, 4, 2, 16, W)
            n = dz * 2 + dy
            red.cs[n] = tbuf[(co + 1) % 2].astype(BF)
            red.c_core(n).start()
            red.own[n] = tbuf[co]

    def c_f(dz, dy):
        c = chunk(dz, dy)
        r = dz * 2 + dy
        return put(fin.at[r], ret.at[me], s_f.at[r], r_f.at[r],
                   dev((z + 4 - dz) % 4, (yh + dy) % 2, x, yl, co))

    def send_back(dz):
        red.third(dz)
        for dy in range(2):
            n = dz * 2 + dy
            fin[n] = red.acc[n].astype(BF)
            if dy:
                c_f(dz, dy).start()
            else:
                @when(dz > 0)
                def _():
                    c_f(dz, dy).start()

    def step(k):
        @when(k < 4)
        def _():
            pass_on(k)

        @when((k >= 1) & (k < 5))
        def _():
            down(k - 1)

        @when((k >= 2) & (k < 6))
        def _():
            red.first(k - 2)

        @when((k >= 3) & (k < 7))
        def _():
            red.second(k - 3)

        @when(k >= 4)
        def _():
            send_back(k - 4)

    loop(8, step)
    ret[me] = fin[0]
    for r in range(1, 8):
        c_f(r // 2, r % 2).wait_recv()
    for n in range(8):
        out[:, n * W:(n + 1) * W] = (state[n] + ret[n].astype(F32)).astype(BF)

    loop(4, red.drain)
    for r in range(1, 8):
        c_f(r // 2, r % 2).wait_send()
        c_in(r // 2, r % 2).wait_send()
    for dz in range(4):
        for d in (1, 2, 3):
            c_g1x(dz, d).wait_send()
            c_g2x(dz, d).wait_send()
        c_g1y(dz).wait_send()
        c_g2y(dz).wait_send()
        c_gc(dz, 0).wait_send()
        c_gc(dz, 1).wait_send()
        c_b1(dz).wait_send()
        c_by(dz).wait_send()
    for d in (1, 2, 3):
        c_a1(d, d).wait_send()
        c_b2(d).wait_send()
        c_az(d).wait_send()
        c_bz(d).wait_send()
    c_a2.wait_send()
    c_ay.wait_send()


VM = pl.BlockSpec(memory_space=pltpu.VMEM)
ANY = pl.BlockSpec(memory_space=pl.ANY)


def project(heads, w_out, resid, gain):
    return pl.pallas_call(
        project_kernel,
        name="project",
        out_shape=(jax.ShapeDtypeStruct((8, 16, W), F32), jax.ShapeDtypeStruct((8, 16, W), BF)),
        in_specs=[VM, ANY, VM, VM],
        out_specs=(VM, VM),
        scratch_shapes=[pltpu.VMEM((8, 768, W), BF), DMA((8,))] + REDUCE_SCRATCH,
        compiler_params=pltpu.CompilerParams(
            collective_id=1, has_side_effects=True, vmem_limit_bytes=50 << 20),
    )(heads, w_out, resid, gain)


def experts(normed, slots, weights, state, w_gate_up, w_down):
    hid2 = w_gate_up.shape[2]
    hid = hid2 // 2
    sems = [
        DMA((8,)), DMA((8,)),
        DMA((4, 3)), DMA((4, 3)), DMA((4,)), DMA((4,)), DMA((4,)), DMA((4,)), DMA((4, 3)), DMA((4, 3)),
        DMA((4, 2)), DMA((4, 2)),
        DMA((3,)), DMA((3,)), DMA((4,)), DMA((4,)), DMA((4,)), DMA((4,)), DMA, DMA,
        DMA, DMA, DMA((3,)), DMA((3,)), DMA((3,)), DMA((3,)), DMA((4,)), DMA((4,)),
        DMA((8,)), DMA((8,)),
    ]
    return pl.pallas_call(
        experts_kernel,
        name="experts",
        out_shape=jax.ShapeDtypeStruct((16, 8 * W), BF),
        in_specs=[VM, VM, VM, VM, ANY, ANY],
        out_specs=VM,
        scratch_shapes=[
            pltpu.VMEM((2, W, hid2), BF),
            pltpu.VMEM((2, hid, W), BF),
            DMA((3,)),
            pltpu.VMEM((8, 2, 4, 2, 16, W), BF),
            pltpu.VMEM((2, 192, W), BF),
            pltpu.VMEM((4, 2, 96, hid2), BF),
            pltpu.VMEM((3, 2, 96, hid2), BF),
            pltpu.VMEM((4, 96, hid2), BF),
            pltpu.VMEM((4, 96, hid2), BF),
            pltpu.VMEM((4, 96, hid2), BF),
            pltpu.VMEM((4, 96, hid2), BF),
            pltpu.VMEM((4, 96, hid2), BF),
            pltpu.VMEM((96, hid2), BF),
            pltpu.VMEM((96, hid2), BF),
            pltpu.VMEM((96, hid2), F32),
            pltpu.VMEM((4, 2, 96, hid), BF),
            pltpu.VMEM((4, 2, 96, hid), BF),
            pltpu.VMEM((2, 192, W), BF),
            pltpu.VMEM((2, 4, 2, 16, W), F32),
            pltpu.VMEM((8, 16, W), BF),
            pltpu.VMEM((8, 16, W), BF),
            tuple(sems),
        ] + REDUCE_SCRATCH,
        compiler_params=pltpu.CompilerParams(
            collective_id=2, has_side_effects=True, vmem_limit_bytes=62 << 20),
    )(normed, slots, weights, state, w_gate_up, w_down)


def routing(expert_ids, route_weights):
    e = lax.axis_index("exp")
    both = jnp.concatenate([expert_ids.astype(F32), route_weights], axis=1)
    every = lax.all_gather(both, ("ctx", "exp"), axis=0, tiled=True)
    mine = (2 * e + jnp.arange(2)).astype(F32)
    match = every[None, :, :8] == mine[:, None, None]
    hit = jnp.any(match, axis=2)
    weight = jnp.sum(jnp.where(match, every[None, :, 8:], 0.0), axis=2)
    hit = hit.reshape(2, 8, 4, 2, 2, 16)
    before = jnp.arange(16)[:, None] > jnp.arange(16)[None, :]
    rank = jnp.sum(jnp.where(before & hit[..., None, :], 1, 0), axis=-1)
    hit, rank, weight = (
        jnp.transpose(t.reshape(2, 8, 4, 2, 2, 16), (1, 0, 4, 2, 3, 5)).reshape(8, 2, 16, 16)
        for t in (hit, rank, weight)
    )
    slot = jnp.where(hit, jnp.arange(16)[:, None] * 6 + rank, -1)
    return slot.reshape(8, 2, 256).astype(jnp.int32), weight.reshape(8, 2, 256)


def attend(queries, latent, block_order, w_uv):
    query_count, heads_dev, feat_width = queries.shape
    lat_width = w_uv.shape[1]
    value_width = w_uv.shape[2]
    block_len = query_count // 2
    stored_blocks = block_order.shape[0]
    score_scale = (value_width + feat_width - lat_width) ** (-0.5)
    ctx_rank = lax.axis_index("ctx")

    def seq_positions(first_row, count):
        row_ids = first_row + jnp.arange(count, dtype=jnp.int32)
        block_ids = row_ids // block_len
        match = block_ids[:, None] == jnp.arange(stored_blocks, dtype=jnp.int32)[None, :]
        block_pos = jnp.sum(jnp.where(match, block_order[None, :], 0), axis=1)
        return block_pos * block_len + row_ids % block_len

    query_pos = seq_positions(ctx_rank * query_count, query_count)
    query_rows = queries.reshape(query_count * heads_dev, feat_width)
    query_pos_rows = jnp.repeat(query_pos, heads_dev)
    keys = lax.all_gather(latent, "ctx", axis=0, tiled=True)
    key_pos = seq_positions(jnp.int32(0), keys.shape[0])
    scores = (
        lax.dot_general(query_rows, keys, (((1,), (1,)), ((), ())), preferred_element_type=F32) * score_scale
    )
    scores = jnp.where(key_pos[None, :] <= query_pos_rows[:, None], scores, -jnp.inf)
    weights = jnp.exp(scores - jnp.max(scores, axis=1)[:, None])
    value_sum = jnp.dot(weights.astype(BF), keys[:, :lat_width], preferred_element_type=F32)
    weight_sum = jnp.sum(weights, axis=1)
    context = (value_sum / weight_sum[:, None]).astype(BF).reshape(query_count, heads_dev, lat_width)
    head_out = jnp.einsum("shl,hlv->shv", context, w_uv, preferred_element_type=F32).astype(BF)
    return head_out.reshape(query_count, heads_dev * value_width)


def body(queries, latent, block_order, w_uv, w_out, resid, norm_gain, expert_ids, route_weights, w_gate_up, w_down):
    slots, weights = routing(expert_ids, route_weights)
    head_out = attend(queries, latent, block_order, w_uv)
    by_core = head_out.reshape(8, 2, 16, -1).transpose(1, 0, 2, 3)
    by_core = jnp.where(lax.axis_index("exp") % 2 == 0, by_core[::-1], by_core).reshape(256, -1)
    state, normed = project(by_core, w_out, resid, norm_gain.reshape(1, -1))
    return experts(normed, slots, weights, state, w_gate_up, w_down)


def solution(mesh):
    return jax.shard_map(
        body,
        mesh=mesh,
        in_specs=(
            P("ctx", "exp", None),
            P("ctx", None),
            P(),
            P("exp", None, None),
            P("exp", None),
            P(("ctx", "exp"), None),
            P(),
            P(("ctx", "exp"), None),
            P(("ctx", "exp"), None),
            P("exp", "ctx", None),
            P("exp", None, "ctx"),
        ),
        out_specs=P(("ctx", "exp"), None),
        check_vma=False,
    )
```

```python
import functools

import jax
import jax.numpy as jnp
from jax import lax
from jax.experimental import pallas as pl
from jax.experimental.pallas import tpu as pltpu
from jax.sharding import PartitionSpec as P

BF = jnp.bfloat16
F32 = jnp.float32
DMA = pltpu.SemaphoreType.DMA
W = 896


def place():
    c = lax.axis_index("ctx")
    e = lax.axis_index("exp")
    return c // 2, c % 2, e // 4, (e // 2) % 2, e % 2


def dev(z, yh, x, yl, co):
    return (z * 2 + yh, x * 4 + yl * 2 + co)


def put(src, dst, ss, rs, device):
    return pltpu.make_async_remote_copy(
        src_ref=src,
        dst_ref=dst,
        send_sem=ss,
        recv_sem=rs,
        device_id=device,
        device_id_type=pl.DeviceIdType.MESH,
    )


def greet(devices):
    barrier = pltpu.get_barrier_semaphore()
    for d in devices:
        pl.semaphore_signal(barrier, inc=1, device_id=d, device_id_type=pl.DeviceIdType.MESH)
    pl.semaphore_wait(barrier, len(devices))


def exp_peers(pos):
    z, yh, x, yl, co = pos
    core = dev(z, yh, x, yl, (co + 1) % 2)
    ylp = dev(z, yh, x, (yl + 1) % 2, co)
    xs = [dev(z, yh, (x + d) % 4, yl, co) for d in (1, 2, 3)]
    return core, ylp, xs


REDUCE_SCRATCH = [
    pltpu.VMEM((8, 4, 2, 16, W), F32),
    pltpu.VMEM((8, 4, 2, 16, W), BF),
    pltpu.VMEM((8, 4, 2, 16, W), BF),
    pltpu.VMEM((8, 4, 2, 16, W), BF),
    pltpu.VMEM((4, 3, 2, 16, W), BF),
    pltpu.VMEM((4, 4, 16, W), BF),
    pltpu.VMEM((4, 16, W), BF),
    pltpu.VMEM((4, 3, 16, W), BF),
    pltpu.VMEM((4, 16, W), BF),
    pltpu.VMEM((4, 3, 16, W), BF),
    pltpu.VMEM((8, 16, W), F32),
    DMA((8,)),
    DMA((8,)),
    DMA((4, 3)),
    DMA((4, 3)),
    DMA((4,)),
    DMA((4,)),
    DMA((4,)),
    DMA((4,)),
    DMA((4, 3)),
    DMA((4, 3)),
]


class Reduce:
    def __init__(self, refs, pos):
        (self.own, self.cs, self.cl, self.s1, self.x1, self.y1, self.y2s, self.x2s, self.y2,
         self.x2, self.acc, *self.sems) = refs
        self.pos = pos
        self.core, self.ylp, self.xs = exp_peers(pos)

    def c_core(self, n):
        return put(self.cs.at[n], self.cl.at[n], self.sems[0].at[n], self.sems[1].at[n], self.core)

    def c_x1(self, i, d):
        xx = (self.pos[2] + d) % 4
        return put(self.s1.at[2 * i, xx], self.x1.at[i, d - 1], self.sems[2].at[i, d - 1],
                   self.sems[3].at[i, d - 1], self.xs[d - 1])

    def c_y1(self, i):
        return put(self.s1.at[2 * i + 1, :, (self.pos[3] + 1) % 2], self.y1.at[i], self.sems[4].at[i],
                   self.sems[5].at[i], self.ylp)

    def c_y2(self, i):
        return put(self.y2s.at[i], self.y2.at[i], self.sems[6].at[i], self.sems[7].at[i], self.ylp)

    def c_x2(self, i, d):
        return put(self.x2s.at[i, d - 1], self.x2.at[i, d - 1], self.sems[8].at[i, d - 1],
                   self.sems[9].at[i, d - 1], self.xs[d - 1])

    def chip_sum(self, n):
        self.c_core(n).wait_recv()
        self.s1[n] = (self.own[n] + self.cl[n].astype(F32)).astype(BF)

    def first(self, i):
        self.chip_sum(2 * i)
        for d in (1, 2, 3):
            self.c_x1(i, d).start()
        self.chip_sum(2 * i + 1)
        self.c_y1(i).start()

    def second(self, i):
        x, yl = self.pos[2], self.pos[3]
        yo = (yl + 1) % 2
        for d in (1, 2, 3):
            self.c_x1(i, d).wait_recv()

        def over_x(which):
            t = self.s1[2 * i, x, which].astype(F32)
            for d in (0, 1, 2):
                t = t + self.x1[i, d, which].astype(F32)
            return t

        self.y2s[i] = over_x(yo).astype(BF)
        self.c_y2(i).start()
        self.acc[2 * i] = over_x(yl)
        self.c_y1(i).wait_recv()
        for d in (1, 2, 3):
            xx = (x + d) % 4
            t = self.s1[2 * i + 1, xx, yl].astype(F32) + self.y1[i, xx].astype(F32)
            self.x2s[i, d - 1] = t.astype(BF)
            self.c_x2(i, d).start()
        self.acc[2 * i + 1] = self.s1[2 * i + 1, x, yl].astype(F32) + self.y1[i, x].astype(F32)

    def third(self, i):
        self.c_y2(i).wait_recv()
        self.acc[2 * i] = self.acc[2 * i] + self.y2[i].astype(F32)
        t = self.acc[2 * i + 1]
        for d in (1, 2, 3):
            self.c_x2(i, d).wait_recv()
            t = t + self.x2[i, d - 1].astype(F32)
        self.acc[2 * i + 1] = t

    def drain(self, i):
        self.c_core(2 * i).wait_send()
        self.c_core(2 * i + 1).wait_send()
        self.c_y1(i).wait_send()
        self.c_y2(i).wait_send()
        for d in (1, 2, 3):
            self.c_x1(i, d).wait_send()
            self.c_x2(i, d).wait_send()


def loop(count, step):
    def body(k, carry):
        step(k)
        return carry

    lax.fori_loop(0, count, body, 0)


def when(cond):
    return pl.when(cond)


def attend_kernel(scale, queries, latent, query_pos, key_pos, w_uv, routes, out, table,
                  kb, top, total, value, s_in, r_in, s_c, r_c,
                  s_tx, r_tx, s_ty, r_ty, s_tc, r_tc, s_tz, r_tz, s_th, r_th):
    pos = place()
    z, yh, x, yl, co = pos
    me = z * 2 + yh
    core, ylp, xs = exp_peers(pos)
    yp = dev(z, (yh + 1) % 2, x, yl, co)
    zs = [dev((z + d) % 4, yh, x, yl, co) for d in (1, 2, 3)]
    greet([core, ylp] + xs + [dev((z + dz) % 4, (yh + dy) % 2, x, yl, co)
                              for dz in range(4) for dy in range(2) if dz or dy])

    def c_in(dz, dy):
        r = dz * 2 + dy
        return put(latent.at[pl.ds(pl.multiple_of(co * 128, 128), 128)], kb.at[me, co], s_in.at[r], r_in.at[r],
                   dev((z + dz) % 4, (yh + dy) % 2, x, yl, co))

    def chunk(r):
        return ((z + 4 - r // 2) % 4) * 2 + (yh + r) % 2

    def c_core(r):
        c = chunk(r)
        return put(kb.at[c, co], kb.at[c, co], s_c.at[r], r_c.at[r], core)

    for r in range(1, 8):
        c_in(r // 2, r % 2).start()
    kb[me] = latent[...].reshape(kb.shape[1:])

    table[z, yh, co, x, yl] = routes[...]

    def t_x(d):
        part = table.at[z, yh, co, x, yl]
        return put(part, part, s_tx.at[d - 1], r_tx.at[d - 1], xs[d - 1])

    def t_z(d):
        part = table.at[z, yh]
        return put(part, part, s_tz.at[d - 1], r_tz.at[d - 1], zs[d - 1])

    t_y = put(table.at[z, yh, co, :, yl], table.at[z, yh, co, :, yl], s_ty, r_ty, ylp)
    t_c = put(table.at[z, yh, co], table.at[z, yh, co], s_tc, r_tc, core)
    t_h = put(table.at[:, yh], table.at[:, yh], s_th, r_th, yp)
    for d in (1, 2, 3):
        t_x(d).start()

    top[...] = jnp.full(top.shape, -1e30, F32)
    total[...] = jnp.zeros(total.shape, F32)
    value[...] = jnp.zeros(value.shape, F32)
    lat_width = value.shape[2]

    def attend_chunk(r):
        c = chunk(r)

        def head(h):
            keys = kb[c].reshape(256, kb.shape[3])
            s = lax.dot_general(queries[h], keys, (((1,), (1,)), ((), ())), preferred_element_type=F32)
            s = jnp.where(key_pos[c] <= query_pos[...], s, -jnp.inf)
            old = top[h, :, :1]
            new = jnp.maximum(old, jnp.max(s, axis=1, keepdims=True))
            p = jnp.exp2((s - new) * scale)
            fade = jnp.exp2((old - new) * scale)
            top[h] = jnp.broadcast_to(new, top.shape[1:])
            total[h] = total[h] * fade + jnp.sum(p, axis=1, keepdims=True)
            value[h] = value[h] * fade + jnp.dot(p.astype(BF), keys[:, :lat_width], preferred_element_type=F32)

        loop(queries.shape[0], head)

    def step(k):
        @when(k < 7)
        def _():
            for r in range(1, 8):
                @when(k + 1 == r)
                def _():
                    c_in(r // 2, r % 2).wait_recv()
            c_core(k + 1).start()

        @when(k == 1)
        def _():
            for d in (1, 2, 3):
                t_x(d).wait_recv()
            t_y.start()

        @when(k == 2)
        def _():
            t_y.wait_recv()
            t_c.start()

        @when(k == 3)
        def _():
            t_c.wait_recv()
            for d in (1, 2, 3):
                t_z(d).start()

        @when(k == 4)
        def _():
            for d in (1, 2, 3):
                t_z(d).wait_recv()
            t_h.start()

        @when(k > 0)
        def _():
            c_core(k).wait_recv()

        attend_chunk(k)

    loop(8, step)

    def finish(h):
        context = (value[h] / total[h, :, :1]).astype(BF)
        r = jnp.dot(context, w_uv[h], preferred_element_type=F32).astype(BF)
        cols = pl.ds(pl.multiple_of(h * 128, 128), 128)
        for half in range(2):
            out[pl.ds(pl.multiple_of((half + co + 1) % 2 * 128, 128), 128), cols] = r[half * 128:half * 128 + 128]

    loop(queries.shape[0], finish)
    t_h.wait_recv()
    for r in range(1, 8):
        c_in(r // 2, r % 2).wait_send()
        c_core(r).wait_send()
    for d in (1, 2, 3):
        t_x(d).wait_send()
        t_z(d).wait_send()
    t_y.wait_send()
    t_c.wait_send()
    t_h.wait_send()


def project_kernel(heads, w_hbm, resid, gain, state, normed, w, wsem, *reduce_refs):
    pos = place()
    core, ylp, xs = exp_peers(pos)

    def load(n):
        return pltpu.make_async_copy(
            w_hbm.at[:, pl.ds(pl.multiple_of(n * W, W), W)], w.at[n], wsem.at[n]
        )

    loop(8, lambda n: load(n).start())
    greet([core, ylp] + xs)
    red = Reduce(reduce_refs, pos)

    def multiply(n):
        load(n).wait()
        t = jnp.dot(heads[...], w[n], preferred_element_type=F32)
        red.cs[n] = t[:128].astype(BF).reshape(4, 2, 16, W)
        red.c_core(n).start()
        red.own[n] = t[128:].reshape(4, 2, 16, W)

    def step(k):
        @when(k < 4)
        def _():
            multiply(2 * k)
            multiply(2 * k + 1)

        @when((k >= 1) & (k < 5))
        def _():
            red.first(k - 1)

        @when((k >= 2) & (k < 6))
        def _():
            red.second(k - 2)

        @when(k >= 3)
        def _():
            red.third(k - 3)

    loop(7, step)
    square = jnp.zeros((16, 1), F32)
    for n in range(8):
        t = resid[:, n * W:(n + 1) * W].astype(F32) + red.acc[n]
        state[n] = t
        square = square + jnp.sum(t * t, axis=1, keepdims=True)
    scale = lax.rsqrt(square / (8 * W) + 1e-06)
    for n in range(8):
        normed[n] = (state[n] * scale * gain[:, n * W:(n + 1) * W]).astype(BF)
    loop(4, red.drain)


def experts_kernel(normed, table, state, wg_hbm, wd_hbm, out,
                   slots, weights, hits, wg, wd, wsem, xb, rows, abuf, la, bbuf, bown, lb1, b2, lb2, a2, la2, suma,
                   acta, actb, yrow, tbuf, fin, ret, sems, *reduce_refs):
    pos = place()
    z, yh, x, yl, co = pos
    me = z * 2 + yh
    core, ylp, xs = exp_peers(pos)
    yo = (yl + 1) % 2
    yp = dev(z, (yh + 1) % 2, x, yl, co)
    zs = [dev((z + d) % 4, yh, x, yl, co) for d in (1, 2, 3)]
    red = Reduce(reduce_refs, pos)
    (s_in, r_in, s_g1x, r_g1x, s_g1y, r_g1y, s_g2y, r_g2y, s_g2x, r_g2x, s_gc, r_gc,
     s_a1, r_a1, s_b1, r_b1, s_b2, r_b2, s_a2, r_a2, s_ay, r_ay, s_az, r_az, s_bz, r_bz, s_by, r_by,
     s_f, r_f) = sems

    loads = [
        pltpu.make_async_copy(wg_hbm.at[0], wg.at[0], wsem.at[0]),
        pltpu.make_async_copy(wg_hbm.at[1], wg.at[1], wsem.at[1]),
        pltpu.make_async_copy(wd_hbm, wd, wsem.at[2]),
    ]
    for cp in loads:
        cp.start()
    ctx = [dev((z + dz) % 4, (yh + dy) % 2, x, yl, co) for dz in range(4) for dy in range(2) if dz or dy]
    greet([core, ylp] + xs + ctx)

    def chunk(dz, dy):
        return ((z + 4 - dz) % 4) * 2 + (yh + dy) % 2

    def c_in(dz, dy):
        zz, yy = (z + dz) % 4, (yh + dy) % 2
        r = dz * 2 + dy
        return put(normed.at[zz * 2 + yy], xb.at[me, co, x, yl], s_in.at[r], r_in.at[r],
                   dev(zz, yy, x, yl, co))

    for dz in (1, 2, 3, 0):
        for dy in range(2):
            if dz or dy:
                c_in(dz, dy).start()
    xb[me, co, x, yl] = normed[me]

    def c_g1x(dz, d):
        c = chunk(dz, 0)
        return put(xb.at[c, co, x, yl], xb.at[c, co, x, yl], s_g1x.at[dz, d - 1], r_g1x.at[dz, d - 1], xs[d - 1])

    def c_g2y(dz):
        c = chunk(dz, 0)
        return put(xb.at[c, co, :, yl], xb.at[c, co, :, yl], s_g2y.at[dz], r_g2y.at[dz], ylp)

    def c_g1y(dz):
        c = chunk(dz, 1)
        return put(xb.at[c, co, x, yl], xb.at[c, co, x, yl], s_g1y.at[dz], r_g1y.at[dz], ylp)

    def c_g2x(dz, d):
        c = chunk(dz, 1)
        return put(xb.at[c, co, x], xb.at[c, co, x], s_g2x.at[dz, d - 1], r_g2x.at[dz, d - 1], xs[d - 1])

    def c_gc(dz, dy):
        c = chunk(dz, dy)
        return put(xb.at[c, co], xb.at[c, co], s_gc.at[dz, dy], r_gc.at[dz, dy], core)

    def gather1(dz):
        @when(dz > 0)
        def _():
            c_in(dz, 0).wait_recv()
        for d in (1, 2, 3):
            c_g1x(dz, d).start()
        c_in(dz, 1).wait_recv()
        c_g1y(dz).start()

    def gather2(dz):
        for d in (1, 2, 3):
            c_g1x(dz, d).wait_recv()
        c_g2y(dz).start()
        c_g1y(dz).wait_recv()
        for d in (1, 2, 3):
            c_g2x(dz, d).start()

    def gather3(dz):
        c_g2y(dz).wait_recv()
        c_gc(dz, 0).start()
        for d in (1, 2, 3):
            c_g2x(dz, d).wait_recv()
        c_gc(dz, 1).start()

    def c_a1(dz, d):
        return put(abuf.at[dz], la.at[d - 1], s_a1.at[d - 1], r_a1.at[d - 1],
                   dev((z + 4 - d) % 4, yh, x, yl, co))

    def c_b1(dz):
        return put(bbuf.at[dz], lb1.at[dz], s_b1.at[dz], r_b1.at[dz], yp)

    def c_b2(dz):
        return put(b2.at[dz], lb2.at[dz], s_b2.at[dz], r_b2.at[dz], dev((z + 4 - dz) % 4, yh, x, yl, co))

    def find(k):
        for i in range(2):
            mine = table[k, :8, :] == (lax.axis_index("exp") * 2 + i).astype(F32)
            hits[k, i:i + 1, :] = jnp.max(jnp.where(mine, 1.0, 0.0), axis=0, keepdims=True)
            weights[k, i:i + 1, :] = jnp.sum(jnp.where(mine, table[k, 8:, :], 0.0), axis=0, keepdims=True)

    loop(8, find)
    one, two = (lax.broadcasted_iota(jnp.int32, (256, 256), a) for a in (0, 1))
    before = jnp.where((one < two) & (one // 16 == two // 16), 1.0, 0.0).astype(BF)
    block = (lax.broadcasted_iota(jnp.int32, (2, 256), 1) // 16 * 6).astype(F32)

    def rank(k):
        r = jnp.dot(hits[k].astype(BF), before, preferred_element_type=F32)
        slots[k] = jnp.where(hits[k] > 0.5, block + r, -1.0)

    loop(8, rank)
    row_id = lax.broadcasted_iota(jnp.int32, (96, 256), 0).astype(F32)

    def gate_up(dz):
        for dy in range(2):
            c_gc(dz, dy).wait_recv()
            c = chunk(dz, dy)
            tokens = xb[c].reshape(256, W)
            for i in range(2):
                pick = (row_id == slots[c, i:i + 1, :]).astype(BF)
                rows[i, dy * 96:(dy + 1) * 96] = jnp.dot(pick, tokens, preferred_element_type=F32).astype(BF)

        def cols(t):
            sl = pl.ds(pl.multiple_of(t * 512, 512), 512)
            r = jnp.dot(rows[0], wg[0, :, sl], preferred_element_type=F32).astype(BF)
            abuf[dz, :, :, sl] = r.reshape(2, 96, 512)

        loop(4, cols)

        for d in (1, 2, 3):
            @when(dz == d)
            def _():
                c_a1(d, d).start()

        def cols(t):
            sl = pl.ds(pl.multiple_of(t * 512, 512), 512)
            r = jnp.dot(rows[1], wg[1, :, sl], preferred_element_type=F32).astype(BF)
            bown[dz, :, sl] = r[:96]
            bbuf[dz, :, sl] = r[96:]

        loop(4, cols)
        c_b1(dz).start()

    def forward_b(dz):
        c_b1(dz).wait_recv()

        def cols(t):
            sl = pl.ds(pl.multiple_of(t * 512, 512), 512)
            b2[dz, :, sl] = (bown[dz, :, sl].astype(F32) + lb1[dz, :, sl].astype(F32)).astype(BF)

        loop(4, cols)

        @when(dz > 0)
        def _():
            c_b2(dz).start()

    def order(k):
        return (k + 1) % 4

    def step(k):
        @when(k < 4)
        def _():
            gather1(order(k))

        @when((k >= 1) & (k < 5))
        def _():
            gather2(order(k - 1))

        @when((k >= 2) & (k < 6))
        def _():
            gather3(order(k - 2))

        @when(k == 3)
        def _():
            loads[0].wait()
            loads[1].wait()

        @when((k >= 3) & (k < 7))
        def _():
            gate_up(order(k - 3))

        @when(k >= 5)
        def _():
            forward_b(order(k - 5))

    loop(9, step)

    for d in (1, 2, 3):
        c_a1(d, d).wait_recv()

    def cols(t):
        sl = pl.ds(pl.multiple_of(t * 256, 256), 256)

        def total(dy):
            r = abuf[0, dy, :, sl].astype(F32)
            for d in range(3):
                r = r + la[d, dy, :, sl].astype(F32)
            return r

        a2[:, sl] = total(1).astype(BF)
        suma[:, sl] = total(0)

    loop(8, cols)
    c_a2 = put(a2, la2, s_a2, r_a2, yp)
    c_a2.start()

    def activate(gate, up):
        return (gate / (1.0 + jnp.exp(-gate)) * up).astype(BF)

    c_a2.wait_recv()

    def cols(t):
        lo = pl.ds(pl.multiple_of(t * 256, 256), 256)
        hi = pl.ds(pl.multiple_of(t * 256 + 1024, 256), 256)
        acta[z, yh, :, lo] = activate(suma[:, lo] + la2[:, lo].astype(F32), suma[:, hi] + la2[:, hi].astype(F32))

    loop(4, cols)
    c_ay = put(acta.at[z, yh], acta.at[z, yh], s_ay, r_ay, yp)
    c_ay.start()

    def c_az(d):
        return put(acta.at[z], acta.at[z], s_az.at[d - 1], r_az.at[d - 1], zs[d - 1])

    def c_bz(d):
        return put(actb.at[z, yh], actb.at[z, yh], s_bz.at[d - 1], r_bz.at[d - 1], zs[d - 1])

    def c_by(dz):
        zz = (z + 4 - dz) % 4
        return put(actb.at[zz, yh], actb.at[zz, yh], s_by.at[dz], r_by.at[dz], yp)

    c_ay.wait_recv()
    for d in (1, 2, 3):
        c_az(d).start()

    for d in (1, 2, 3):
        c_b2(d).wait_recv()

    def cols(t):
        lo = pl.ds(pl.multiple_of(t * 256, 256), 256)
        hi = pl.ds(pl.multiple_of(t * 256 + 1024, 256), 256)

        def total(sl):
            r = b2[0, :, sl].astype(F32)
            for d in (1, 2, 3):
                r = r + lb2[d, :, sl].astype(F32)
            return r

        actb[z, yh, :, lo] = activate(total(lo), total(hi))

    loop(4, cols)
    for d in (1, 2, 3):
        c_bz(d).start()
    loads[2].wait()

    def pass_on(dz):
        for d in (1, 2, 3):
            @when(dz == d)
            def _():
                c_bz(d).wait_recv()
        c_by(dz).start()

    def down(dz):
        zz = (z + 4 - dz) % 4
        for d in (1, 2, 3):
            @when(dz == d)
            def _():
                c_az(d).wait_recv()
        c_by(dz).wait_recv()
        yrow[0] = jnp.dot(acta[zz].reshape(192, 1024), wd[0], preferred_element_type=F32).astype(BF)
        yrow[1] = jnp.dot(actb[zz].reshape(192, 1024), wd[1], preferred_element_type=F32).astype(BF)
        for dy in range(2):
            yy = (yh + dy) % 2
            c = zz * 2 + yy
            t = jnp.zeros((256, W), F32)
            for i in range(2):
                pick = jnp.where(row_id == slots[c, i:i + 1, :], weights[c, i:i + 1, :], 0.0).astype(BF)
                t = t + lax.dot_general(
                    pick, yrow[i, pl.ds(pl.multiple_of(yy * 96, 96), 96)], (((0,), (0,)), ((), ())),
                    preferred_element_type=F32)
            tbuf[...] = t.reshape(2, 4, 2, 16, W)
            n = dz * 2 + dy
            red.cs[n] = tbuf[(co + 1) % 2].astype(BF)
            red.c_core(n).start()
            red.own[n] = tbuf[co]

    def c_f(dz, dy):
        c = chunk(dz, dy)
        r = dz * 2 + dy
        return put(fin.at[r], ret.at[me], s_f.at[r], r_f.at[r],
                   dev((z + 4 - dz) % 4, (yh + dy) % 2, x, yl, co))

    def send_back(dz):
        red.third(dz)
        for dy in range(2):
            n = dz * 2 + dy
            fin[n] = red.acc[n].astype(BF)
            if dy:
                c_f(dz, dy).start()
            else:
                @when(dz > 0)
                def _():
                    c_f(dz, dy).start()

    def step(k):
        @when(k < 4)
        def _():
            pass_on(k)

        @when((k >= 1) & (k < 5))
        def _():
            down(k - 1)

        @when((k >= 2) & (k < 6))
        def _():
            red.first(k - 2)

        @when((k >= 3) & (k < 7))
        def _():
            red.second(k - 3)

        @when(k >= 4)
        def _():
            send_back(k - 4)

    loop(8, step)
    ret[me] = fin[0]
    for r in range(1, 8):
        c_f(r // 2, r % 2).wait_recv()
    for n in range(8):
        out[:, n * W:(n + 1) * W] = (state[n] + ret[n].astype(F32)).astype(BF)

    loop(4, red.drain)
    for r in range(1, 8):
        c_f(r // 2, r % 2).wait_send()
        c_in(r // 2, r % 2).wait_send()
    for dz in range(4):
        for d in (1, 2, 3):
            c_g1x(dz, d).wait_send()
            c_g2x(dz, d).wait_send()
        c_g1y(dz).wait_send()
        c_g2y(dz).wait_send()
        c_gc(dz, 0).wait_send()
        c_gc(dz, 1).wait_send()
        c_b1(dz).wait_send()
        c_by(dz).wait_send()
    for d in (1, 2, 3):
        c_a1(d, d).wait_send()
        c_b2(d).wait_send()
        c_az(d).wait_send()
        c_bz(d).wait_send()
    c_a2.wait_send()
    c_ay.wait_send()


VM = pl.BlockSpec(memory_space=pltpu.VMEM)
ANY = pl.BlockSpec(memory_space=pl.ANY)


def project(heads, w_out, resid, gain):
    return pl.pallas_call(
        project_kernel,
        name="project",
        out_shape=(jax.ShapeDtypeStruct((8, 16, W), F32), jax.ShapeDtypeStruct((8, 16, W), BF)),
        in_specs=[VM, ANY, VM, VM],
        out_specs=(VM, VM),
        scratch_shapes=[pltpu.VMEM((8, 768, W), BF), DMA((8,))] + REDUCE_SCRATCH,
        compiler_params=pltpu.CompilerParams(
            collective_id=1, has_side_effects=True, vmem_limit_bytes=50 << 20),
    )(heads, w_out, resid, gain)


def experts(normed, table, state, w_gate_up, w_down):
    hid2 = w_gate_up.shape[2]
    hid = hid2 // 2
    sems = [
        DMA((8,)), DMA((8,)),
        DMA((4, 3)), DMA((4, 3)), DMA((4,)), DMA((4,)), DMA((4,)), DMA((4,)), DMA((4, 3)), DMA((4, 3)),
        DMA((4, 2)), DMA((4, 2)),
        DMA((3,)), DMA((3,)), DMA((4,)), DMA((4,)), DMA((4,)), DMA((4,)), DMA, DMA,
        DMA, DMA, DMA((3,)), DMA((3,)), DMA((3,)), DMA((3,)), DMA((4,)), DMA((4,)),
        DMA((8,)), DMA((8,)),
    ]
    return pl.pallas_call(
        experts_kernel,
        name="experts",
        out_shape=jax.ShapeDtypeStruct((16, 8 * W), BF),
        in_specs=[VM, VM, VM, ANY, ANY],
        out_specs=VM,
        scratch_shapes=[
            pltpu.VMEM((8, 2, 256), F32),
            pltpu.VMEM((8, 2, 256), F32),
            pltpu.VMEM((8, 2, 256), F32),
            pltpu.VMEM((2, W, hid2), BF),
            pltpu.VMEM((2, hid, W), BF),
            DMA((3,)),
            pltpu.VMEM((8, 2, 4, 2, 16, W), BF),
            pltpu.VMEM((2, 192, W), BF),
            pltpu.VMEM((4, 2, 96, hid2), BF),
            pltpu.VMEM((3, 2, 96, hid2), BF),
            pltpu.VMEM((4, 96, hid2), BF),
            pltpu.VMEM((4, 96, hid2), BF),
            pltpu.VMEM((4, 96, hid2), BF),
            pltpu.VMEM((4, 96, hid2), BF),
            pltpu.VMEM((4, 96, hid2), BF),
            pltpu.VMEM((96, hid2), BF),
            pltpu.VMEM((96, hid2), BF),
            pltpu.VMEM((96, hid2), F32),
            pltpu.VMEM((4, 2, 96, hid), BF),
            pltpu.VMEM((4, 2, 96, hid), BF),
            pltpu.VMEM((2, 192, W), BF),
            pltpu.VMEM((2, 4, 2, 16, W), F32),
            pltpu.VMEM((8, 16, W), BF),
            pltpu.VMEM((8, 16, W), BF),
            tuple(sems),
        ] + REDUCE_SCRATCH,
        compiler_params=pltpu.CompilerParams(
            collective_id=2, has_side_effects=True, vmem_limit_bytes=62 << 20),
    )(normed, table, state, w_gate_up, w_down)


def attend(queries, latent, query_pos, key_pos, w_uv, routes):
    heads_dev, query_count, feat_width = queries.shape
    lat_width, value_width = w_uv.shape[1:]
    score_scale = (value_width + feat_width - lat_width) ** (-0.5)
    return pl.pallas_call(
        functools.partial(attend_kernel, score_scale * 1.4426950408889634),
        name="attend",
        out_shape=(
            jax.ShapeDtypeStruct((query_count, heads_dev * value_width), BF),
            jax.ShapeDtypeStruct((4, 2, 2, 4, 2, 16, 16), F32),
        ),
        in_specs=[VM] * 6,
        out_specs=(VM, VM),
        scratch_shapes=[
            pltpu.VMEM((8, 2, 128, feat_width), BF),
            pltpu.VMEM((heads_dev, query_count, 128), F32),
            pltpu.VMEM((heads_dev, query_count, 128), F32),
            pltpu.VMEM((heads_dev, query_count, lat_width), F32),
            DMA((8,)), DMA((8,)), DMA((8,)), DMA((8,)),
            DMA((3,)), DMA((3,)), DMA, DMA, DMA, DMA, DMA((3,)), DMA((3,)), DMA, DMA,
        ],
        compiler_params=pltpu.CompilerParams(
            collective_id=3, has_side_effects=True, vmem_limit_bytes=40 << 20),
    )(queries, latent, query_pos, key_pos, w_uv, routes)


def positions(block_order):
    return (block_order[:, None] * 128 + jnp.arange(128, dtype=jnp.int32)[None, :]).reshape(8, 256)


def body(queries, latent, block_order, w_uv, w_out, resid, norm_gain, expert_ids, route_weights, w_gate_up, w_down):
    def by_core(t, axis):
        shape = t.shape
        t = t.reshape(shape[:axis] + (8, 2, 16) + shape[axis + 1:])
        return jnp.swapaxes(t, axis, axis + 1).reshape(shape)

    pos = positions(block_order)
    mine = lax.dynamic_index_in_dim(pos, lax.axis_index("ctx"), 0, keepdims=False)
    routes = jnp.concatenate([expert_ids.astype(F32), route_weights], axis=1).T
    head_out, table = attend(
        by_core(queries, 0).transpose(1, 0, 2), latent, by_core(mine, 0)[:, None], pos[:, None, :], w_uv, routes)
    table = table.reshape(8, 16, 16, 16).transpose(0, 2, 1, 3).reshape(8, 16, 256)
    state, normed = project(head_out, w_out, resid, norm_gain.reshape(1, -1))
    return experts(normed, table, state, w_gate_up, w_down)


def solution(mesh):
    return jax.shard_map(
        body,
        mesh=mesh,
        in_specs=(
            P("ctx", "exp", None),
            P("ctx", None),
            P(),
            P("exp", None, None),
            P("exp", None),
            P(("ctx", "exp"), None),
            P(),
            P(("ctx", "exp"), None),
            P(("ctx", "exp"), None),
            P("exp", "ctx", None),
            P("exp", None, "ctx"),
        ),
        out_specs=P(("ctx", "exp"), None),
        check_vma=False,
    )
```

```python
import functools

import jax
import jax.numpy as jnp
from jax import lax
from jax.experimental import pallas as pl
from jax.experimental.pallas import tpu as pltpu
from jax.sharding import PartitionSpec as P

BF = jnp.bfloat16
F32 = jnp.float32
DMA = pltpu.SemaphoreType.DMA
W = 896


def place():
    c = lax.axis_index("ctx")
    e = lax.axis_index("exp")
    return c // 2, c % 2, e // 4, (e // 2) % 2, e % 2


def dev(z, yh, x, yl, co):
    return (z * 2 + yh, x * 4 + yl * 2 + co)


def put(src, dst, ss, rs, device):
    return pltpu.make_async_remote_copy(
        src_ref=src,
        dst_ref=dst,
        send_sem=ss,
        recv_sem=rs,
        device_id=device,
        device_id_type=pl.DeviceIdType.MESH,
    )


def greet(devices):
    barrier = pltpu.get_barrier_semaphore()
    for d in devices:
        pl.semaphore_signal(barrier, inc=1, device_id=d, device_id_type=pl.DeviceIdType.MESH)
    pl.semaphore_wait(barrier, len(devices))


def exp_peers(pos):
    z, yh, x, yl, co = pos
    core = dev(z, yh, x, yl, (co + 1) % 2)
    ylp = dev(z, yh, x, (yl + 1) % 2, co)
    xs = [dev(z, yh, (x + d) % 4, yl, co) for d in (1, 2, 3)]
    return core, ylp, xs


REDUCE_SCRATCH = [
    pltpu.VMEM((8, 4, 2, 16, W), F32),
    pltpu.VMEM((8, 4, 2, 16, W), BF),
    pltpu.VMEM((8, 4, 2, 16, W), BF),
    pltpu.VMEM((8, 4, 2, 16, W), BF),
    pltpu.VMEM((4, 3, 2, 16, W), BF),
    pltpu.VMEM((8, 4, 16, W), BF),
    pltpu.VMEM((4, 16, W), BF),
    pltpu.VMEM((8, 3, 16, W), BF),
    pltpu.VMEM((4, 16, W), BF),
    pltpu.VMEM((8, 3, 16, W), BF),
    pltpu.VMEM((8, 16, W), F32),
    DMA((8,)),
    DMA((8,)),
    DMA((4, 3)),
    DMA((4, 3)),
    DMA((8,)),
    DMA((8,)),
    DMA((4,)),
    DMA((4,)),
    DMA((8, 3)),
    DMA((8, 3)),
]


class Reduce:
    def __init__(self, refs, pos, crossed):
        (self.own, self.cs, self.cl, self.s1, self.x1, self.y1, self.y2s, self.x2s, self.y2,
         self.x2, self.acc, *self.sems) = refs
        self.pos = pos
        self.crossed = crossed
        self.core, self.ylp, self.xs = exp_peers(pos)

    def c_core(self, n):
        return put(self.cs.at[n], self.cl.at[n], self.sems[0].at[n], self.sems[1].at[n], self.core)

    def c_x1(self, i, d):
        xx = (self.pos[2] + d) % 4
        return put(self.s1.at[2 * i, xx], self.x1.at[i, d - 1], self.sems[2].at[i, d - 1],
                   self.sems[3].at[i, d - 1], self.xs[d - 1])

    def c_y1(self, n):
        return put(self.s1.at[n, :, (self.pos[3] + 1) % 2], self.y1.at[n], self.sems[4].at[n],
                   self.sems[5].at[n], self.ylp)

    def c_y2(self, i):
        return put(self.y2s.at[i], self.y2.at[i], self.sems[6].at[i], self.sems[7].at[i], self.ylp)

    def c_x2(self, n, part, odd):
        plus = (part == 1) == odd
        return put(self.x2s.at[n, part], self.x2.at[n, part], self.sems[8].at[n, part],
                   self.sems[9].at[n, part], self.xs[0 if plus else 2])

    def over_y(self, n, xx):
        return self.s1[n, xx, self.pos[3]].astype(F32) + self.y1[n, xx].astype(F32)

    def first(self, i):
        for j in range(2):
            n = 2 * i + j
            self.c_core(n).wait_recv()
            self.s1[n] = (self.own[n] + self.cl[n].astype(F32)).astype(BF)
            if self.crossed and j == 0:
                for d in (1, 2, 3):
                    self.c_x1(i, d).start()
            else:
                self.c_y1(n).start()

    def second(self, i):
        x, yl = self.pos[2], self.pos[3]
        for j in range(2):
            n = 2 * i + j
            if self.crossed and j == 0:
                for d in (1, 2, 3):
                    self.c_x1(i, d).wait_recv()

                def over_x(which):
                    t = self.s1[n, x, which].astype(F32)
                    for d in (0, 1, 2):
                        t = t + self.x1[i, d, which].astype(F32)
                    return t

                self.y2s[i] = over_x((yl + 1) % 2).astype(BF)
                self.c_y2(i).start()
                self.acc[n] = over_x(yl)
            else:
                self.c_y1(n).wait_recv()
                for part, d in ((0, 2), (1, 1 if j else 3)):
                    self.x2s[n, part] = self.over_y(n, (x + d) % 4).astype(BF)
                    self.c_x2(n, part, j == 1).start()
                self.acc[n] = self.over_y(n, x)

    def carry(self, i):
        for j in range(2):
            n = 2 * i + j
            if not (self.crossed and j == 0):
                self.c_x2(n, 0, j == 1).wait_recv()
                xx = (self.pos[2] + (3 if j else 1)) % 4
                self.x2s[n, 2] = (self.over_y(n, xx) + self.x2[n, 0].astype(F32)).astype(BF)
                self.c_x2(n, 2, j == 1).start()

    def third(self, i):
        for j in range(2):
            n = 2 * i + j
            t = self.acc[n]
            if self.crossed and j == 0:
                self.c_y2(i).wait_recv()
                t = t + self.y2[i].astype(F32)
            else:
                for part in (1, 2):
                    self.c_x2(n, part, j == 1).wait_recv()
                    t = t + self.x2[n, part].astype(F32)
            self.acc[n] = t

    def drain(self, i):
        for j in range(2):
            n = 2 * i + j
            self.c_core(n).wait_send()
            if self.crossed and j == 0:
                self.c_y2(i).wait_send()
            else:
                self.c_y1(n).wait_send()
            for d in (1, 2, 3):
                if self.crossed and j == 0:
                    self.c_x1(i, d).wait_send()
                else:
                    self.c_x2(n, d - 1, j == 1).wait_send()


REDUCE_X_SCRATCH = [
    pltpu.VMEM((8, 4, 2, 16, W), F32),
    pltpu.VMEM((8, 4, 2, 16, W), BF),
    pltpu.VMEM((8, 4, 2, 16, W), BF),
    pltpu.VMEM((8, 4, 2, 16, W), BF),
    pltpu.VMEM((8, 2, 16, W), BF),
    pltpu.VMEM((8, 3, 2, 16, W), BF),
    pltpu.VMEM((8, 16, W), BF),
    pltpu.VMEM((8, 16, W), BF),
    pltpu.VMEM((8, 16, W), F32),
    DMA((8,)),
    DMA((8,)),
    DMA((8, 3)),
    DMA((8, 3)),
    DMA((8,)),
    DMA((8,)),
]


class ReduceX:
    def __init__(self, refs, pos):
        (self.own, self.cs, self.cl, self.s1, self.xc, self.xl, self.ys, self.yr, self.acc, *self.sems) = refs
        self.pos = pos
        self.core, self.ylp, self.xs = exp_peers(pos)

    def c_core(self, n):
        return put(self.cs.at[n], self.cl.at[n], self.sems[0].at[n], self.sems[1].at[n], self.core)

    def c_x(self, n, part, odd):
        x = self.pos[2]
        if part == 2:
            src = self.xc.at[n]
        else:
            src = self.s1.at[n, (x + 2) % 4 if part == 0 else (x + (1 if odd else 3)) % 4]
        plus = (part == 1) == odd
        return put(src, self.xl.at[n, part], self.sems[2].at[n, part], self.sems[3].at[n, part],
                   self.xs[0 if plus else 2])

    def c_y(self, n):
        return put(self.ys.at[n], self.yr.at[n], self.sems[4].at[n], self.sems[5].at[n], self.ylp)

    def first(self, i):
        for j in range(2):
            n = 2 * i + j
            self.c_core(n).wait_recv()
            self.s1[n] = (self.own[n] + self.cl[n].astype(F32)).astype(BF)
            self.c_x(n, 0, j == 1).start()
            self.c_x(n, 1, j == 1).start()

    def second(self, i):
        for j in range(2):
            n = 2 * i + j
            self.c_x(n, 0, j == 1).wait_recv()
            near = (self.pos[2] + (3 if j else 1)) % 4
            self.xc[n] = (self.s1[n, near].astype(F32) + self.xl[n, 0].astype(F32)).astype(BF)
            self.c_x(n, 2, j == 1).start()

    def carry(self, i):
        x, yl = self.pos[2], self.pos[3]
        for j in range(2):
            n = 2 * i + j
            self.c_x(n, 1, j == 1).wait_recv()
            self.c_x(n, 2, j == 1).wait_recv()

            def over_x(which):
                t = self.s1[n, x, which].astype(F32)
                return t + self.xl[n, 1, which].astype(F32) + self.xl[n, 2, which].astype(F32)

            self.ys[n] = over_x((yl + 1) % 2).astype(BF)
            self.c_y(n).start()
            self.acc[n] = over_x(yl)

    def third(self, i):
        for j in range(2):
            n = 2 * i + j
            self.c_y(n).wait_recv()
            self.acc[n] = self.acc[n] + self.yr[n].astype(F32)

    def drain(self, i):
        for j in range(2):
            n = 2 * i + j
            self.c_core(n).wait_send()
            self.c_y(n).wait_send()
            for part in range(3):
                self.c_x(n, part, j == 1).wait_send()


def loop(count, step):
    def body(k, carry):
        step(k)
        return carry

    lax.fori_loop(0, count, body, 0)


def when(cond):
    return pl.when(cond)


def attend_kernel(scale, block_order, queries, latent, w_uv, ids, weights, out, table,
                  kb, near, qs, top, scores, mid, part, some,
                  s_a, r_a, s_ay, r_ay, s_b, r_b, s_by, r_by, s_c, r_c,
                  s_tx, r_tx, s_ty, r_ty, s_tc, r_tc, s_tz, r_tz, s_th, r_th):
    pos = place()
    z, yh, x, yl, co = pos
    core, ylp, xs = exp_peers(pos)
    yp = dev(z, (yh + 1) % 2, x, yl, co)
    zs = [dev((z + d) % 4, yh, x, yl, co) for d in (1, 2, 3)]
    above, below = zs[0], zs[2]
    feat = latent.shape[0]
    heads = queries.shape[0]
    lat_width = w_uv.shape[1]
    greet([core, ylp, yp] + xs + zs)

    def c_a(p):
        plane, first, count = ((0, 0, 64), (0, 0, 64), (1, 0, 32), (3, 32, 32))[p]
        src = kb.at[(z + plane) % 4, yh, co, pl.ds(first, count)]
        return put(src, src, s_a.at[p], r_a.at[p], above if p in (0, 3) else below)

    def c_ay(dz):
        src = kb.at[(z + 4 - dz) % 4, yh, co, pl.ds(0, 64)]
        return put(src, src, s_ay.at[dz], r_ay.at[dz], yp)

    def c_b(p):
        if p < 2:
            src = kb.at[z, :, co, pl.ds(64, 64)]
        elif p == 2:
            src = kb.at[(z + 1) % 4, 0, co, pl.ds(64, 64)]
        else:
            src = kb.at[(z + 3) % 4, 1, co, pl.ds(64, 64)]
        return put(src, src, s_b.at[p], r_b.at[p], above if p in (0, 3) else below)

    own = kb.at[z, yh, co, pl.ds(64, 64)]
    c_by = put(own, own, s_by, r_by, yp)

    def c_core(dz, dy):
        src = kb.at[(z + 4 - dz) % 4, (yh + dy) % 2, co]
        return put(src, src, s_c.at[dz, dy], r_c.at[dz, dy], core)

    kb[z, yh, :, :, feat:] = jnp.zeros((2, 128, kb.shape[4] - feat), BF)
    kb[z, yh, :, :, :feat] = latent[...].T.reshape(2, 128, feat)
    c_a(0).start()
    c_a(1).start()
    c_by.start()
    c_ay(0).start()

    near[co, x, yl] = jnp.zeros((16, 128), BF)
    near[co, x, yl, :, :16] = jnp.concatenate([ids[...].astype(F32), weights[...]], axis=0).astype(BF)

    def t_x(d):
        src = near.at[co, x, yl]
        return put(src, src, s_tx.at[d - 1], r_tx.at[d - 1], xs[d - 1])

    def t_z(d):
        src = table.at[z, yh]
        return put(src, src, s_tz.at[d - 1], r_tz.at[d - 1], zs[d - 1])

    t_y = put(near.at[co, :, yl], near.at[co, :, yl], s_ty, r_ty, ylp)
    t_c = put(near.at[co], near.at[co], s_tc, r_tc, core)
    t_h = put(table.at[:, yh], table.at[:, yh], s_th, r_th, yp)
    for d in (1, 2, 3):
        t_x(d).start()

    def pack():
        row = lax.broadcasted_iota(jnp.int32, (128, 256), 0)
        col = lax.broadcasted_iota(jnp.int32, (128, 256), 1)
        t = jnp.zeros((16, 256), F32)
        for i in range(16):
            move = jnp.where((col - row == 16 * i) & (row < 16), 1.0, 0.0).astype(BF)
            t = t + jnp.dot(near[i // 8, i // 2 % 4, i % 2], move, preferred_element_type=F32)
        table[z, yh] = t

    def turn(h):
        qs[h] = queries[h].T

    loop(heads, turn)
    top[...] = jnp.full(top.shape, -jnp.inf, F32)

    def place_of(c, axis):
        shape = (1, 256) if axis else (256, 1)
        at = lax.broadcasted_iota(jnp.int32, shape, axis)
        return jnp.where(at < 128, block_order[2 * c] * 128 + at, block_order[2 * c + 1] * 128 + (at - 128))

    def attend_chunk(r):
        zz, yy = (z + 4 - r // 2) % 4, (yh + r) % 2
        hidden = jnp.where(place_of(zz * 2 + yy, 1) <= place_of(z * 2 + yh, 0), 0.0, -jnp.inf)
        keys = kb[zz, yy].reshape(256, kb.shape[4])[:, :feat]
        for h in range(heads):
            s = lax.dot_general(qs[h], keys, (((1,), (1,)), ((), ())), preferred_element_type=F32)
            s = s + hidden
            scores[r, h] = s
            top[h] = jnp.maximum(top[h], jnp.maximum(s[:, :128], s[:, 128:]))

    def weigh(h, most, chunks):
        total = jnp.zeros((256, 128), F32)
        value = jnp.zeros((256, lat_width), F32)
        for r in chunks:
            p = jnp.exp2((scores[r, h] - most) * scale)
            total = total + (p[:, :128] + p[:, 128:])
            keys = kb[(z + 4 - r // 2) % 4, (yh + r) % 2].reshape(256, kb.shape[4])[:, :lat_width]
            value = value + jnp.dot(p.astype(BF), keys, preferred_element_type=F32)
        return total, value

    early, late = (0, 1, 2, 6), (3, 7, 4, 5)

    def begin(h):
        most = jnp.max(top[h], axis=1, keepdims=True)
        mid[h] = jnp.broadcast_to(most, mid.shape[1:])
        part[h], some[h] = weigh(h, most, early)

    def finish(h):
        most = jnp.max(top[h], axis=1, keepdims=True)
        fade = jnp.exp2((mid[h, :, :1] - most) * scale)
        total, value = weigh(h, most, late)
        total = jnp.sum(total + part[h] * fade, axis=1, keepdims=True)
        context = ((value + some[h] * fade) / total).astype(BF)
        r = jnp.dot(context, w_uv[h], preferred_element_type=F32).astype(BF)
        cols = pl.ds(pl.multiple_of(h * 128, 128), 128)
        for g in range(16):
            row = (g % 2 + co + 1) % 2 * 128 + g // 2 * 16
            out[pl.ds(pl.multiple_of(row, 16), 16), cols] = r[g * 16:g * 16 + 16]

    attend_chunk(0)
    c_by.wait_recv()
    c_b(0).start()
    c_b(1).start()
    c_ay(0).wait_recv()
    c_core(0, 1).start()
    c_a(0).wait_recv()
    c_a(3).start()
    c_ay(1).start()
    c_a(1).wait_recv()
    c_a(2).start()
    c_ay(3).start()
    for d in (1, 2, 3):
        t_x(d).wait_recv()
    t_y.start()
    c_core(0, 1).wait_recv()
    attend_chunk(1)
    c_b(0).wait_recv()
    c_b(3).start()
    c_core(1, 0).start()
    c_b(1).wait_recv()
    c_b(2).start()
    c_core(3, 0).start()
    c_a(2).wait_recv()
    c_a(3).wait_recv()
    c_ay(2).start()
    t_y.wait_recv()
    t_c.start()
    c_core(1, 0).wait_recv()
    attend_chunk(2)
    c_ay(1).wait_recv()
    c_core(1, 1).start()
    c_ay(3).wait_recv()
    c_core(3, 1).start()
    c_core(3, 0).wait_recv()
    attend_chunk(6)
    t_c.wait_recv()
    pack()
    for d in (1, 2, 3):
        t_z(d).start()
    loop(heads, begin)
    c_b(2).wait_recv()
    c_b(3).wait_recv()
    c_core(2, 0).start()
    c_ay(2).wait_recv()
    c_core(2, 1).start()
    for d in (1, 2, 3):
        t_z(d).wait_recv()
    t_h.start()
    c_core(1, 1).wait_recv()
    attend_chunk(3)
    c_core(3, 1).wait_recv()
    attend_chunk(7)
    c_core(2, 0).wait_recv()
    attend_chunk(4)
    c_core(2, 1).wait_recv()
    attend_chunk(5)
    loop(heads, finish)
    t_h.wait_recv()
    for p in range(4):
        c_a(p).wait_send()
        c_b(p).wait_send()
        c_ay(p).wait_send()
    c_by.wait_send()
    for r in range(1, 8):
        c_core(r // 2, r % 2).wait_send()
    for d in (1, 2, 3):
        t_x(d).wait_send()
        t_z(d).wait_send()
    t_y.wait_send()
    t_c.wait_send()
    t_h.wait_send()


def project_kernel(heads, w_hbm, resid, gain, state, normed, w, wsem, *reduce_refs):
    pos = place()
    core, ylp, xs = exp_peers(pos)

    def load(n):
        return pltpu.make_async_copy(
            w_hbm.at[:, pl.ds(pl.multiple_of(n * W, W), W)], w.at[n], wsem.at[n]
        )

    loop(8, lambda n: load(n).start())
    greet([core, ylp] + xs)
    red = Reduce(reduce_refs, pos, True)

    def multiply(n):
        load(n).wait()
        t = jnp.dot(heads[...], w[n], preferred_element_type=F32)
        red.cs[n] = t[:128].astype(BF).reshape(4, 2, 16, W)
        red.c_core(n).start()
        red.own[n] = t[128:].reshape(4, 2, 16, W)

    def step(k):
        @when(k < 4)
        def _():
            multiply(2 * k)
            multiply(2 * k + 1)

        @when((k >= 1) & (k < 5))
        def _():
            red.first(k - 1)

        @when((k >= 2) & (k < 6))
        def _():
            red.second(k - 2)

        @when((k >= 3) & (k < 7))
        def _():
            red.carry(k - 3)

        @when(k >= 4)
        def _():
            red.third(k - 4)

    loop(8, step)
    square = jnp.zeros((16, 1), F32)
    for n in range(8):
        t = resid[:, n * W:(n + 1) * W].astype(F32) + red.acc[n]
        state[n] = t
        square = square + jnp.sum(t * t, axis=1, keepdims=True)
    scale = lax.rsqrt(square / (8 * W) + 1e-06)
    for n in range(8):
        normed[n] = (state[n] * scale * gain[:, n * W:(n + 1) * W]).astype(BF)
    loop(4, red.drain)


def experts_kernel(normed, table, state, wg_hbm, wd_hbm, out,
                   slots, weights, hits, wg, wd, wsem, xb, rows, abuf, fa, la, bbuf, bown, lb1, b2, fb, lb2, a2, la2, suma,
                   acta, actb, yrow, fin, ret, sems, *reduce_refs):
    pos = place()
    z, yh, x, yl, co = pos
    me = z * 2 + yh
    core, ylp, xs = exp_peers(pos)
    yo = (yl + 1) % 2
    yp = dev(z, (yh + 1) % 2, x, yl, co)
    zs = [dev((z + d) % 4, yh, x, yl, co) for d in (1, 2, 3)]
    red = ReduceX(reduce_refs, pos)
    (s_in, r_in, s_gy, r_gy, s_gx, r_gx, s_gc, r_gc,
     s_a1, r_a1, s_b1, r_b1, s_b2, r_b2, s_a2, r_a2, s_ay, r_ay, s_az, r_az, s_bz, r_bz, s_by, r_by,
     s_f, r_f) = sems
    na, nb = a2.shape[1], bown.shape[2]
    n1 = na - 48
    half = nb // 2
    above, below = zs[0], zs[2]

    loads = [
        pltpu.make_async_copy(wg_hbm.at[0], wg.at[0], wsem.at[0]),
        pltpu.make_async_copy(wg_hbm.at[1], wg.at[1], wsem.at[1]),
        pltpu.make_async_copy(wd_hbm, wd, wsem.at[2]),
    ]
    for cp in loads:
        cp.start()
    ctx = [dev((z + dz) % 4, (yh + dy) % 2, x, yl, co) for dz in range(4) for dy in range(2) if dz or dy]
    greet([core, ylp] + xs + ctx)

    def chunk(dz, dy):
        return ((z + 4 - dz) % 4) * 2 + (yh + dy) % 2

    def c_in(dz, dy):
        zz, yy = (z + dz) % 4, (yh + dy) % 2
        r = dz * 2 + dy
        return put(normed.at[zz * 2 + yy], xb.at[me, co, x, yl], s_in.at[r], r_in.at[r],
                   dev(zz, yy, x, yl, co))

    for dz in (1, 2, 3, 0):
        for dy in range(2):
            if dz or dy:
                c_in(dz, dy).start()
    xb[me, co, x, yl] = normed[me]

    def c_gy(dz, dy):
        c = chunk(dz, dy)
        return put(xb.at[c, co, x, yl], xb.at[c, co, x, yl], s_gy.at[dz, dy], r_gy.at[dz, dy], ylp)

    def c_gx(dz, dy, part):
        c = chunk(dz, dy)
        r = dz * 2 + dy
        src = x if part < 2 else (x + (3 if dy else 1)) % 4
        plus = part == 0 or (part == 2 and dy == 1)
        return put(xb.at[c, co, src], xb.at[c, co, src], s_gx.at[r, part], r_gx.at[r, part], xs[0 if plus else 2])

    def c_gc(dz, dy):
        c = chunk(dz, dy)
        return put(xb.at[c, co], xb.at[c, co], s_gc.at[dz, dy], r_gc.at[dz, dy], core)

    def gather1(dz):
        @when(dz > 0)
        def _():
            c_in(dz, 0).wait_recv()
        c_gy(dz, 0).start()
        c_in(dz, 1).wait_recv()
        c_gy(dz, 1).start()

    def gather2(dz):
        for dy in range(2):
            c_gy(dz, dy).wait_recv()
            c_gx(dz, dy, 0).start()
            c_gx(dz, dy, 1).start()

    def gather3(dz):
        for dy in range(2):
            c_gx(dz, dy, 0).wait_recv()
            c_gx(dz, dy, 1).wait_recv()
            c_gx(dz, dy, 2).start()

    def gather4(dz):
        for dy in range(2):
            c_gx(dz, dy, 2).wait_recv()
            c_gc(dz, dy).start()

    def c_far(g, dy):
        return put(abuf.at[g, 2, dy], fa.at[g, dy], s_a1.at[g, 0, dy], r_a1.at[g, 0, dy], above if dy else below)

    def c_below(g, dy):
        return put(abuf.at[g, 1, dy], la.at[g, 0, dy], s_a1.at[g, 1, dy], r_a1.at[g, 1, dy], below)

    def c_above(g, dy):
        return put(abuf.at[g, 3, dy], la.at[g, 1, dy], s_a1.at[g, 2, dy], r_a1.at[g, 2, dy], above)

    def c_b1(g, dz):
        return put(bbuf.at[g, dz], lb1.at[g, dz], s_b1.at[g, dz], r_b1.at[g, dz], yp)

    def part(h):
        return pl.ds(h * half, half)

    def c_bfar(g, h):
        return put(b2.at[g, 2, part(h)], fb.at[g, part(h)], s_b2.at[g, 0, h], r_b2.at[g, 0, h],
                   above if h else below)

    def c_bbelow(g, h):
        return put(b2.at[g, 1, part(h)], lb2.at[g, 0, part(h)], s_b2.at[g, 1, h], r_b2.at[g, 1, h], below)

    def c_babove(g, h):
        return put(b2.at[g, 3, part(h)], lb2.at[g, 1, part(h)], s_b2.at[g, 2, h], r_b2.at[g, 2, h], above)

    def c_a2(g):
        return put(a2.at[g], la2.at[g], s_a2.at[g], r_a2.at[g], yp)

    def c_ay(g):
        return put(acta.at[g, z, yh], acta.at[g, z, yh], s_ay.at[g], r_ay.at[g], yp)

    def c_az(g, p):
        if p < 2:
            src = acta.at[g, z]
        elif p == 2:
            src = acta.at[g, (z + 1) % 4, 0]
        else:
            src = acta.at[g, (z + 3) % 4, 1]
        return put(src, src, s_az.at[g, p], r_az.at[g, p], above if p in (0, 3) else below)

    def c_bz(g, p):
        if p < 2:
            src = actb.at[g, z, yh]
        elif p == 2:
            src = actb.at[g, (z + 1) % 4, yh, part(0)]
        else:
            src = actb.at[g, (z + 3) % 4, yh, part(1)]
        return put(src, src, s_bz.at[g, p], r_bz.at[g, p], above if p in (0, 3) else below)

    def c_by(g, dz):
        zz = (z + 4 - dz) % 4
        return put(actb.at[g, zz, yh], actb.at[g, zz, yh], s_by.at[g, dz], r_by.at[g, dz], yp)

    def find(k):
        for i in range(2):
            mine = table[k, :8, :] == (lax.axis_index("exp") * 2 + i).astype(F32)
            hits[k, i:i + 1, :] = jnp.max(jnp.where(mine, 1.0, 0.0), axis=0, keepdims=True)
            weights[k, i:i + 1, :] = jnp.sum(jnp.where(mine, table[k, 8:, :], 0.0), axis=0, keepdims=True)

    loop(8, find)
    one, two = (lax.broadcasted_iota(jnp.int32, (256, 256), a) for a in (0, 1))
    before = jnp.where((one < two) & (one // 16 == two // 16), 1.0, 0.0).astype(BF)
    block = (lax.broadcasted_iota(jnp.int32, (2, 256), 1) // 16 * 6).astype(F32)

    def rank(k):
        r = jnp.dot(hits[k].astype(BF), before, preferred_element_type=F32)
        slots[k] = jnp.where(hits[k] > 0.5, block + r, -1.0)

    loop(8, rank)
    row_id = lax.broadcasted_iota(jnp.int32, (48, 128), 0).astype(F32)

    def chosen(c, i, g):
        tokens = slice(g * 128, g * 128 + 128)
        return row_id == slots[c, i:i + 1, tokens] - 48.0 * g, weights[c, i:i + 1, tokens]

    def gate_up(dz):
        for dy in range(2):
            c_gc(dz, dy).wait_recv()
            c = chunk(dz, dy)
            for g in range(2):
                tokens = xb[c, g].reshape(128, W)
                for i in range(2):
                    pick = chosen(c, i, g)[0].astype(BF)
                    rows[i, g, dy * 48:(dy + 1) * 48] = jnp.dot(
                        pick, tokens, preferred_element_type=F32).astype(BF)

        def cols(t):
            sl = pl.ds(pl.multiple_of(t * 512, 512), 512)
            r = jnp.dot(rows[0].reshape(192, W), wg[0, :, sl], preferred_element_type=F32)
            abuf[:, dz, :, :48, sl] = r.astype(BF).reshape(2, 2, 48, 512)
            r = jnp.dot(rows[1].reshape(192, W), wg[1, :, sl], preferred_element_type=F32)
            r = r.astype(BF).reshape(2, 2, 48, 512)
            abuf[:, dz, :, 48:, sl] = r[:, :, :n1]
            bown[:, dz, :, sl] = r[:, 0, n1:]
            bbuf[:, dz, :, sl] = r[:, 1, n1:]

        loop(4, cols)

        @when(dz == 2)
        def _():
            c_far(0, 0).start()
            c_far(0, 1).start()

        @when(dz == 1)
        def _():
            c_below(0, 1).start()

        @when(dz == 3)
        def _():
            c_above(0, 0).start()

        c_b1(0, dz).start()

    def carry_a(g):
        for dy, dz, c in ((0, 1, c_below), (1, 3, c_above)):
            c_far(g, dy).wait_recv()

            def cols(t):
                sl = pl.ds(pl.multiple_of(t * 512, 512), 512)
                abuf[g, dz, dy, :, sl] = (abuf[g, dz, dy, :, sl].astype(F32) + fa[g, dy, :, sl].astype(F32)).astype(BF)

            loop(4, cols)
            c(g, dy).start()

    def forward_b(g):
        def one(dz):
            c_b1(g, dz).wait_recv()
            b2[g, dz] = (bown[g, dz].astype(F32) + lb1[g, dz].astype(F32)).astype(BF)

        loop(4, one)
        c_bfar(g, 0).start()
        c_bfar(g, 1).start()
        c_bbelow(g, 1).start()
        c_babove(g, 0).start()

    def carry_b(g):
        for h, dz, c in ((0, 1, c_bbelow), (1, 3, c_babove)):
            c_bfar(g, h).wait_recv()
            b2[g, dz, part(h)] = (b2[g, dz, part(h)].astype(F32) + fb[g, part(h)].astype(F32)).astype(BF)
            c(g, h).start()

    def sum_a(g):
        for dy in range(2):
            c_below(g, dy).wait_recv()
            c_above(g, dy).wait_recv()

        def cols(t):
            sl = pl.ds(pl.multiple_of(t * 512, 512), 512)

            def total(dy):
                r = abuf[g, 0, dy, :, sl].astype(F32)
                return r + la[g, 0, dy, :, sl].astype(F32) + la[g, 1, dy, :, sl].astype(F32)

            a2[g, :, sl] = total(1).astype(BF)
            suma[g, :, sl] = total(0)

        loop(4, cols)
        c_a2(g).start()

    def activate(gate, up):
        return (gate / (1.0 + jnp.exp(-gate)) * up).astype(BF)

    def halves(t):
        return tuple(pl.ds(pl.multiple_of(t * 256 + o, 256), 256) for o in (0, wd.shape[1]))

    def act_a(g):
        c_a2(g).wait_recv()

        def cols(t):
            def total(sl):
                return suma[g, :, sl] + la2[g, :, sl].astype(F32)

            lo, hi = halves(t)
            acta[g, z, yh, :, lo] = activate(total(lo), total(hi))

        loop(4, cols)
        c_ay(g).start()

    def act_b(g):
        for h in range(2):
            c_bbelow(g, h).wait_recv()
            c_babove(g, h).wait_recv()

        def cols(t):
            def total(sl):
                r = b2[g, 0, :, sl].astype(F32)
                return r + lb2[g, 0, :, sl].astype(F32) + lb2[g, 1, :, sl].astype(F32)

            lo, hi = halves(t)
            actb[g, z, yh, :, lo] = activate(total(lo), total(hi))

        loop(4, cols)
        c_bz(g, 0).start()
        c_bz(g, 1).start()
        c_by(g, 0).start()

    def spread_a(g):
        c_ay(g).wait_recv()
        c_az(g, 0).start()
        c_az(g, 1).start()

    def pass_on(g):
        for p in range(2):
            c_bz(g, p).wait_recv()
            c_bz(g, 3 - p).start()
        c_by(g, 1).start()
        c_by(g, 3).start()
        for p in range(2):
            c_az(g, p).wait_recv()
            c_az(g, 3 - p).start()

    def pass_far(g):
        c_bz(g, 2).wait_recv()
        c_bz(g, 3).wait_recv()
        c_by(g, 2).start()

    def order(k):
        return 2 - k + 3 * (k // 2) - 2 * (k // 3)

    def step(k):
        @when(k < 4)
        def _():
            gather1(order(k))

        @when((k >= 1) & (k < 5))
        def _():
            gather2(order(k - 1))

        @when((k >= 2) & (k < 6))
        def _():
            gather3(order(k - 2))

        @when(k == 4)
        def _():
            loads[0].wait()
            loads[1].wait()

        @when(k >= 4)
        def _():
            gate_up(order(k - 4))

        @when((k >= 3) & (k < 7))
        def _():
            gather4(order(k - 3))

    loop(8, step)
    def nearest(k):
        return k + k // 2 - 2 * (k // 3)

    def down(g, k):
        dz = nearest(k)
        zz = (z + 4 - dz) % 4

        if k == 3:
            c_az(g, 2).wait_recv()
            c_az(g, 3).wait_recv()
        c_by(g, dz).wait_recv()
        yrow[0] = jnp.dot(acta[g, zz, :, :48].reshape(96, -1), wd[0], preferred_element_type=F32).astype(BF)
        one = jnp.concatenate([acta[g, zz, :, 48:], actb[g, zz]], axis=1).reshape(96, -1)
        yrow[1] = jnp.dot(one, wd[1], preferred_element_type=F32).astype(BF)
        for dy in range(2):
            yy = (yh + dy) % 2
            c = zz * 2 + yy
            n = k * 2 + dy
            pick = jnp.concatenate([jnp.where(*chosen(c, i, g), 0.0) for i in range(2)], axis=0).astype(BF)
            sl = pl.ds(pl.multiple_of(yy * 48, 16), 48)
            t = lax.dot_general(
                pick, jnp.concatenate([yrow[0, sl], yrow[1, sl]], axis=0), (((0,), (0,)), ((), ())),
                preferred_element_type=F32).reshape(4, 2, 16, W)

            @when(co == g)
            def _():
                red.own[n] = t

            @when(co != g)
            def _():
                red.cs[n] = t.astype(BF)
                red.c_core(n).start()

    def c_f(k, dy):
        zz, yy = (z + 4 - nearest(k)) % 4, (yh + dy) % 2
        r = k * 2 + dy
        return put(fin.at[r], ret.at[me], s_f.at[r], r_f.at[r], dev(zz, yy, x, yl, co))

    def send_back(k):
        red.third(k)
        for dy in range(2):
            n = k * 2 + dy
            fin[n] = red.acc[n].astype(BF)
            if n:
                c_f(k, dy).start()

    def back(g, *stages):
        @when(co == g)
        def _():
            for stage, k in stages:
                stage(k)

    first, second, carry = red.first, red.second, red.carry
    carry_a(0)
    c_far(1, 0).start()
    c_far(1, 1).start()
    c_below(1, 1).start()
    c_above(1, 0).start()
    for dz in (2, 1, 3, 0):
        c_b1(1, dz).start()
    forward_b(0)
    sum_a(0)
    carry_b(0)
    act_a(0)
    carry_a(1)
    act_b(0)
    spread_a(0)
    forward_b(1)
    sum_a(1)
    carry_b(1)
    loads[2].wait()
    pass_on(0)
    down(0, 0)
    act_a(1)
    back(0, (first, 0))
    act_b(1)
    down(0, 1)
    spread_a(1)
    back(0, (second, 0), (first, 1))
    down(0, 2)
    back(0, (carry, 0), (second, 1), (first, 2))
    pass_far(0)
    down(0, 3)
    back(0, (send_back, 0), (carry, 1), (second, 2), (first, 3))
    pass_on(1)
    down(1, 0)
    back(0, (send_back, 1), (carry, 2), (second, 3))
    back(1, (first, 0))
    down(1, 1)
    back(0, (send_back, 2), (carry, 3))
    back(1, (second, 0), (first, 1))
    down(1, 2)
    back(0, (send_back, 3))
    back(1, (carry, 0), (second, 1), (first, 2))
    pass_far(1)
    down(1, 3)
    back(1, (send_back, 0), (carry, 1), (second, 2), (first, 3))
    back(1, (send_back, 1), (carry, 2), (second, 3))
    back(1, (send_back, 2), (carry, 3))
    back(1, (send_back, 3))
    ret[me] = fin[0]
    for r in range(1, 8):
        c_f(r // 2, r % 2).wait_recv()
    for n in range(8):
        out[:, n * W:(n + 1) * W] = (state[n] + ret[n].astype(F32)).astype(BF)

    loop(4, red.drain)
    for r in range(1, 8):
        c_f(r // 2, r % 2).wait_send()
        c_in(r // 2, r % 2).wait_send()
    for dz in range(4):
        for dy in range(2):
            for p in range(3):
                c_gx(dz, dy, p).wait_send()
            c_gy(dz, dy).wait_send()
            c_gc(dz, dy).wait_send()
        for g in range(2):
            c_b1(g, dz).wait_send()
            c_by(g, dz).wait_send()
    for g in range(2):
        for h in range(2):
            c_far(g, h).wait_send()
            c_below(g, h).wait_send()
            c_above(g, h).wait_send()
            c_bfar(g, h).wait_send()
            c_bbelow(g, h).wait_send()
            c_babove(g, h).wait_send()
        for p in range(4):
            c_az(g, p).wait_send()
            c_bz(g, p).wait_send()
        c_a2(g).wait_send()
        c_ay(g).wait_send()


VM = pl.BlockSpec(memory_space=pltpu.VMEM)
ANY = pl.BlockSpec(memory_space=pl.ANY)


def project(heads, w_out, resid, gain):
    return pl.pallas_call(
        project_kernel,
        name="project",
        out_shape=(jax.ShapeDtypeStruct((8, 16, W), F32), jax.ShapeDtypeStruct((8, 16, W), BF)),
        in_specs=[VM, ANY, VM, VM],
        out_specs=(VM, VM),
        scratch_shapes=[pltpu.VMEM((8, 768, W), BF), DMA((8,))] + REDUCE_SCRATCH,
        compiler_params=pltpu.CompilerParams(
            collective_id=1, has_side_effects=True, vmem_limit_bytes=50 << 20),
    )(heads, w_out, resid, gain)


def experts(normed, table, state, w_gate_up, w_down):
    hid2 = w_gate_up.shape[2]
    hid = hid2 // 2
    na, nb = 64, 32
    sems = [
        DMA((8,)), DMA((8,)),
        DMA((4, 2)), DMA((4, 2)), DMA((8, 3)), DMA((8, 3)),
        DMA((4, 2)), DMA((4, 2)),
        DMA((2, 3, 2)), DMA((2, 3, 2)), DMA((2, 4)), DMA((2, 4)), DMA((2, 3, 2)), DMA((2, 3, 2)),
        DMA((2,)), DMA((2,)), DMA((2,)), DMA((2,)), DMA((2, 4)), DMA((2, 4)), DMA((2, 4)), DMA((2, 4)),
        DMA((2, 4)), DMA((2, 4)),
        DMA((8,)), DMA((8,)),
    ]
    return pl.pallas_call(
        experts_kernel,
        name="experts",
        out_shape=jax.ShapeDtypeStruct((16, 8 * W), BF),
        in_specs=[VM, VM, VM, ANY, ANY],
        out_specs=VM,
        scratch_shapes=[
            pltpu.VMEM((8, 2, 256), F32),
            pltpu.VMEM((8, 2, 256), F32),
            pltpu.VMEM((8, 2, 256), F32),
            pltpu.VMEM((2, W, hid2), BF),
            pltpu.VMEM((2, hid, W), BF),
            DMA((3,)),
            pltpu.VMEM((8, 2, 4, 2, 16, W), BF),
            pltpu.VMEM((2, 2, 96, W), BF),
            pltpu.VMEM((2, 4, 2, na, hid2), BF),
            pltpu.VMEM((2, 2, na, hid2), BF),
            pltpu.VMEM((2, 2, 2, na, hid2), BF),
            pltpu.VMEM((2, 4, nb, hid2), BF),
            pltpu.VMEM((2, 4, nb, hid2), BF),
            pltpu.VMEM((2, 4, nb, hid2), BF),
            pltpu.VMEM((2, 4, nb, hid2), BF),
            pltpu.VMEM((2, nb, hid2), BF),
            pltpu.VMEM((2, 2, nb, hid2), BF),
            pltpu.VMEM((2, na, hid2), BF),
            pltpu.VMEM((2, na, hid2), BF),
            pltpu.VMEM((2, na, hid2), F32),
            pltpu.VMEM((2, 4, 2, na, hid), BF),
            pltpu.VMEM((2, 4, 2, nb, hid), BF),
            pltpu.VMEM((2, 96, W), BF),
            pltpu.VMEM((8, 16, W), BF),
            pltpu.VMEM((8, 16, W), BF),
            tuple(sems),
        ] + REDUCE_X_SCRATCH,
        compiler_params=pltpu.CompilerParams(
            collective_id=2, has_side_effects=True, vmem_limit_bytes=62 << 20),
    )(normed, table, state, w_gate_up, w_down)


def attend(block_order, queries, latent, w_uv, ids, weights):
    heads_dev, feat_width, query_count = queries.shape
    lat_width, value_width = w_uv.shape[1:]
    score_scale = (value_width + feat_width - lat_width) ** (-0.5)
    return pl.pallas_call(
        functools.partial(attend_kernel, score_scale * 1.4426950408889634),
        name="attend",
        out_shape=(
            jax.ShapeDtypeStruct((query_count, heads_dev * value_width), BF),
            jax.ShapeDtypeStruct((4, 2, 16, 256), F32),
        ),
        in_specs=[pl.BlockSpec(memory_space=pltpu.SMEM)] + [VM] * 5,
        out_specs=(VM, VM),
        scratch_shapes=[
            pltpu.VMEM((4, 2, 2, 128, (feat_width + 127) // 128 * 128), BF),
            pltpu.VMEM((2, 4, 2, 16, 128), BF),
            pltpu.VMEM((heads_dev, query_count, feat_width), BF),
            pltpu.VMEM((heads_dev, query_count, 128), F32),
            pltpu.VMEM((8, heads_dev, query_count, 256), F32),
            pltpu.VMEM((heads_dev, query_count, 128), F32),
            pltpu.VMEM((heads_dev, query_count, 128), F32),
            pltpu.VMEM((heads_dev, query_count, lat_width), F32),
            DMA((4,)), DMA((4,)), DMA((4,)), DMA((4,)), DMA((4,)), DMA((4,)), DMA, DMA,
            DMA((4, 2)), DMA((4, 2)),
            DMA((3,)), DMA((3,)), DMA, DMA, DMA, DMA, DMA((3,)), DMA((3,)), DMA, DMA,
        ],
        compiler_params=pltpu.CompilerParams(
            collective_id=3, has_side_effects=True, vmem_limit_bytes=40 << 20),
    )(block_order, queries, latent, w_uv, ids, weights)


def body(queries, latent, block_order, w_uv, w_out, resid, norm_gain, expert_ids, route_weights, w_gate_up, w_down):
    head_out, table = attend(
        block_order, queries.transpose(1, 2, 0), latent.T, w_uv, expert_ids.T, route_weights.T)
    table = table.reshape(8, 16, 256)
    state, normed = project(head_out, w_out, resid, norm_gain.reshape(1, -1))
    return experts(normed, table, state, w_gate_up, w_down)


def solution(mesh):
    return jax.shard_map(
        body,
        mesh=mesh,
        in_specs=(
            P("ctx", "exp", None),
            P("ctx", None),
            P(),
            P("exp", None, None),
            P("exp", None),
            P(("ctx", "exp"), None),
            P(),
            P(("ctx", "exp"), None),
            P(("ctx", "exp"), None),
            P("exp", "ctx", None),
            P("exp", None, "ctx"),
        ),
        out_specs=P(("ctx", "exp"), None),
        check_vma=False,
    )
```

```python
import functools

import jax
import jax.numpy as jnp
from jax import lax
from jax.experimental import pallas as pl
from jax.experimental.pallas import tpu as pltpu
from jax.sharding import PartitionSpec as P

BF = jnp.bfloat16
F32 = jnp.float32
DMA = pltpu.SemaphoreType.DMA
W = 896


def place():
    c = lax.axis_index("ctx")
    e = lax.axis_index("exp")
    return c // 2, c % 2, e // 4, (e // 2) % 2, e % 2


def dev(z, yh, x, yl, co):
    return (z * 2 + yh, x * 4 + yl * 2 + co)


def put(src, dst, ss, rs, device):
    return pltpu.make_async_remote_copy(
        src_ref=src,
        dst_ref=dst,
        send_sem=ss,
        recv_sem=rs,
        device_id=device,
        device_id_type=pl.DeviceIdType.MESH,
    )


def greet(devices):
    barrier = pltpu.get_barrier_semaphore()
    for d in devices:
        pl.semaphore_signal(barrier, inc=1, device_id=d, device_id_type=pl.DeviceIdType.MESH)
    pl.semaphore_wait(barrier, len(devices))


def exp_peers(pos):
    z, yh, x, yl, co = pos
    core = dev(z, yh, x, yl, (co + 1) % 2)
    ylp = dev(z, yh, x, (yl + 1) % 2, co)
    xs = [dev(z, yh, (x + d) % 4, yl, co) for d in (1, 2, 3)]
    return core, ylp, xs


REDUCE_SCRATCH = [
    pltpu.VMEM((8, 4, 2, 16, W), F32),
    pltpu.VMEM((8, 4, 2, 16, W), BF),
    pltpu.VMEM((8, 4, 2, 16, W), BF),
    pltpu.VMEM((8, 4, 2, 16, W), BF),
    pltpu.VMEM((4, 3, 2, 16, W), BF),
    pltpu.VMEM((8, 4, 16, W), BF),
    pltpu.VMEM((4, 16, W), BF),
    pltpu.VMEM((8, 3, 16, W), BF),
    pltpu.VMEM((4, 16, W), BF),
    pltpu.VMEM((8, 3, 16, W), BF),
    pltpu.VMEM((8, 16, W), F32),
    DMA((8,)),
    DMA((8,)),
    DMA((4, 3)),
    DMA((4, 3)),
    DMA((8,)),
    DMA((8,)),
    DMA((4,)),
    DMA((4,)),
    DMA((8, 3)),
    DMA((8, 3)),
]


class Reduce:
    def __init__(self, refs, pos, crossed):
        (self.own, self.cs, self.cl, self.s1, self.x1, self.y1, self.y2s, self.x2s, self.y2,
         self.x2, self.acc, *self.sems) = refs
        self.pos = pos
        self.crossed = crossed
        self.core, self.ylp, self.xs = exp_peers(pos)

    def c_core(self, n):
        return put(self.cs.at[n], self.cl.at[n], self.sems[0].at[n], self.sems[1].at[n], self.core)

    def c_x1(self, i, d):
        xx = (self.pos[2] + d) % 4
        return put(self.s1.at[2 * i, xx], self.x1.at[i, d - 1], self.sems[2].at[i, d - 1],
                   self.sems[3].at[i, d - 1], self.xs[d - 1])

    def c_y1(self, n):
        return put(self.s1.at[n, :, (self.pos[3] + 1) % 2], self.y1.at[n], self.sems[4].at[n],
                   self.sems[5].at[n], self.ylp)

    def c_y2(self, i):
        return put(self.y2s.at[i], self.y2.at[i], self.sems[6].at[i], self.sems[7].at[i], self.ylp)

    def c_x2(self, n, part, odd):
        plus = (part == 1) == odd
        return put(self.x2s.at[n, part], self.x2.at[n, part], self.sems[8].at[n, part],
                   self.sems[9].at[n, part], self.xs[0 if plus else 2])

    def over_y(self, n, xx):
        return self.s1[n, xx, self.pos[3]].astype(F32) + self.y1[n, xx].astype(F32)

    def first(self, i):
        for j in range(2):
            n = 2 * i + j
            self.c_core(n).wait_recv()
            self.s1[n] = (self.own[n] + self.cl[n].astype(F32)).astype(BF)
            if self.crossed and j == 0:
                for d in (1, 2, 3):
                    self.c_x1(i, d).start()
            else:
                self.c_y1(n).start()

    def second(self, i):
        x, yl = self.pos[2], self.pos[3]
        for j in range(2):
            n = 2 * i + j
            if self.crossed and j == 0:
                for d in (1, 2, 3):
                    self.c_x1(i, d).wait_recv()

                def over_x(which):
                    t = self.s1[n, x, which].astype(F32)
                    for d in (0, 1, 2):
                        t = t + self.x1[i, d, which].astype(F32)
                    return t

                self.y2s[i] = over_x((yl + 1) % 2).astype(BF)
                self.c_y2(i).start()
                self.acc[n] = over_x(yl)
            else:
                self.c_y1(n).wait_recv()
                for part, d in ((0, 2), (1, 1 if j else 3)):
                    self.x2s[n, part] = self.over_y(n, (x + d) % 4).astype(BF)
                    self.c_x2(n, part, j == 1).start()
                self.acc[n] = self.over_y(n, x)

    def carry(self, i):
        for j in range(2):
            n = 2 * i + j
            if not (self.crossed and j == 0):
                self.c_x2(n, 0, j == 1).wait_recv()
                xx = (self.pos[2] + (3 if j else 1)) % 4
                self.x2s[n, 2] = (self.over_y(n, xx) + self.x2[n, 0].astype(F32)).astype(BF)
                self.c_x2(n, 2, j == 1).start()

    def third(self, i):
        for j in range(2):
            n = 2 * i + j
            t = self.acc[n]
            if self.crossed and j == 0:
                self.c_y2(i).wait_recv()
                t = t + self.y2[i].astype(F32)
            else:
                for part in (1, 2):
                    self.c_x2(n, part, j == 1).wait_recv()
                    t = t + self.x2[n, part].astype(F32)
            self.acc[n] = t

    def drain(self, i):
        for j in range(2):
            n = 2 * i + j
            self.c_core(n).wait_send()
            if self.crossed and j == 0:
                self.c_y2(i).wait_send()
            else:
                self.c_y1(n).wait_send()
            for d in (1, 2, 3):
                if self.crossed and j == 0:
                    self.c_x1(i, d).wait_send()
                else:
                    self.c_x2(n, d - 1, j == 1).wait_send()


REDUCE_X_SCRATCH = [
    pltpu.VMEM((8, 4, 2, 16, W), F32),
    pltpu.VMEM((8, 4, 2, 16, W), BF),
    pltpu.VMEM((8, 4, 2, 16, W), BF),
    pltpu.VMEM((8, 4, 2, 16, W), BF),
    pltpu.VMEM((8, 2, 16, W), BF),
    pltpu.VMEM((8, 3, 2, 16, W), BF),
    pltpu.VMEM((8, 16, W), BF),
    pltpu.VMEM((8, 16, W), BF),
    pltpu.VMEM((8, 16, W), F32),
    DMA((8,)),
    DMA((8,)),
    DMA((8, 3)),
    DMA((8, 3)),
    DMA((8,)),
    DMA((8,)),
]


class ReduceX:
    def __init__(self, refs, pos):
        (self.own, self.cs, self.cl, self.s1, self.xc, self.xl, self.ys, self.yr, self.acc, *self.sems) = refs
        self.pos = pos
        self.core, self.ylp, self.xs = exp_peers(pos)

    def c_core(self, n):
        return put(self.cs.at[n], self.cl.at[n], self.sems[0].at[n], self.sems[1].at[n], self.core)

    def c_x(self, n, part, odd):
        x = self.pos[2]
        if part == 2:
            src = self.xc.at[n]
        else:
            src = self.s1.at[n, (x + 2) % 4 if part == 0 else (x + (1 if odd else 3)) % 4]
        plus = (part == 1) == odd
        return put(src, self.xl.at[n, part], self.sems[2].at[n, part], self.sems[3].at[n, part],
                   self.xs[0 if plus else 2])

    def c_y(self, n):
        return put(self.ys.at[n], self.yr.at[n], self.sems[4].at[n], self.sems[5].at[n], self.ylp)

    def first(self, i):
        for j in range(2):
            n = 2 * i + j
            self.c_core(n).wait_recv()
            self.s1[n] = (self.own[n] + self.cl[n].astype(F32)).astype(BF)
            self.c_x(n, 0, j == 1).start()
            self.c_x(n, 1, j == 1).start()

    def second(self, i):
        for j in range(2):
            n = 2 * i + j
            self.c_x(n, 0, j == 1).wait_recv()
            near = (self.pos[2] + (3 if j else 1)) % 4
            self.xc[n] = (self.s1[n, near].astype(F32) + self.xl[n, 0].astype(F32)).astype(BF)
            self.c_x(n, 2, j == 1).start()

    def carry(self, i):
        x, yl = self.pos[2], self.pos[3]
        for j in range(2):
            n = 2 * i + j
            self.c_x(n, 1, j == 1).wait_recv()
            self.c_x(n, 2, j == 1).wait_recv()

            def over_x(which):
                t = self.s1[n, x, which].astype(F32)
                return t + self.xl[n, 1, which].astype(F32) + self.xl[n, 2, which].astype(F32)

            self.ys[n] = over_x((yl + 1) % 2).astype(BF)
            self.c_y(n).start()
            self.acc[n] = over_x(yl)

    def third(self, i):
        for j in range(2):
            n = 2 * i + j
            self.c_y(n).wait_recv()
            self.acc[n] = self.acc[n] + self.yr[n].astype(F32)

    def drain(self, i):
        for j in range(2):
            n = 2 * i + j
            self.c_core(n).wait_send()
            self.c_y(n).wait_send()
            for part in range(3):
                self.c_x(n, part, j == 1).wait_send()


def loop(count, step):
    def body(k, carry):
        step(k)
        return carry

    lax.fori_loop(0, count, body, 0)


def when(cond):
    return pl.when(cond)


def fetch(pairs, sems):
    copies = [pltpu.make_async_copy(src, dst, sems.at[i]) for i, (src, dst) in enumerate(pairs)]
    for cp in copies:
        cp.start()
    return copies


def attend_part(scale, loads, block_order, queries, latent, w_uv, ids, weights, out, table,
                  kb, near, qs, top, scores, mid, part, some,
                  s_a, r_a, s_ay, r_ay, s_b, r_b, s_by, r_by, s_c, r_c,
                  s_tx, r_tx, s_ty, r_ty, s_tc, r_tc, s_tz, r_tz, s_th, r_th):
    pos = place()
    z, yh, x, yl, co = pos
    core, ylp, xs = exp_peers(pos)
    yp = dev(z, (yh + 1) % 2, x, yl, co)
    zs = [dev((z + d) % 4, yh, x, yl, co) for d in (1, 2, 3)]
    above, below = zs[0], zs[2]
    feat = latent.shape[0]
    heads = queries.shape[0]
    lat_width = w_uv.shape[1]
    greet([core, ylp, yp] + xs + zs)
    got_latent, got_ids, got_weights, got_queries, got_w = loads

    def c_a(p):
        plane, first, count = ((0, 0, 64), (0, 0, 64), (1, 0, 32), (3, 32, 32))[p]
        src = kb.at[(z + plane) % 4, yh, co, pl.ds(first, count)]
        return put(src, src, s_a.at[p], r_a.at[p], above if p in (0, 3) else below)

    def c_ay(dz):
        src = kb.at[(z + 4 - dz) % 4, yh, co, pl.ds(0, 64)]
        return put(src, src, s_ay.at[dz], r_ay.at[dz], yp)

    def c_b(p):
        if p < 2:
            src = kb.at[z, :, co, pl.ds(64, 64)]
        elif p == 2:
            src = kb.at[(z + 1) % 4, 0, co, pl.ds(64, 64)]
        else:
            src = kb.at[(z + 3) % 4, 1, co, pl.ds(64, 64)]
        return put(src, src, s_b.at[p], r_b.at[p], above if p in (0, 3) else below)

    own = kb.at[z, yh, co, pl.ds(64, 64)]
    c_by = put(own, own, s_by, r_by, yp)

    def c_core(dz, dy):
        src = kb.at[(z + 4 - dz) % 4, (yh + dy) % 2, co]
        return put(src, src, s_c.at[dz, dy], r_c.at[dz, dy], core)

    got_latent.wait()
    kb[z, yh, :, :, feat:] = jnp.zeros((2, 128, kb.shape[4] - feat), BF)
    kb[z, yh, :, :, :feat] = latent[...].T.reshape(2, 128, feat)
    c_a(0).start()
    c_a(1).start()
    c_by.start()
    c_ay(0).start()

    got_ids.wait()
    got_weights.wait()
    near[co, x, yl] = jnp.zeros((16, 128), BF)
    near[co, x, yl, :, :16] = jnp.concatenate([ids[...].astype(F32), weights[...]], axis=0).astype(BF)

    def t_x(d):
        src = near.at[co, x, yl]
        return put(src, src, s_tx.at[d - 1], r_tx.at[d - 1], xs[d - 1])

    def t_z(d):
        src = table.at[z, yh]
        return put(src, src, s_tz.at[d - 1], r_tz.at[d - 1], zs[d - 1])

    t_y = put(near.at[co, :, yl], near.at[co, :, yl], s_ty, r_ty, ylp)
    t_c = put(near.at[co], near.at[co], s_tc, r_tc, core)
    t_h = put(table.at[:, yh], table.at[:, yh], s_th, r_th, yp)
    for d in (1, 2, 3):
        t_x(d).start()

    def pack():
        row = lax.broadcasted_iota(jnp.int32, (128, 256), 0)
        col = lax.broadcasted_iota(jnp.int32, (128, 256), 1)
        t = jnp.zeros((16, 256), F32)
        for i in range(16):
            move = jnp.where((col - row == 16 * i) & (row < 16), 1.0, 0.0).astype(BF)
            t = t + jnp.dot(near[i // 8, i // 2 % 4, i % 2], move, preferred_element_type=F32)
        table[z, yh] = t

    def turn(h):
        qs[h] = queries[h].T

    got_queries.wait()
    loop(heads, turn)
    top[...] = jnp.full(top.shape, -jnp.inf, F32)

    def place_of(c, axis):
        shape = (1, 256) if axis else (256, 1)
        at = lax.broadcasted_iota(jnp.int32, shape, axis)
        return jnp.where(at < 128, block_order[2 * c] * 128 + at, block_order[2 * c + 1] * 128 + (at - 128))

    def attend_chunk(r):
        zz, yy = (z + 4 - r // 2) % 4, (yh + r) % 2
        hidden = jnp.where(place_of(zz * 2 + yy, 1) <= place_of(z * 2 + yh, 0), 0.0, -jnp.inf)
        keys = kb[zz, yy].reshape(256, kb.shape[4])[:, :feat]
        for h in range(heads):
            s = lax.dot_general(qs[h], keys, (((1,), (1,)), ((), ())), preferred_element_type=F32)
            s = s + hidden
            scores[r, h] = s
            top[h] = jnp.maximum(top[h], jnp.maximum(s[:, :128], s[:, 128:]))

    def weigh(h, most, chunks):
        total = jnp.zeros((256, 128), F32)
        value = jnp.zeros((256, lat_width), F32)
        for r in chunks:
            p = jnp.exp2((scores[r, h] - most) * scale)
            total = total + (p[:, :128] + p[:, 128:])
            keys = kb[(z + 4 - r // 2) % 4, (yh + r) % 2].reshape(256, kb.shape[4])[:, :lat_width]
            value = value + jnp.dot(p.astype(BF), keys, preferred_element_type=F32)
        return total, value

    early, late = (0, 1, 2, 6), (3, 7, 4, 5)

    def begin(h):
        most = jnp.max(top[h], axis=1, keepdims=True)
        mid[h] = jnp.broadcast_to(most, mid.shape[1:])
        part[h], some[h] = weigh(h, most, early)

    def finish(h):
        most = jnp.max(top[h], axis=1, keepdims=True)
        fade = jnp.exp2((mid[h, :, :1] - most) * scale)
        total, value = weigh(h, most, late)
        total = jnp.sum(total + part[h] * fade, axis=1, keepdims=True)
        context = ((value + some[h] * fade) / total).astype(BF)
        r = jnp.dot(context, w_uv[h], preferred_element_type=F32).astype(BF)
        cols = pl.ds(pl.multiple_of(h * 128, 128), 128)
        for g in range(16):
            row = (g % 2 + co + 1) % 2 * 128 + g // 2 * 16
            out[pl.ds(pl.multiple_of(row, 16), 16), cols] = r[g * 16:g * 16 + 16]

    attend_chunk(0)
    c_by.wait_recv()
    c_b(0).start()
    c_b(1).start()
    c_ay(0).wait_recv()
    c_core(0, 1).start()
    c_a(0).wait_recv()
    c_a(3).start()
    c_ay(1).start()
    c_a(1).wait_recv()
    c_a(2).start()
    c_ay(3).start()
    for d in (1, 2, 3):
        t_x(d).wait_recv()
    t_y.start()
    c_core(0, 1).wait_recv()
    attend_chunk(1)
    c_b(0).wait_recv()
    c_b(3).start()
    c_core(1, 0).start()
    c_b(1).wait_recv()
    c_b(2).start()
    c_core(3, 0).start()
    c_a(2).wait_recv()
    c_a(3).wait_recv()
    c_ay(2).start()
    t_y.wait_recv()
    t_c.start()
    c_core(1, 0).wait_recv()
    attend_chunk(2)
    c_ay(1).wait_recv()
    c_core(1, 1).start()
    c_ay(3).wait_recv()
    c_core(3, 1).start()
    c_core(3, 0).wait_recv()
    attend_chunk(6)
    t_c.wait_recv()
    pack()
    for d in (1, 2, 3):
        t_z(d).start()
    loop(heads, begin)
    c_b(2).wait_recv()
    c_b(3).wait_recv()
    c_core(2, 0).start()
    c_ay(2).wait_recv()
    c_core(2, 1).start()
    for d in (1, 2, 3):
        t_z(d).wait_recv()
    t_h.start()
    c_core(1, 1).wait_recv()
    attend_chunk(3)
    c_core(3, 1).wait_recv()
    attend_chunk(7)
    c_core(2, 0).wait_recv()
    attend_chunk(4)
    c_core(2, 1).wait_recv()
    attend_chunk(5)
    got_w.wait()
    loop(heads, finish)
    t_h.wait_recv()
    for p in range(4):
        c_a(p).wait_send()
        c_b(p).wait_send()
        c_ay(p).wait_send()
    c_by.wait_send()
    for r in range(1, 8):
        c_core(r // 2, r % 2).wait_send()
    for d in (1, 2, 3):
        t_x(d).wait_send()
        t_z(d).wait_send()
    t_y.wait_send()
    t_c.wait_send()
    t_h.wait_send()


def project_part(heads, load, last, resid, gain, state, normed, w, *reduce_refs):
    pos = place()
    red = Reduce(reduce_refs, pos, True)

    def multiply(n):
        load(n).wait()
        t = jnp.dot(heads[...], w[n], preferred_element_type=F32)
        red.cs[n] = t[:128].astype(BF).reshape(4, 2, 16, W)
        red.c_core(n).start()
        red.own[n] = t[128:].reshape(4, 2, 16, W)

    def step(k):
        @when(k < 4)
        def _():
            multiply(2 * k)
            multiply(2 * k + 1)

        @when((k >= 1) & (k < 5))
        def _():
            red.first(k - 1)

        @when((k >= 2) & (k < 6))
        def _():
            red.second(k - 2)

        @when((k >= 3) & (k < 7))
        def _():
            red.carry(k - 3)

        @when(k >= 4)
        def _():
            red.third(k - 4)

    loop(8, step)
    for cp in last:
        cp.wait()
    square = jnp.zeros((16, 1), F32)
    for n in range(8):
        t = resid[:, n * W:(n + 1) * W].astype(F32) + red.acc[n]
        state[n] = t
        square = square + jnp.sum(t * t, axis=1, keepdims=True)
    scale = lax.rsqrt(square / (8 * W) + 1e-06)
    for n in range(8):
        normed[n] = (state[n] * scale * gain[:, n * W:(n + 1) * W]).astype(BF)
    loop(4, red.drain)


ATTEND_SEMS = [
    DMA((4,)), DMA((4,)), DMA((4,)), DMA((4,)), DMA((4,)), DMA((4,)), DMA, DMA,
    DMA((4, 2)), DMA((4, 2)),
    DMA((3,)), DMA((3,)), DMA, DMA, DMA, DMA, DMA((3,)), DMA((3,)), DMA, DMA,
]


def front_kernel(scale, block_order, queries_hbm, latent_hbm, w_uv_hbm, ids_hbm, weights_hbm, w_hbm, resid_hbm,
                 gain_hbm, state, normed, table, queries, latent, w_uv, ids, weights, resid, gain, heads, w,
                 lsem, wsem, *refs):
    loads = fetch([(latent_hbm, latent), (ids_hbm, ids), (weights_hbm, weights), (queries_hbm, queries),
                   (w_uv_hbm, w_uv), (resid_hbm, resid), (gain_hbm, gain)], lsem)

    def load(n):
        return pltpu.make_async_copy(
            w_hbm.at[:, pl.ds(pl.multiple_of(n * W, W), W)], w.at[n], wsem.at[n]
        )

    loop(8, lambda n: load(n).start())
    count = 8 + len(ATTEND_SEMS)
    attend_part(scale, loads[:5], block_order, queries, latent, w_uv, ids, weights, heads, table, *refs[:count])
    project_part(heads, load, loads[5:], resid, gain, state, normed, w, *refs[count:])


def experts_kernel(normed_hbm, table_hbm, state_hbm, wg_hbm, wd_hbm, out,
                   normed, table, state, lsem, slots, weights, hits, wg, wd, wsem, xb, rows, abuf, fa, la, bbuf, bown, lb1, b2, fb, lb2, a2, la2, suma,
                   acta, actb, yrow, fin, ret, sems, *reduce_refs):
    pos = place()
    z, yh, x, yl, co = pos
    me = z * 2 + yh
    core, ylp, xs = exp_peers(pos)
    yo = (yl + 1) % 2
    yp = dev(z, (yh + 1) % 2, x, yl, co)
    zs = [dev((z + d) % 4, yh, x, yl, co) for d in (1, 2, 3)]
    red = ReduceX(reduce_refs, pos)
    (s_in, r_in, s_gy, r_gy, s_gx, r_gx, s_gc, r_gc,
     s_a1, r_a1, s_b1, r_b1, s_b2, r_b2, s_a2, r_a2, s_ay, r_ay, s_az, r_az, s_bz, r_bz, s_by, r_by,
     s_f, r_f) = sems
    na, nb = a2.shape[1], bown.shape[2]
    n1 = na - 48
    half = nb // 2
    above, below = zs[0], zs[2]

    got_normed, got_table, got_state = fetch(
        [(normed_hbm, normed), (table_hbm, table), (state_hbm, state)], lsem)
    loads = [
        pltpu.make_async_copy(wg_hbm.at[0], wg.at[0], wsem.at[0]),
        pltpu.make_async_copy(wg_hbm.at[1], wg.at[1], wsem.at[1]),
        pltpu.make_async_copy(wd_hbm, wd, wsem.at[2]),
    ]
    for cp in loads:
        cp.start()
    ctx = [dev((z + dz) % 4, (yh + dy) % 2, x, yy, co)
           for dz in range(4) for dy in range(2) for yy in (yl, yo) if dz or dy]
    greet([core, ylp] + xs + ctx)
    got_normed.wait()

    def chunk(dz, dy):
        return ((z + 4 - dz) % 4) * 2 + (yh + dy) % 2

    def c_in(dz, dy):
        zz, yy = (z + dz) % 4, (yh + dy) % 2
        r = dz * 2 + dy
        return put(normed.at[zz * 2 + yy], xb.at[me, co, x, yl], s_in.at[r], r_in.at[r],
                   dev(zz, yy, x, yl, co))

    xb[me, co, x, yl] = normed[me]

    def c_gy(dz, dy):
        zz, yy = (z + dz) % 4, (yh + dy) % 2
        return put(normed.at[zz * 2 + yy], xb.at[me, co, x, yl], s_gy.at[dz, dy], r_gy.at[dz, dy],
                   dev(zz, yy, x, yo, co))

    for dz in (2, 1, 3, 0):
        for dy in range(2):
            if dz or dy:
                c_in(dz, dy).start()
            c_gy(dz, dy).start()

    def c_gx(dz, dy, part):
        c = chunk(dz, dy)
        r = dz * 2 + dy
        src = x if part < 2 else (x + (3 if dy else 1)) % 4
        plus = part == 0 or (part == 2 and dy == 1)
        return put(xb.at[c, co, src], xb.at[c, co, src], s_gx.at[r, part], r_gx.at[r, part], xs[0 if plus else 2])

    def c_gc(dz, dy):
        c = chunk(dz, dy)
        return put(xb.at[c, co], xb.at[c, co], s_gc.at[dz, dy], r_gc.at[dz, dy], core)

    def gather1(dz):
        @when(dz > 0)
        def _():
            c_in(dz, 0).wait_recv()
        c_in(dz, 1).wait_recv()

    def gather2(dz):
        for dy in range(2):
            c_gy(dz, dy).wait_recv()
            c_gx(dz, dy, 0).start()
            c_gx(dz, dy, 1).start()

    def gather3(dz):
        for dy in range(2):
            c_gx(dz, dy, 0).wait_recv()
            c_gx(dz, dy, 1).wait_recv()
            c_gx(dz, dy, 2).start()

    def gather4(dz):
        for dy in range(2):
            c_gx(dz, dy, 2).wait_recv()
            c_gc(dz, dy).start()

    def c_far(g, dy):
        return put(abuf.at[g, 2, dy], fa.at[g, dy], s_a1.at[g, 0, dy], r_a1.at[g, 0, dy], above if dy else below)

    def c_below(g, dy):
        return put(abuf.at[g, 1, dy], la.at[g, 0, dy], s_a1.at[g, 1, dy], r_a1.at[g, 1, dy], below)

    def c_above(g, dy):
        return put(abuf.at[g, 3, dy], la.at[g, 1, dy], s_a1.at[g, 2, dy], r_a1.at[g, 2, dy], above)

    def c_b1(g, dz):
        return put(bbuf.at[g, dz], lb1.at[g, dz], s_b1.at[g, dz], r_b1.at[g, dz], yp)

    def part(h):
        return pl.ds(h * half, half)

    def c_bfar(g, h):
        return put(b2.at[g, 2, part(h)], fb.at[g, part(h)], s_b2.at[g, 0, h], r_b2.at[g, 0, h],
                   above if h else below)

    def c_bbelow(g, h):
        return put(b2.at[g, 1, part(h)], lb2.at[g, 0, part(h)], s_b2.at[g, 1, h], r_b2.at[g, 1, h], below)

    def c_babove(g, h):
        return put(b2.at[g, 3, part(h)], lb2.at[g, 1, part(h)], s_b2.at[g, 2, h], r_b2.at[g, 2, h], above)

    def c_a2(g):
        return put(a2.at[g], la2.at[g], s_a2.at[g], r_a2.at[g], yp)

    def c_ay(g):
        return put(acta.at[g, z, yh], acta.at[g, z, yh], s_ay.at[g], r_ay.at[g], yp)

    def c_az(g, p):
        if p < 2:
            src = acta.at[g, z]
        elif p == 2:
            src = acta.at[g, (z + 1) % 4, 0]
        else:
            src = acta.at[g, (z + 3) % 4, 1]
        return put(src, src, s_az.at[g, p], r_az.at[g, p], above if p in (0, 3) else below)

    def c_bz(g, p):
        if p < 2:
            src = actb.at[g, z, yh]
        elif p == 2:
            src = actb.at[g, (z + 1) % 4, yh, part(0)]
        else:
            src = actb.at[g, (z + 3) % 4, yh, part(1)]
        return put(src, src, s_bz.at[g, p], r_bz.at[g, p], above if p in (0, 3) else below)

    def c_by(g, dz):
        zz = (z + 4 - dz) % 4
        return put(actb.at[g, zz, yh], actb.at[g, zz, yh], s_by.at[g, dz], r_by.at[g, dz], yp)

    def find(k):
        for i in range(2):
            mine = table[k, :8, :] == (lax.axis_index("exp") * 2 + i).astype(F32)
            hits[k, i:i + 1, :] = jnp.max(jnp.where(mine, 1.0, 0.0), axis=0, keepdims=True)
            weights[k, i:i + 1, :] = jnp.sum(jnp.where(mine, table[k, 8:, :], 0.0), axis=0, keepdims=True)

    got_table.wait()
    loop(8, find)
    one, two = (lax.broadcasted_iota(jnp.int32, (256, 256), a) for a in (0, 1))
    before = jnp.where((one < two) & (one // 16 == two // 16), 1.0, 0.0).astype(BF)
    block = (lax.broadcasted_iota(jnp.int32, (2, 256), 1) // 16 * 6).astype(F32)

    def rank(k):
        r = jnp.dot(hits[k].astype(BF), before, preferred_element_type=F32)
        slots[k] = jnp.where(hits[k] > 0.5, block + r, -1.0)

    loop(8, rank)
    row_id = lax.broadcasted_iota(jnp.int32, (48, 128), 0).astype(F32)

    def chosen(c, i, g):
        tokens = slice(g * 128, g * 128 + 128)
        return row_id == slots[c, i:i + 1, tokens] - 48.0 * g, weights[c, i:i + 1, tokens]

    def gate_up(dz):
        for dy in range(2):
            c_gc(dz, dy).wait_recv()
            c = chunk(dz, dy)
            for g in range(2):
                tokens = xb[c, g].reshape(128, W)
                for i in range(2):
                    pick = chosen(c, i, g)[0].astype(BF)
                    rows[i, g, dy * 48:(dy + 1) * 48] = jnp.dot(
                        pick, tokens, preferred_element_type=F32).astype(BF)

        def cols(t):
            sl = pl.ds(pl.multiple_of(t * 512, 512), 512)
            r = jnp.dot(rows[0].reshape(192, W), wg[0, :, sl], preferred_element_type=F32)
            abuf[:, dz, :, :48, sl] = r.astype(BF).reshape(2, 2, 48, 512)
            r = jnp.dot(rows[1].reshape(192, W), wg[1, :, sl], preferred_element_type=F32)
            r = r.astype(BF).reshape(2, 2, 48, 512)
            abuf[:, dz, :, 48:, sl] = r[:, :, :n1]
            bown[:, dz, :, sl] = r[:, 0, n1:]
            bbuf[:, dz, :, sl] = r[:, 1, n1:]

        loop(4, cols)

        @when(dz == 2)
        def _():
            c_far(0, 0).start()
            c_far(0, 1).start()

        @when(dz == 1)
        def _():
            c_below(0, 1).start()

        @when(dz == 3)
        def _():
            c_above(0, 0).start()

        c_b1(0, dz).start()

    def carry_a(g):
        for dy, dz, c in ((0, 1, c_below), (1, 3, c_above)):
            c_far(g, dy).wait_recv()

            def cols(t):
                sl = pl.ds(pl.multiple_of(t * 512, 512), 512)
                abuf[g, dz, dy, :, sl] = (abuf[g, dz, dy, :, sl].astype(F32) + fa[g, dy, :, sl].astype(F32)).astype(BF)

            loop(4, cols)
            c(g, dy).start()

    def forward_b(g):
        def one(dz):
            c_b1(g, dz).wait_recv()
            b2[g, dz] = (bown[g, dz].astype(F32) + lb1[g, dz].astype(F32)).astype(BF)

        loop(4, one)
        c_bfar(g, 0).start()
        c_bfar(g, 1).start()
        c_bbelow(g, 1).start()
        c_babove(g, 0).start()

    def carry_b(g):
        for h, dz, c in ((0, 1, c_bbelow), (1, 3, c_babove)):
            c_bfar(g, h).wait_recv()
            b2[g, dz, part(h)] = (b2[g, dz, part(h)].astype(F32) + fb[g, part(h)].astype(F32)).astype(BF)
            c(g, h).start()

    def sum_a(g):
        for dy in range(2):
            c_below(g, dy).wait_recv()
            c_above(g, dy).wait_recv()

        def cols(t):
            sl = pl.ds(pl.multiple_of(t * 512, 512), 512)

            def total(dy):
                r = abuf[g, 0, dy, :, sl].astype(F32)
                return r + la[g, 0, dy, :, sl].astype(F32) + la[g, 1, dy, :, sl].astype(F32)

            a2[g, :, sl] = total(1).astype(BF)
            suma[g, :, sl] = total(0)

        loop(4, cols)
        c_a2(g).start()

    def activate(gate, up):
        return (gate / (1.0 + jnp.exp(-gate)) * up).astype(BF)

    def halves(t):
        return tuple(pl.ds(pl.multiple_of(t * 256 + o, 256), 256) for o in (0, wd.shape[1]))

    def act_a(g):
        c_a2(g).wait_recv()

        def cols(t):
            def total(sl):
                return suma[g, :, sl] + la2[g, :, sl].astype(F32)

            lo, hi = halves(t)
            acta[g, z, yh, :, lo] = activate(total(lo), total(hi))

        loop(4, cols)
        c_ay(g).start()

    def act_b(g):
        for h in range(2):
            c_bbelow(g, h).wait_recv()
            c_babove(g, h).wait_recv()

        def cols(t):
            def total(sl):
                r = b2[g, 0, :, sl].astype(F32)
                return r + lb2[g, 0, :, sl].astype(F32) + lb2[g, 1, :, sl].astype(F32)

            lo, hi = halves(t)
            actb[g, z, yh, :, lo] = activate(total(lo), total(hi))

        loop(4, cols)
        c_bz(g, 0).start()
        c_bz(g, 1).start()
        c_by(g, 0).start()

    def spread_a(g):
        c_ay(g).wait_recv()
        c_az(g, 0).start()
        c_az(g, 1).start()

    def pass_on(g):
        for p in range(2):
            c_bz(g, p).wait_recv()
            c_bz(g, 3 - p).start()
        c_by(g, 1).start()
        c_by(g, 3).start()
        for p in range(2):
            c_az(g, p).wait_recv()
            c_az(g, 3 - p).start()

    def pass_far(g):
        c_bz(g, 2).wait_recv()
        c_bz(g, 3).wait_recv()
        c_by(g, 2).start()

    def order(k):
        return 2 - k + 3 * (k // 2) - 2 * (k // 3)

    def step(k):
        @when(k < 4)
        def _():
            gather1(order(k))

        @when((k >= 1) & (k < 5))
        def _():
            gather2(order(k - 1))

        @when((k >= 2) & (k < 6))
        def _():
            gather3(order(k - 2))

        @when(k == 4)
        def _():
            loads[0].wait()
            loads[1].wait()

        @when(k >= 4)
        def _():
            gate_up(order(k - 4))

        @when((k >= 3) & (k < 7))
        def _():
            gather4(order(k - 3))

    loop(8, step)
    def nearest(k):
        return k + k // 2 - 2 * (k // 3)

    def down(g, k):
        dz = nearest(k)
        zz = (z + 4 - dz) % 4

        if k == 3:
            c_az(g, 2).wait_recv()
            c_az(g, 3).wait_recv()
        c_by(g, dz).wait_recv()
        yrow[0] = jnp.dot(acta[g, zz, :, :48].reshape(96, -1), wd[0], preferred_element_type=F32).astype(BF)
        one = jnp.concatenate([acta[g, zz, :, 48:], actb[g, zz]], axis=1).reshape(96, -1)
        yrow[1] = jnp.dot(one, wd[1], preferred_element_type=F32).astype(BF)
        for dy in range(2):
            yy = (yh + dy) % 2
            c = zz * 2 + yy
            n = k * 2 + dy
            pick = jnp.concatenate([jnp.where(*chosen(c, i, g), 0.0) for i in range(2)], axis=0).astype(BF)
            sl = pl.ds(pl.multiple_of(yy * 48, 16), 48)
            t = lax.dot_general(
                pick, jnp.concatenate([yrow[0, sl], yrow[1, sl]], axis=0), (((0,), (0,)), ((), ())),
                preferred_element_type=F32).reshape(4, 2, 16, W)

            @when(co == g)
            def _():
                red.own[n] = t

            @when(co != g)
            def _():
                red.cs[n] = t.astype(BF)
                red.c_core(n).start()

    def c_f(k, dy):
        zz, yy = (z + 4 - nearest(k)) % 4, (yh + dy) % 2
        r = k * 2 + dy
        return put(fin.at[r], ret.at[me], s_f.at[r], r_f.at[r], dev(zz, yy, x, yl, co))

    def send_back(k):
        red.third(k)
        for dy in range(2):
            n = k * 2 + dy
            fin[n] = red.acc[n].astype(BF)
            if n:
                c_f(k, dy).start()

    def back(g, *stages):
        @when(co == g)
        def _():
            for stage, k in stages:
                stage(k)

    first, second, carry = red.first, red.second, red.carry
    carry_a(0)
    c_far(1, 0).start()
    c_far(1, 1).start()
    c_below(1, 1).start()
    c_above(1, 0).start()
    for dz in (2, 1, 3, 0):
        c_b1(1, dz).start()
    forward_b(0)
    sum_a(0)
    carry_b(0)
    act_a(0)
    carry_a(1)
    act_b(0)
    spread_a(0)
    forward_b(1)
    sum_a(1)
    carry_b(1)
    loads[2].wait()
    pass_on(0)
    down(0, 0)
    act_a(1)
    back(0, (first, 0))
    act_b(1)
    down(0, 1)
    spread_a(1)
    back(0, (second, 0), (first, 1))
    down(0, 2)
    back(0, (carry, 0), (second, 1), (first, 2))
    pass_far(0)
    down(0, 3)
    pass_on(1)
    down(1, 0)
    back(0, (send_back, 0), (carry, 1), (second, 2), (first, 3))
    back(1, (first, 0))
    down(1, 1)
    back(1, (second, 0), (first, 1))
    down(1, 2)
    back(1, (carry, 0), (second, 1), (first, 2))
    back(0, (send_back, 1), (carry, 2), (second, 3))
    pass_far(1)
    down(1, 3)
    back(1, (first, 3), (send_back, 0), (carry, 1), (second, 2))
    back(0, (send_back, 2), (carry, 3))
    back(1, (second, 3), (send_back, 1), (carry, 2))
    back(1, (carry, 3), (send_back, 2))
    back(1, (send_back, 3))
    back(0, (send_back, 3))
    got_state.wait()
    ret[me] = fin[0]
    for r in range(1, 8):
        c_f(r // 2, r % 2).wait_recv()
    for n in range(8):
        out[:, n * W:(n + 1) * W] = (state[n] + ret[n].astype(F32)).astype(BF)

    loop(4, red.drain)
    for r in range(1, 8):
        c_f(r // 2, r % 2).wait_send()
        c_in(r // 2, r % 2).wait_send()
    for dz in range(4):
        for dy in range(2):
            for p in range(3):
                c_gx(dz, dy, p).wait_send()
            c_gy(dz, dy).wait_send()
            c_gc(dz, dy).wait_send()
        for g in range(2):
            c_b1(g, dz).wait_send()
            c_by(g, dz).wait_send()
    for g in range(2):
        for h in range(2):
            c_far(g, h).wait_send()
            c_below(g, h).wait_send()
            c_above(g, h).wait_send()
            c_bfar(g, h).wait_send()
            c_bbelow(g, h).wait_send()
            c_babove(g, h).wait_send()
        for p in range(4):
            c_az(g, p).wait_send()
            c_bz(g, p).wait_send()
        c_a2(g).wait_send()
        c_ay(g).wait_send()


VM = pl.BlockSpec(memory_space=pltpu.VMEM)
ANY = pl.BlockSpec(memory_space=pl.ANY)


def experts(normed, table, state, w_gate_up, w_down):
    hid2 = w_gate_up.shape[2]
    hid = hid2 // 2
    na, nb = 64, 32
    sems = [
        DMA((8,)), DMA((8,)),
        DMA((4, 2)), DMA((4, 2)), DMA((8, 3)), DMA((8, 3)),
        DMA((4, 2)), DMA((4, 2)),
        DMA((2, 3, 2)), DMA((2, 3, 2)), DMA((2, 4)), DMA((2, 4)), DMA((2, 3, 2)), DMA((2, 3, 2)),
        DMA((2,)), DMA((2,)), DMA((2,)), DMA((2,)), DMA((2, 4)), DMA((2, 4)), DMA((2, 4)), DMA((2, 4)),
        DMA((2, 4)), DMA((2, 4)),
        DMA((8,)), DMA((8,)),
    ]
    return pl.pallas_call(
        experts_kernel,
        name="experts",
        out_shape=jax.ShapeDtypeStruct((16, 8 * W), BF),
        in_specs=[ANY] * 5,
        out_specs=VM,
        scratch_shapes=[
            pltpu.VMEM(normed.shape, BF),
            pltpu.VMEM(table.shape, F32),
            pltpu.VMEM(state.shape, F32),
            DMA((3,)),
            pltpu.VMEM((8, 2, 256), F32),
            pltpu.VMEM((8, 2, 256), F32),
            pltpu.VMEM((8, 2, 256), F32),
            pltpu.VMEM((2, W, hid2), BF),
            pltpu.VMEM((2, hid, W), BF),
            DMA((3,)),
            pltpu.VMEM((8, 2, 4, 2, 16, W), BF),
            pltpu.VMEM((2, 2, 96, W), BF),
            pltpu.VMEM((2, 4, 2, na, hid2), BF),
            pltpu.VMEM((2, 2, na, hid2), BF),
            pltpu.VMEM((2, 2, 2, na, hid2), BF),
            pltpu.VMEM((2, 4, nb, hid2), BF),
            pltpu.VMEM((2, 4, nb, hid2), BF),
            pltpu.VMEM((2, 4, nb, hid2), BF),
            pltpu.VMEM((2, 4, nb, hid2), BF),
            pltpu.VMEM((2, nb, hid2), BF),
            pltpu.VMEM((2, 2, nb, hid2), BF),
            pltpu.VMEM((2, na, hid2), BF),
            pltpu.VMEM((2, na, hid2), BF),
            pltpu.VMEM((2, na, hid2), F32),
            pltpu.VMEM((2, 4, 2, na, hid), BF),
            pltpu.VMEM((2, 4, 2, nb, hid), BF),
            pltpu.VMEM((2, 96, W), BF),
            pltpu.VMEM((8, 16, W), BF),
            pltpu.VMEM((8, 16, W), BF),
            tuple(sems),
        ] + REDUCE_X_SCRATCH,
        compiler_params=pltpu.CompilerParams(
            collective_id=2, has_side_effects=True, vmem_limit_bytes=62 << 20),
    )(normed, table, state, w_gate_up, w_down)


def front(block_order, queries, latent, w_uv, ids, weights, w_out, resid, gain):
    heads_dev, feat_width, query_count = queries.shape
    lat_width, value_width = w_uv.shape[1:]
    score_scale = (value_width + feat_width - lat_width) ** (-0.5)
    return pl.pallas_call(
        functools.partial(front_kernel, score_scale * 1.4426950408889634),
        name="front",
        out_shape=(
            jax.ShapeDtypeStruct((8, 16, W), F32),
            jax.ShapeDtypeStruct((8, 16, W), BF),
            jax.ShapeDtypeStruct((4, 2, 16, 256), F32),
        ),
        in_specs=[pl.BlockSpec(memory_space=pltpu.SMEM)] + [ANY] * 8,
        out_specs=(VM, VM, VM),
        scratch_shapes=[
            pltpu.VMEM(queries.shape, BF),
            pltpu.VMEM(latent.shape, BF),
            pltpu.VMEM(w_uv.shape, BF),
            pltpu.VMEM(ids.shape, jnp.int32),
            pltpu.VMEM(weights.shape, F32),
            pltpu.VMEM(resid.shape, BF),
            pltpu.VMEM(gain.shape, F32),
            pltpu.VMEM((query_count, heads_dev * value_width), BF),
            pltpu.VMEM((8, 768, W), BF),
            DMA((7,)),
            DMA((8,)),
            pltpu.VMEM((4, 2, 2, 128, (feat_width + 127) // 128 * 128), BF),
            pltpu.VMEM((2, 4, 2, 16, 128), BF),
            pltpu.VMEM((heads_dev, query_count, feat_width), BF),
            pltpu.VMEM((heads_dev, query_count, 128), F32),
            pltpu.VMEM((8, heads_dev, query_count, 256), F32),
            pltpu.VMEM((heads_dev, query_count, 128), F32),
            pltpu.VMEM((heads_dev, query_count, 128), F32),
            pltpu.VMEM((heads_dev, query_count, lat_width), F32),
        ] + ATTEND_SEMS + REDUCE_SCRATCH,
        compiler_params=pltpu.CompilerParams(
            collective_id=3, has_side_effects=True, vmem_limit_bytes=62 << 20),
    )(block_order, queries, latent, w_uv, ids, weights, w_out, resid, gain)


def body(queries, latent, block_order, w_uv, w_out, resid, norm_gain, expert_ids, route_weights, w_gate_up, w_down):
    state, normed, table = front(
        block_order, queries.transpose(1, 2, 0), latent.T, w_uv, expert_ids.T, route_weights.T,
        w_out, resid, norm_gain.reshape(1, -1))
    return experts(normed, table.reshape(8, 16, 256), state, w_gate_up, w_down)


def solution(mesh):
    return jax.shard_map(
        body,
        mesh=mesh,
        in_specs=(
            P("ctx", "exp", None),
            P("ctx", None),
            P(),
            P("exp", None, None),
            P("exp", None),
            P(("ctx", "exp"), None),
            P(),
            P(("ctx", "exp"), None),
            P(("ctx", "exp"), None),
            P("exp", "ctx", None),
            P("exp", None, "ctx"),
        ),
        out_specs=P(("ctx", "exp"), None),
        check_vma=False,
    )
```

```python
import functools

import jax
import jax.numpy as jnp
from jax import lax
from jax.experimental import pallas as pl
from jax.experimental.pallas import tpu as pltpu
from jax.sharding import PartitionSpec as P

BF = jnp.bfloat16
F32 = jnp.float32
DMA = pltpu.SemaphoreType.DMA
W = 896


def place():
    c = lax.axis_index("ctx")
    e = lax.axis_index("exp")
    return c // 2, c % 2, e // 4, (e // 2) % 2, e % 2


def dev(z, yh, x, yl, co):
    return (z * 2 + yh, x * 4 + yl * 2 + co)


def put(src, dst, ss, rs, device):
    return pltpu.make_async_remote_copy(
        src_ref=src,
        dst_ref=dst,
        send_sem=ss,
        recv_sem=rs,
        device_id=device,
        device_id_type=pl.DeviceIdType.MESH,
    )


def greet(devices):
    barrier = pltpu.get_barrier_semaphore()
    for d in devices:
        pl.semaphore_signal(barrier, inc=1, device_id=d, device_id_type=pl.DeviceIdType.MESH)
    pl.semaphore_wait(barrier, len(devices))


def exp_peers(pos):
    z, yh, x, yl, co = pos
    core = dev(z, yh, x, yl, (co + 1) % 2)
    ylp = dev(z, yh, x, (yl + 1) % 2, co)
    xs = [dev(z, yh, (x + d) % 4, yl, co) for d in (1, 2, 3)]
    return core, ylp, xs


REDUCE_SCRATCH = [
    pltpu.VMEM((8, 4, 2, 16, W), F32),
    pltpu.VMEM((8, 4, 2, 16, W), BF),
    pltpu.VMEM((8, 4, 2, 16, W), BF),
    pltpu.VMEM((8, 4, 2, 16, W), BF),
    pltpu.VMEM((4, 3, 2, 16, W), BF),
    pltpu.VMEM((4, 2, 16, W), BF),
    pltpu.VMEM((8, 4, 16, W), BF),
    pltpu.VMEM((4, 16, W), BF),
    pltpu.VMEM((8, 3, 16, W), BF),
    pltpu.VMEM((4, 16, W), BF),
    pltpu.VMEM((8, 3, 16, W), BF),
    pltpu.VMEM((8, 16, W), F32),
    DMA((8,)),
    DMA((8,)),
    DMA((4, 3)),
    DMA((4, 3)),
    DMA((8,)),
    DMA((8,)),
    DMA((4,)),
    DMA((4,)),
    DMA((8, 3)),
    DMA((8, 3)),
]


class Reduce:
    def __init__(self, refs, pos, crossed):
        (self.own, self.cs, self.cl, self.s1, self.x1, self.xc, self.y1, self.y2s, self.x2s, self.y2,
         self.x2, self.acc, *self.sems) = refs
        self.pos = pos
        self.crossed = crossed
        self.core, self.ylp, self.xs = exp_peers(pos)

    def c_core(self, n):
        return put(self.cs.at[n], self.cl.at[n], self.sems[0].at[n], self.sems[1].at[n], self.core)

    def c_x1(self, i, part):
        z, yh, x, yl, co = self.pos
        way = 1 + 2 * (i % 2)
        if part == 2:
            src = self.xc.at[i]
        else:
            src = self.s1.at[2 * i, (x + (2 if part == 0 else 4 - way)) % 4]
        to = (x + (4 - way if part == 1 else way)) % 4
        return put(src, self.x1.at[i, part], self.sems[2].at[i, part], self.sems[3].at[i, part],
                   dev(z, yh, to, yl, co))

    def c_y1(self, n):
        return put(self.s1.at[n, :, (self.pos[3] + 1) % 2], self.y1.at[n], self.sems[4].at[n],
                   self.sems[5].at[n], self.ylp)

    def c_y2(self, i):
        return put(self.y2s.at[i], self.y2.at[i], self.sems[6].at[i], self.sems[7].at[i], self.ylp)

    def c_x2(self, n, part, odd):
        plus = (part == 1) == odd
        return put(self.x2s.at[n, part], self.x2.at[n, part], self.sems[8].at[n, part],
                   self.sems[9].at[n, part], self.xs[0 if plus else 2])

    def over_y(self, n, xx):
        return self.s1[n, xx, self.pos[3]].astype(F32) + self.y1[n, xx].astype(F32)

    def first(self, i):
        for j in range(2):
            n = 2 * i + j
            self.c_core(n).wait_recv()
            self.s1[n] = (self.own[n] + self.cl[n].astype(F32)).astype(BF)
            if self.crossed and j == 0:
                self.c_x1(i, 0).start()
                self.c_x1(i, 1).start()
            else:
                self.c_y1(n).start()

    def second(self, i):
        x, yl = self.pos[2], self.pos[3]
        for j in range(2):
            n = 2 * i + j
            if self.crossed and j == 0:
                self.c_x1(i, 0).wait_recv()
                near = (x + 1 + 2 * (i % 2)) % 4
                self.xc[i] = (self.s1[n, near].astype(F32) + self.x1[i, 0].astype(F32)).astype(BF)
                self.c_x1(i, 2).start()
            else:
                self.c_y1(n).wait_recv()
                for part, d in ((0, 2), (1, 1 if j else 3)):
                    self.x2s[n, part] = self.over_y(n, (x + d) % 4).astype(BF)
                    self.c_x2(n, part, j == 1).start()
                self.acc[n] = self.over_y(n, x)

    def carry(self, i):
        for j in range(2):
            n = 2 * i + j
            if self.crossed and j == 0:
                self.c_x1(i, 1).wait_recv()
                self.c_x1(i, 2).wait_recv()

                def over_x(which):
                    t = self.s1[n, self.pos[2], which].astype(F32)
                    return t + self.x1[i, 1, which].astype(F32) + self.x1[i, 2, which].astype(F32)

                self.y2s[i] = over_x((self.pos[3] + 1) % 2).astype(BF)
                self.c_y2(i).start()
                self.acc[n] = over_x(self.pos[3])
            else:
                self.c_x2(n, 0, j == 1).wait_recv()
                xx = (self.pos[2] + (3 if j else 1)) % 4
                self.x2s[n, 2] = (self.over_y(n, xx) + self.x2[n, 0].astype(F32)).astype(BF)
                self.c_x2(n, 2, j == 1).start()

    def third(self, i):
        for j in range(2):
            n = 2 * i + j
            t = self.acc[n]
            if self.crossed and j == 0:
                self.c_y2(i).wait_recv()
                t = t + self.y2[i].astype(F32)
            else:
                for part in (1, 2):
                    self.c_x2(n, part, j == 1).wait_recv()
                    t = t + self.x2[n, part].astype(F32)
            self.acc[n] = t

    def drain(self, i):
        for j in range(2):
            n = 2 * i + j
            self.c_core(n).wait_send()
            if self.crossed and j == 0:
                self.c_y2(i).wait_send()
            else:
                self.c_y1(n).wait_send()
            for d in (1, 2, 3):
                if self.crossed and j == 0:
                    self.c_x1(i, d - 1).wait_send()
                else:
                    self.c_x2(n, d - 1, j == 1).wait_send()


REDUCE_X_SCRATCH = [
    pltpu.VMEM((8, 4, 2, 16, W), F32),
    pltpu.VMEM((8, 4, 2, 16, W), BF),
    pltpu.VMEM((8, 4, 2, 16, W), BF),
    pltpu.VMEM((8, 4, 2, 16, W), BF),
    pltpu.VMEM((8, 2, 16, W), BF),
    pltpu.VMEM((8, 3, 2, 16, W), BF),
    pltpu.VMEM((8, 16, W), BF),
    pltpu.VMEM((8, 16, W), BF),
    pltpu.VMEM((8, 16, W), F32),
    DMA((8,)),
    DMA((8,)),
    DMA((8, 3)),
    DMA((8, 3)),
    DMA((8,)),
    DMA((8,)),
]


class ReduceX:
    def __init__(self, refs, pos):
        (self.own, self.cs, self.cl, self.s1, self.xc, self.xl, self.ys, self.yr, self.acc, *self.sems) = refs
        self.pos = pos
        self.core, self.ylp, self.xs = exp_peers(pos)

    def c_core(self, n):
        return put(self.cs.at[n], self.cl.at[n], self.sems[0].at[n], self.sems[1].at[n], self.core)

    def c_x(self, n, part, odd):
        x = self.pos[2]
        if part == 2:
            src = self.xc.at[n]
        else:
            src = self.s1.at[n, (x + 2) % 4 if part == 0 else (x + (1 if odd else 3)) % 4]
        plus = (part == 1) == odd
        return put(src, self.xl.at[n, part], self.sems[2].at[n, part], self.sems[3].at[n, part],
                   self.xs[0 if plus else 2])

    def c_y(self, n):
        return put(self.ys.at[n], self.yr.at[n], self.sems[4].at[n], self.sems[5].at[n], self.ylp)

    def first(self, i):
        for j in range(2):
            n = 2 * i + j
            self.c_core(n).wait_recv()
            self.s1[n] = (self.own[n] + self.cl[n].astype(F32)).astype(BF)
            self.c_x(n, 0, j == 1).start()
            self.c_x(n, 1, j == 1).start()

    def second(self, i):
        for j in range(2):
            n = 2 * i + j
            self.c_x(n, 0, j == 1).wait_recv()
            near = (self.pos[2] + (3 if j else 1)) % 4
            self.xc[n] = (self.s1[n, near].astype(F32) + self.xl[n, 0].astype(F32)).astype(BF)
            self.c_x(n, 2, j == 1).start()

    def carry(self, i):
        x, yl = self.pos[2], self.pos[3]
        for j in range(2):
            n = 2 * i + j
            self.c_x(n, 1, j == 1).wait_recv()
            self.c_x(n, 2, j == 1).wait_recv()

            def over_x(which):
                t = self.s1[n, x, which].astype(F32)
                return t + self.xl[n, 1, which].astype(F32) + self.xl[n, 2, which].astype(F32)

            self.ys[n] = over_x((yl + 1) % 2).astype(BF)
            self.c_y(n).start()
            self.acc[n] = over_x(yl)

    def third(self, i):
        for j in range(2):
            n = 2 * i + j
            self.c_y(n).wait_recv()
            self.acc[n] = self.acc[n] + self.yr[n].astype(F32)

    def drain(self, i):
        for j in range(2):
            n = 2 * i + j
            self.c_core(n).wait_send()
            self.c_y(n).wait_send()
            for part in range(3):
                self.c_x(n, part, j == 1).wait_send()


def loop(count, step):
    def body(k, carry):
        step(k)
        return carry

    lax.fori_loop(0, count, body, 0)


def when(cond):
    return pl.when(cond)


def fetch(pairs, sems):
    copies = [pltpu.make_async_copy(src, dst, sems.at[i]) for i, (src, dst) in enumerate(pairs)]
    for cp in copies:
        cp.start()
    return copies


def attend_part(scale, loads, block_order, queries, latent, w_uv, ids, weights, out, table,
                  kb, near, qs, top, scores, mid, part, some,
                  s_a, r_a, s_ay, r_ay, s_b, r_b, s_by, r_by, s_c, r_c,
                  s_tx, r_tx, s_ty, r_ty, s_tc, r_tc, s_tz, r_tz, s_th, r_th):
    pos = place()
    z, yh, x, yl, co = pos
    core, ylp, xs = exp_peers(pos)
    yp = dev(z, (yh + 1) % 2, x, yl, co)
    zs = [dev((z + d) % 4, yh, x, yl, co) for d in (1, 2, 3)]
    above, below = zs[0], zs[2]
    feat = latent.shape[0]
    heads = queries.shape[0]
    lat_width = w_uv.shape[1]
    greet([core, ylp, yp] + xs + zs)
    got_latent, got_ids, got_weights, got_queries, got_w = loads

    def c_a(p):
        plane, first, count = ((0, 0, 64), (0, 0, 64), (1, 0, 32), (3, 32, 32))[p]
        src = kb.at[(z + plane) % 4, yh, co, pl.ds(first, count)]
        return put(src, src, s_a.at[p], r_a.at[p], above if p in (0, 3) else below)

    def c_ay(dz):
        src = kb.at[(z + 4 - dz) % 4, yh, co, pl.ds(0, 64)]
        return put(src, src, s_ay.at[dz], r_ay.at[dz], yp)

    def c_b(p):
        if p < 2:
            src = kb.at[z, :, co, pl.ds(64, 64)]
        elif p == 2:
            src = kb.at[(z + 1) % 4, 0, co, pl.ds(64, 64)]
        else:
            src = kb.at[(z + 3) % 4, 1, co, pl.ds(64, 64)]
        return put(src, src, s_b.at[p], r_b.at[p], above if p in (0, 3) else below)

    own = kb.at[z, yh, co, pl.ds(64, 64)]
    c_by = put(own, own, s_by, r_by, yp)

    def c_core(dz, dy):
        src = kb.at[(z + 4 - dz) % 4, (yh + dy) % 2, co]
        return put(src, src, s_c.at[dz, dy], r_c.at[dz, dy], core)

    got_latent.wait()
    kb[z, yh, :, :, feat:] = jnp.zeros((2, 128, kb.shape[4] - feat), BF)
    kb[z, yh, :, :, :feat] = latent[...].T.reshape(2, 128, feat)
    c_a(0).start()
    c_a(1).start()
    c_by.start()
    c_ay(0).start()

    got_ids.wait()
    got_weights.wait()
    near[co, x, yl] = jnp.zeros((16, 128), BF)
    near[co, x, yl, :, :16] = jnp.concatenate([ids[...].astype(F32), weights[...]], axis=0).astype(BF)

    def t_x(d):
        src = near.at[co, x, yl]
        return put(src, src, s_tx.at[d - 1], r_tx.at[d - 1], xs[d - 1])

    def t_z(d):
        src = table.at[z, yh]
        return put(src, src, s_tz.at[d - 1], r_tz.at[d - 1], zs[d - 1])

    t_y = put(near.at[co, :, yl], near.at[co, :, yl], s_ty, r_ty, ylp)
    t_c = put(near.at[co], near.at[co], s_tc, r_tc, core)
    t_h = put(table.at[:, yh], table.at[:, yh], s_th, r_th, yp)
    for d in (1, 2, 3):
        t_x(d).start()

    def pack():
        row = lax.broadcasted_iota(jnp.int32, (128, 256), 0)
        col = lax.broadcasted_iota(jnp.int32, (128, 256), 1)
        t = jnp.zeros((16, 256), F32)
        for i in range(16):
            move = jnp.where((col - row == 16 * i) & (row < 16), 1.0, 0.0).astype(BF)
            t = t + jnp.dot(near[i // 8, i // 2 % 4, i % 2], move, preferred_element_type=F32)
        table[z, yh] = t

    def turn(h):
        qs[h] = queries[h].T

    got_queries.wait()
    loop(heads, turn)
    top[...] = jnp.full(top.shape, -jnp.inf, F32)

    def place_of(c, axis):
        shape = (1, 256) if axis else (256, 1)
        at = lax.broadcasted_iota(jnp.int32, shape, axis)
        return jnp.where(at < 128, block_order[2 * c] * 128 + at, block_order[2 * c + 1] * 128 + (at - 128))

    def attend_chunk(r):
        zz, yy = (z + 4 - r // 2) % 4, (yh + r) % 2
        hidden = jnp.where(place_of(zz * 2 + yy, 1) <= place_of(z * 2 + yh, 0), 0.0, -jnp.inf)
        keys = kb[zz, yy].reshape(256, kb.shape[4])[:, :feat]
        for h in range(heads):
            s = lax.dot_general(qs[h], keys, (((1,), (1,)), ((), ())), preferred_element_type=F32)
            s = s + hidden
            scores[r, h] = s
            top[h] = jnp.maximum(top[h], jnp.maximum(s[:, :128], s[:, 128:]))

    def weigh(h, most, chunks):
        total = jnp.zeros((256, 128), F32)
        value = jnp.zeros((256, lat_width), F32)
        for r in chunks:
            p = jnp.exp2((scores[r, h] - most) * scale)
            total = total + (p[:, :128] + p[:, 128:])
            keys = kb[(z + 4 - r // 2) % 4, (yh + r) % 2].reshape(256, kb.shape[4])[:, :lat_width]
            value = value + jnp.dot(p.astype(BF), keys, preferred_element_type=F32)
        return total, value

    early, late = (0, 1, 2, 6), (3, 7, 4, 5)

    def begin(h):
        most = jnp.max(top[h], axis=1, keepdims=True)
        mid[h] = jnp.broadcast_to(most, mid.shape[1:])
        part[h], some[h] = weigh(h, most, early)

    def finish(h):
        most = jnp.max(top[h], axis=1, keepdims=True)
        fade = jnp.exp2((mid[h, :, :1] - most) * scale)
        total, value = weigh(h, most, late)
        total = jnp.sum(total + part[h] * fade, axis=1, keepdims=True)
        context = ((value + some[h] * fade) / total).astype(BF)
        r = jnp.dot(context, w_uv[h], preferred_element_type=F32).astype(BF)
        cols = pl.ds(pl.multiple_of(h * 128, 128), 128)
        for g in range(16):
            row = (g % 2 + co + 1) % 2 * 128 + g // 2 * 16
            out[pl.ds(pl.multiple_of(row, 16), 16), cols] = r[g * 16:g * 16 + 16]

    c_by.wait_recv()
    c_b(0).start()
    c_b(1).start()
    c_ay(0).wait_recv()
    c_core(0, 1).start()
    c_a(0).wait_recv()
    c_a(3).start()
    c_ay(1).start()
    c_a(1).wait_recv()
    c_a(2).start()
    c_ay(3).start()
    attend_chunk(0)
    for d in (1, 2, 3):
        t_x(d).wait_recv()
    t_y.start()
    c_core(0, 1).wait_recv()
    attend_chunk(1)
    c_b(0).wait_recv()
    c_b(3).start()
    c_core(1, 0).start()
    c_b(1).wait_recv()
    c_b(2).start()
    c_core(3, 0).start()
    c_a(2).wait_recv()
    c_a(3).wait_recv()
    c_ay(2).start()
    t_y.wait_recv()
    t_c.start()
    c_core(1, 0).wait_recv()
    attend_chunk(2)
    c_ay(1).wait_recv()
    c_core(1, 1).start()
    c_ay(3).wait_recv()
    c_core(3, 1).start()
    c_core(3, 0).wait_recv()
    attend_chunk(6)
    t_c.wait_recv()
    pack()
    for d in (1, 2, 3):
        t_z(d).start()
    loop(heads, begin)
    c_b(2).wait_recv()
    c_b(3).wait_recv()
    c_core(2, 0).start()
    c_ay(2).wait_recv()
    c_core(2, 1).start()
    for d in (1, 2, 3):
        t_z(d).wait_recv()
    t_h.start()
    c_core(1, 1).wait_recv()
    attend_chunk(3)
    c_core(3, 1).wait_recv()
    attend_chunk(7)
    c_core(2, 0).wait_recv()
    attend_chunk(4)
    c_core(2, 1).wait_recv()
    attend_chunk(5)
    got_w.wait()
    loop(heads, finish)
    t_h.wait_recv()
    for p in range(4):
        c_a(p).wait_send()
        c_b(p).wait_send()
        c_ay(p).wait_send()
    c_by.wait_send()
    for r in range(1, 8):
        c_core(r // 2, r % 2).wait_send()
    for d in (1, 2, 3):
        t_x(d).wait_send()
        t_z(d).wait_send()
    t_y.wait_send()
    t_c.wait_send()
    t_h.wait_send()


def project_part(heads, load, last, resid, gain, state, normed, w, *reduce_refs):
    pos = place()
    red = Reduce(reduce_refs, pos, True)

    def multiply(n):
        load(n).wait()
        t = jnp.dot(heads[...], w[n], preferred_element_type=F32)
        red.cs[n] = t[:128].astype(BF).reshape(4, 2, 16, W)
        red.c_core(n).start()
        red.own[n] = t[128:].reshape(4, 2, 16, W)

    def step(k):
        @when(k < 4)
        def _():
            multiply(2 * k)
            multiply(2 * k + 1)

        @when((k >= 1) & (k < 5))
        def _():
            red.first(k - 1)

        @when((k >= 2) & (k < 6))
        def _():
            red.second(k - 2)

        @when((k >= 3) & (k < 7))
        def _():
            red.carry(k - 3)

        @when(k >= 4)
        def _():
            red.third(k - 4)

    loop(8, step)
    for cp in last:
        cp.wait()
    square = jnp.zeros((16, 1), F32)
    for n in range(8):
        t = resid[:, n * W:(n + 1) * W].astype(F32) + red.acc[n]
        state[n] = t
        square = square + jnp.sum(t * t, axis=1, keepdims=True)
    scale = lax.rsqrt(square / (8 * W) + 1e-06)
    for n in range(8):
        normed[n] = (state[n] * scale * gain[:, n * W:(n + 1) * W]).astype(BF)
    loop(4, red.drain)


ATTEND_SEMS = [
    DMA((4,)), DMA((4,)), DMA((4,)), DMA((4,)), DMA((4,)), DMA((4,)), DMA, DMA,
    DMA((4, 2)), DMA((4, 2)),
    DMA((3,)), DMA((3,)), DMA, DMA, DMA, DMA, DMA((3,)), DMA((3,)), DMA, DMA,
]


def front_kernel(scale, block_order, queries_hbm, latent_hbm, w_uv_hbm, ids_hbm, weights_hbm, w_hbm, resid_hbm,
                 gain_hbm, state, normed, table, queries, latent, w_uv, ids, weights, resid, gain, heads, w,
                 lsem, wsem, *refs):
    loads = fetch([(latent_hbm, latent), (ids_hbm, ids), (weights_hbm, weights), (queries_hbm, queries),
                   (w_uv_hbm, w_uv), (resid_hbm, resid), (gain_hbm, gain)], lsem)

    def load(n):
        return pltpu.make_async_copy(
            w_hbm.at[:, pl.ds(pl.multiple_of(n * W, W), W)], w.at[n], wsem.at[n]
        )

    loop(8, lambda n: load(n).start())
    count = 8 + len(ATTEND_SEMS)
    attend_part(scale, loads[:5], block_order, queries, latent, w_uv, ids, weights, heads, table, *refs[:count])
    project_part(heads, load, loads[5:], resid, gain, state, normed, w, *refs[count:])


def experts_kernel(normed_hbm, table_hbm, state_hbm, wg_hbm, wd_hbm, out,
                   normed, table, state, lsem, slots, weights, hits, wg, wd, wsem, xb, rows, abuf, fa, la, bbuf, bown, lb1, b2, fb, lb2, a2, la2, suma,
                   acta, actb, yrow, fin, ret, sems, *reduce_refs):
    pos = place()
    z, yh, x, yl, co = pos
    me = z * 2 + yh
    core, ylp, xs = exp_peers(pos)
    yo = (yl + 1) % 2
    yp = dev(z, (yh + 1) % 2, x, yl, co)
    zs = [dev((z + d) % 4, yh, x, yl, co) for d in (1, 2, 3)]
    red = ReduceX(reduce_refs, pos)
    (s_in, r_in, s_gy, r_gy, s_gx, r_gx, s_gc, r_gc,
     s_a1, r_a1, s_b1, r_b1, s_b2, r_b2, s_a2, r_a2, s_ay, r_ay, s_az, r_az, s_bz, r_bz, s_by, r_by,
     s_f, r_f) = sems
    na, nb = a2.shape[1], bown.shape[2]
    n1 = na - 48
    half = nb // 2
    above, below = zs[0], zs[2]

    got_normed, got_table, got_state = fetch(
        [(normed_hbm, normed), (table_hbm, table), (state_hbm, state)], lsem)
    loads = [
        pltpu.make_async_copy(wg_hbm.at[0], wg.at[0], wsem.at[0]),
        pltpu.make_async_copy(wg_hbm.at[1], wg.at[1], wsem.at[1]),
        pltpu.make_async_copy(wd_hbm, wd, wsem.at[2]),
    ]
    for cp in loads:
        cp.start()
    ctx = [dev((z + dz) % 4, (yh + dy) % 2, x, yy, co)
           for dz in range(4) for dy in range(2) for yy in (yl, yo) if dz or dy]
    greet([core, ylp] + xs + ctx)
    got_normed.wait()

    def chunk(dz, dy):
        return ((z + 4 - dz) % 4) * 2 + (yh + dy) % 2

    def c_in(dz, dy):
        zz, yy = (z + dz) % 4, (yh + dy) % 2
        r = dz * 2 + dy
        return put(normed.at[zz * 2 + yy], xb.at[me, co, x, yl], s_in.at[r], r_in.at[r],
                   dev(zz, yy, x, yl, co))

    xb[me, co, x, yl] = normed[me]

    def c_gy(dz, dy):
        zz, yy = (z + dz) % 4, (yh + dy) % 2
        return put(normed.at[zz * 2 + yy], xb.at[me, co, x, yl], s_gy.at[dz, dy], r_gy.at[dz, dy],
                   dev(zz, yy, x, yo, co))

    for dz in (2, 1, 3, 0):
        for dy in range(2):
            if dz or dy:
                c_in(dz, dy).start()
            c_gy(dz, dy).start()

    def c_gx(dz, dy, part):
        c = chunk(dz, dy)
        r = dz * 2 + dy
        src = x if part < 2 else (x + (3 if dy else 1)) % 4
        plus = part == 0 or (part == 2 and dy == 1)
        return put(xb.at[c, co, src], xb.at[c, co, src], s_gx.at[r, part], r_gx.at[r, part], xs[0 if plus else 2])

    def c_gc(dz, dy):
        c = chunk(dz, dy)
        return put(xb.at[c, co], xb.at[c, co], s_gc.at[dz, dy], r_gc.at[dz, dy], core)

    def gather1(dz):
        if dz:
            c_in(dz, 0).wait_recv()
        c_in(dz, 1).wait_recv()

    def gather2(dz):
        for dy in range(2):
            c_gy(dz, dy).wait_recv()
            c_gx(dz, dy, 0).start()
            c_gx(dz, dy, 1).start()

    def gather3(dz):
        for dy in range(2):
            c_gx(dz, dy, 0).wait_recv()
            c_gx(dz, dy, 1).wait_recv()
            c_gx(dz, dy, 2).start()

    def gather4(dz):
        for dy in range(2):
            c_gx(dz, dy, 2).wait_recv()
            c_gc(dz, dy).start()

    def c_far(g, dy):
        return put(abuf.at[g, 2, dy], fa.at[g, dy], s_a1.at[g, 0, dy], r_a1.at[g, 0, dy], above if dy else below)

    def c_below(g, dy):
        return put(abuf.at[g, 1, dy], la.at[g, 0, dy], s_a1.at[g, 1, dy], r_a1.at[g, 1, dy], below)

    def c_above(g, dy):
        return put(abuf.at[g, 3, dy], la.at[g, 1, dy], s_a1.at[g, 2, dy], r_a1.at[g, 2, dy], above)

    def c_b1(g, dz):
        return put(bbuf.at[g, dz], lb1.at[g, dz], s_b1.at[g, dz], r_b1.at[g, dz], yp)

    def part(h):
        return pl.ds(h * half, half)

    def c_bfar(g, h):
        return put(b2.at[g, 2, part(h)], fb.at[g, part(h)], s_b2.at[g, 0, h], r_b2.at[g, 0, h],
                   above if h else below)

    def c_bbelow(g, h):
        return put(b2.at[g, 1, part(h)], lb2.at[g, 0, part(h)], s_b2.at[g, 1, h], r_b2.at[g, 1, h], below)

    def c_babove(g, h):
        return put(b2.at[g, 3, part(h)], lb2.at[g, 1, part(h)], s_b2.at[g, 2, h], r_b2.at[g, 2, h], above)

    def c_a2(g):
        return put(a2.at[g], la2.at[g], s_a2.at[g], r_a2.at[g], yp)

    def c_ay(g):
        return put(acta.at[g, z, yh], acta.at[g, z, yh], s_ay.at[g], r_ay.at[g], yp)

    def c_az(g, p):
        if p < 2:
            src = acta.at[g, z]
        elif p == 2:
            src = acta.at[g, (z + 1) % 4, 0]
        else:
            src = acta.at[g, (z + 3) % 4, 1]
        return put(src, src, s_az.at[g, p], r_az.at[g, p], above if p in (0, 3) else below)

    def c_bz(g, p):
        if p < 2:
            src = actb.at[g, z, yh]
        elif p == 2:
            src = actb.at[g, (z + 1) % 4, yh, part(0)]
        else:
            src = actb.at[g, (z + 3) % 4, yh, part(1)]
        return put(src, src, s_bz.at[g, p], r_bz.at[g, p], above if p in (0, 3) else below)

    def c_by(g, dz):
        zz = (z + 4 - dz) % 4
        return put(actb.at[g, zz, yh], actb.at[g, zz, yh], s_by.at[g, dz], r_by.at[g, dz], yp)

    def find(k):
        for i in range(2):
            mine = table[k, :8, :] == (lax.axis_index("exp") * 2 + i).astype(F32)
            hits[k, i:i + 1, :] = jnp.max(jnp.where(mine, 1.0, 0.0), axis=0, keepdims=True)
            weights[k, i:i + 1, :] = jnp.sum(jnp.where(mine, table[k, 8:, :], 0.0), axis=0, keepdims=True)

    got_table.wait()
    loop(8, find)
    one, two = (lax.broadcasted_iota(jnp.int32, (256, 256), a) for a in (0, 1))
    before = jnp.where((one < two) & (one // 16 == two // 16), 1.0, 0.0).astype(BF)
    block = (lax.broadcasted_iota(jnp.int32, (2, 256), 1) // 16 * 6).astype(F32)

    def rank(k):
        r = jnp.dot(hits[k].astype(BF), before, preferred_element_type=F32)
        slots[k] = jnp.where(hits[k] > 0.5, block + r, -1.0)

    loop(8, rank)
    row_id = lax.broadcasted_iota(jnp.int32, (48, 128), 0).astype(F32)

    def chosen(c, i, g):
        tokens = slice(g * 128, g * 128 + 128)
        return row_id == slots[c, i:i + 1, tokens] - 48.0 * g, weights[c, i:i + 1, tokens]

    def gate_up(dz):
        for dy in range(2):
            c_gc(dz, dy).wait_recv()
            c = chunk(dz, dy)
            for g in range(2):
                tokens = xb[c, g].reshape(128, W)
                for i in range(2):
                    pick = chosen(c, i, g)[0].astype(BF)
                    rows[i, g, dy * 48:(dy + 1) * 48] = jnp.dot(
                        pick, tokens, preferred_element_type=F32).astype(BF)

        def cols(t):
            sl = pl.ds(pl.multiple_of(t * 512, 512), 512)
            r = jnp.dot(rows[0].reshape(192, W), wg[0, :, sl], preferred_element_type=F32)
            abuf[:, dz, :, :48, sl] = r.astype(BF).reshape(2, 2, 48, 512)
            r = jnp.dot(rows[1].reshape(192, W), wg[1, :, sl], preferred_element_type=F32)
            r = r.astype(BF).reshape(2, 2, 48, 512)
            abuf[:, dz, :, 48:, sl] = r[:, :, :n1]
            bown[:, dz, :, sl] = r[:, 0, n1:]
            bbuf[:, dz, :, sl] = r[:, 1, n1:]

        loop(4, cols)

        @when(dz == 2)
        def _():
            c_far(0, 0).start()
            c_far(0, 1).start()

        @when(dz == 1)
        def _():
            c_below(0, 1).start()

        @when(dz == 3)
        def _():
            c_above(0, 0).start()

        c_b1(0, dz).start()

    def carry_a(g):
        for dy, dz, c in ((0, 1, c_below), (1, 3, c_above)):
            c_far(g, dy).wait_recv()

            def cols(t):
                sl = pl.ds(pl.multiple_of(t * 512, 512), 512)
                abuf[g, dz, dy, :, sl] = (abuf[g, dz, dy, :, sl].astype(F32) + fa[g, dy, :, sl].astype(F32)).astype(BF)

            loop(4, cols)
            c(g, dy).start()

    def forward_b(g):
        def one(dz):
            c_b1(g, dz).wait_recv()
            b2[g, dz] = (bown[g, dz].astype(F32) + lb1[g, dz].astype(F32)).astype(BF)

        loop(4, one)
        c_bfar(g, 0).start()
        c_bfar(g, 1).start()
        c_bbelow(g, 1).start()
        c_babove(g, 0).start()

    def carry_b(g):
        for h, dz, c in ((0, 1, c_bbelow), (1, 3, c_babove)):
            c_bfar(g, h).wait_recv()
            b2[g, dz, part(h)] = (b2[g, dz, part(h)].astype(F32) + fb[g, part(h)].astype(F32)).astype(BF)
            c(g, h).start()

    def sum_a(g):
        for dy in range(2):
            c_below(g, dy).wait_recv()
            c_above(g, dy).wait_recv()

        def cols(t):
            sl = pl.ds(pl.multiple_of(t * 512, 512), 512)

            def total(dy):
                r = abuf[g, 0, dy, :, sl].astype(F32)
                return r + la[g, 0, dy, :, sl].astype(F32) + la[g, 1, dy, :, sl].astype(F32)

            a2[g, :, sl] = total(1).astype(BF)
            suma[g, :, sl] = total(0)

        loop(4, cols)
        c_a2(g).start()

    def activate(gate, up):
        return (gate / (1.0 + jnp.exp(-gate)) * up).astype(BF)

    def halves(t):
        return tuple(pl.ds(pl.multiple_of(t * 256 + o, 256), 256) for o in (0, wd.shape[1]))

    def act_a(g):
        c_a2(g).wait_recv()

        def cols(t):
            def total(sl):
                return suma[g, :, sl] + la2[g, :, sl].astype(F32)

            lo, hi = halves(t)
            acta[g, z, yh, :, lo] = activate(total(lo), total(hi))

        loop(4, cols)
        c_ay(g).start()

    def act_b(g):
        for h in range(2):
            c_bbelow(g, h).wait_recv()
            c_babove(g, h).wait_recv()

        def cols(t):
            def total(sl):
                r = b2[g, 0, :, sl].astype(F32)
                return r + lb2[g, 0, :, sl].astype(F32) + lb2[g, 1, :, sl].astype(F32)

            lo, hi = halves(t)
            actb[g, z, yh, :, lo] = activate(total(lo), total(hi))

        loop(4, cols)
        c_bz(g, 0).start()
        c_bz(g, 1).start()
        c_by(g, 0).start()

    def spread_a(g):
        c_ay(g).wait_recv()
        c_az(g, 0).start()
        c_az(g, 1).start()

    def pass_on(g):
        for p in range(2):
            c_bz(g, p).wait_recv()
            c_bz(g, 3 - p).start()
        c_by(g, 1).start()
        c_by(g, 3).start()
        for p in range(2):
            c_az(g, p).wait_recv()
            c_az(g, 3 - p).start()

    def pass_far(g):
        c_bz(g, 2).wait_recv()
        c_bz(g, 3).wait_recv()
        c_by(g, 2).start()

    def order(k):
        return 2 - k + 3 * (k // 2) - 2 * (k // 3)

    for dz in (2, 1, 3, 0):
        gather1(dz)
        gather2(dz)
    gather3(order(0))
    loads[0].wait()
    loads[1].wait()

    def step(k):
        @when(k < 3)
        def _():
            gather3(order(k + 1))

        gather4(order(k))
        gate_up(order(k))

    loop(4, step)

    def nearest(k):
        return k + k // 2 - 2 * (k // 3)

    def down(g, k):
        dz = nearest(k)
        zz = (z + 4 - dz) % 4

        if k == 3:
            c_az(g, 2).wait_recv()
            c_az(g, 3).wait_recv()
        c_by(g, dz).wait_recv()
        yrow[0] = jnp.dot(acta[g, zz, :, :48].reshape(96, -1), wd[0], preferred_element_type=F32).astype(BF)
        one = jnp.concatenate([acta[g, zz, :, 48:], actb[g, zz]], axis=1).reshape(96, -1)
        yrow[1] = jnp.dot(one, wd[1], preferred_element_type=F32).astype(BF)
        for dy in range(2):
            yy = (yh + dy) % 2
            c = zz * 2 + yy
            n = k * 2 + dy
            pick = jnp.concatenate([jnp.where(*chosen(c, i, g), 0.0) for i in range(2)], axis=0).astype(BF)
            sl = pl.ds(pl.multiple_of(yy * 48, 16), 48)
            t = lax.dot_general(
                pick, jnp.concatenate([yrow[0, sl], yrow[1, sl]], axis=0), (((0,), (0,)), ((), ())),
                preferred_element_type=F32).reshape(4, 2, 16, W)

            @when(co == g)
            def _():
                red.own[n] = t

            @when(co != g)
            def _():
                red.cs[n] = t.astype(BF)
                red.c_core(n).start()

    def c_f(k, dy):
        zz, yy = (z + 4 - nearest(k)) % 4, (yh + dy) % 2
        r = k * 2 + dy
        return put(fin.at[r], ret.at[me], s_f.at[r], r_f.at[r], dev(zz, yy, x, yl, co))

    def send_back(k):
        red.third(k)
        for dy in range(2):
            n = k * 2 + dy
            fin[n] = red.acc[n].astype(BF)
            if n:
                c_f(k, dy).start()

    def back(g, *stages):
        @when(co == g)
        def _():
            for stage, k in stages:
                stage(k)

    first, second, carry = red.first, red.second, red.carry
    carry_a(0)
    c_far(1, 0).start()
    c_far(1, 1).start()
    c_below(1, 1).start()
    c_above(1, 0).start()
    for dz in (2, 1, 3, 0):
        c_b1(1, dz).start()
    forward_b(0)
    sum_a(0)
    carry_b(0)
    act_a(0)
    carry_a(1)
    act_b(0)
    spread_a(0)
    forward_b(1)
    sum_a(1)
    carry_b(1)
    loads[2].wait()
    pass_on(0)
    down(0, 0)
    act_a(1)
    back(0, (first, 0))
    act_b(1)
    down(0, 1)
    spread_a(1)
    back(0, (second, 0), (first, 1))
    down(0, 2)
    back(0, (carry, 0), (second, 1), (first, 2))
    pass_far(0)
    down(0, 3)
    pass_on(1)
    down(1, 0)
    back(0, (send_back, 0), (carry, 1), (second, 2), (first, 3))
    back(1, (first, 0))
    down(1, 1)
    back(1, (second, 0), (first, 1))
    down(1, 2)
    back(1, (carry, 0), (second, 1), (first, 2))
    back(0, (send_back, 1), (carry, 2), (second, 3))
    pass_far(1)
    down(1, 3)
    back(1, (first, 3), (send_back, 0), (carry, 1), (second, 2))
    back(0, (send_back, 2), (carry, 3))
    back(1, (second, 3), (send_back, 1), (carry, 2))
    back(1, (carry, 3), (send_back, 2))
    back(1, (send_back, 3))
    back(0, (send_back, 3))
    got_state.wait()
    ret[me] = fin[0]
    for r in range(1, 8):
        c_f(r // 2, r % 2).wait_recv()
    for n in range(8):
        out[:, n * W:(n + 1) * W] = (state[n] + ret[n].astype(F32)).astype(BF)

    loop(4, red.drain)
    for r in range(1, 8):
        c_f(r // 2, r % 2).wait_send()
        c_in(r // 2, r % 2).wait_send()
    for dz in range(4):
        for dy in range(2):
            for p in range(3):
                c_gx(dz, dy, p).wait_send()
            c_gy(dz, dy).wait_send()
            c_gc(dz, dy).wait_send()
        for g in range(2):
            c_b1(g, dz).wait_send()
            c_by(g, dz).wait_send()
    for g in range(2):
        for h in range(2):
            c_far(g, h).wait_send()
            c_below(g, h).wait_send()
            c_above(g, h).wait_send()
            c_bfar(g, h).wait_send()
            c_bbelow(g, h).wait_send()
            c_babove(g, h).wait_send()
        for p in range(4):
            c_az(g, p).wait_send()
            c_bz(g, p).wait_send()
        c_a2(g).wait_send()
        c_ay(g).wait_send()


VM = pl.BlockSpec(memory_space=pltpu.VMEM)
ANY = pl.BlockSpec(memory_space=pl.ANY)


def experts(normed, table, state, w_gate_up, w_down):
    hid2 = w_gate_up.shape[2]
    hid = hid2 // 2
    na, nb = 64, 32
    sems = [
        DMA((8,)), DMA((8,)),
        DMA((4, 2)), DMA((4, 2)), DMA((8, 3)), DMA((8, 3)),
        DMA((4, 2)), DMA((4, 2)),
        DMA((2, 3, 2)), DMA((2, 3, 2)), DMA((2, 4)), DMA((2, 4)), DMA((2, 3, 2)), DMA((2, 3, 2)),
        DMA((2,)), DMA((2,)), DMA((2,)), DMA((2,)), DMA((2, 4)), DMA((2, 4)), DMA((2, 4)), DMA((2, 4)),
        DMA((2, 4)), DMA((2, 4)),
        DMA((8,)), DMA((8,)),
    ]
    return pl.pallas_call(
        experts_kernel,
        name="experts",
        out_shape=jax.ShapeDtypeStruct((16, 8 * W), BF),
        in_specs=[ANY] * 5,
        out_specs=VM,
        scratch_shapes=[
            pltpu.VMEM(normed.shape, BF),
            pltpu.VMEM(table.shape, F32),
            pltpu.VMEM(state.shape, F32),
            DMA((3,)),
            pltpu.VMEM((8, 2, 256), F32),
            pltpu.VMEM((8, 2, 256), F32),
            pltpu.VMEM((8, 2, 256), F32),
            pltpu.VMEM((2, W, hid2), BF),
            pltpu.VMEM((2, hid, W), BF),
            DMA((3,)),
            pltpu.VMEM((8, 2, 4, 2, 16, W), BF),
            pltpu.VMEM((2, 2, 96, W), BF),
            pltpu.VMEM((2, 4, 2, na, hid2), BF),
            pltpu.VMEM((2, 2, na, hid2), BF),
            pltpu.VMEM((2, 2, 2, na, hid2), BF),
            pltpu.VMEM((2, 4, nb, hid2), BF),
            pltpu.VMEM((2, 4, nb, hid2), BF),
            pltpu.VMEM((2, 4, nb, hid2), BF),
            pltpu.VMEM((2, 4, nb, hid2), BF),
            pltpu.VMEM((2, nb, hid2), BF),
            pltpu.VMEM((2, 2, nb, hid2), BF),
            pltpu.VMEM((2, na, hid2), BF),
            pltpu.VMEM((2, na, hid2), BF),
            pltpu.VMEM((2, na, hid2), F32),
            pltpu.VMEM((2, 4, 2, na, hid), BF),
            pltpu.VMEM((2, 4, 2, nb, hid), BF),
            pltpu.VMEM((2, 96, W), BF),
            pltpu.VMEM((8, 16, W), BF),
            pltpu.VMEM((8, 16, W), BF),
            tuple(sems),
        ] + REDUCE_X_SCRATCH,
        compiler_params=pltpu.CompilerParams(
            collective_id=2, has_side_effects=True, vmem_limit_bytes=62 << 20),
    )(normed, table, state, w_gate_up, w_down)


def front(block_order, queries, latent, w_uv, ids, weights, w_out, resid, gain):
    heads_dev, feat_width, query_count = queries.shape
    lat_width, value_width = w_uv.shape[1:]
    score_scale = (value_width + feat_width - lat_width) ** (-0.5)
    return pl.pallas_call(
        functools.partial(front_kernel, score_scale * 1.4426950408889634),
        name="front",
        out_shape=(
            jax.ShapeDtypeStruct((8, 16, W), F32),
            jax.ShapeDtypeStruct((8, 16, W), BF),
            jax.ShapeDtypeStruct((4, 2, 16, 256), F32),
        ),
        in_specs=[pl.BlockSpec(memory_space=pltpu.SMEM)] + [ANY] * 8,
        out_specs=(VM, VM, VM),
        scratch_shapes=[
            pltpu.VMEM(queries.shape, BF),
            pltpu.VMEM(latent.shape, BF),
            pltpu.VMEM(w_uv.shape, BF),
            pltpu.VMEM(ids.shape, jnp.int32),
            pltpu.VMEM(weights.shape, F32),
            pltpu.VMEM(resid.shape, BF),
            pltpu.VMEM(gain.shape, F32),
            pltpu.VMEM((query_count, heads_dev * value_width), BF),
            pltpu.VMEM((8, 768, W), BF),
            DMA((7,)),
            DMA((8,)),
            pltpu.VMEM((4, 2, 2, 128, (feat_width + 127) // 128 * 128), BF),
            pltpu.VMEM((2, 4, 2, 16, 128), BF),
            pltpu.VMEM((heads_dev, query_count, feat_width), BF),
            pltpu.VMEM((heads_dev, query_count, 128), F32),
            pltpu.VMEM((8, heads_dev, query_count, 256), F32),
            pltpu.VMEM((heads_dev, query_count, 128), F32),
            pltpu.VMEM((heads_dev, query_count, 128), F32),
            pltpu.VMEM((heads_dev, query_count, lat_width), F32),
        ] + ATTEND_SEMS + REDUCE_SCRATCH,
        compiler_params=pltpu.CompilerParams(
            collective_id=3, has_side_effects=True, vmem_limit_bytes=62 << 20),
    )(block_order, queries, latent, w_uv, ids, weights, w_out, resid, gain)


def body(queries, latent, block_order, w_uv, w_out, resid, norm_gain, expert_ids, route_weights, w_gate_up, w_down):
    state, normed, table = front(
        block_order, queries.transpose(1, 2, 0), latent.T, w_uv, expert_ids.T, route_weights.T,
        w_out, resid, norm_gain.reshape(1, -1))
    return experts(normed, table.reshape(8, 16, 256), state, w_gate_up, w_down)


def solution(mesh):
    return jax.shard_map(
        body,
        mesh=mesh,
        in_specs=(
            P("ctx", "exp", None),
            P("ctx", None),
            P(),
            P("exp", None, None),
            P("exp", None),
            P(("ctx", "exp"), None),
            P(),
            P(("ctx", "exp"), None),
            P(("ctx", "exp"), None),
            P("exp", "ctx", None),
            P("exp", None, "ctx"),
        ),
        out_specs=P(("ctx", "exp"), None),
        check_vma=False,
    )
```

```python
import functools

import jax
import jax.numpy as jnp
from jax import lax
from jax.experimental import pallas as pl
from jax.experimental.pallas import tpu as pltpu
from jax.sharding import PartitionSpec as P

BF = jnp.bfloat16
F32 = jnp.float32
DMA = pltpu.SemaphoreType.DMA
W = 896


def place():
    c = lax.axis_index("ctx")
    e = lax.axis_index("exp")
    return c // 2, c % 2, e // 4, (e // 2) % 2, e % 2


def dev(z, yh, x, yl, co):
    return (z * 2 + yh, x * 4 + yl * 2 + co)


def put(src, dst, ss, rs, device):
    return pltpu.make_async_remote_copy(
        src_ref=src,
        dst_ref=dst,
        send_sem=ss,
        recv_sem=rs,
        device_id=device,
        device_id_type=pl.DeviceIdType.MESH,
    )


def greet(devices):
    barrier = pltpu.get_barrier_semaphore()
    for d in devices:
        pl.semaphore_signal(barrier, inc=1, device_id=d, device_id_type=pl.DeviceIdType.MESH)
    pl.semaphore_wait(barrier, len(devices))


def exp_peers(pos):
    z, yh, x, yl, co = pos
    core = dev(z, yh, x, yl, (co + 1) % 2)
    ylp = dev(z, yh, x, (yl + 1) % 2, co)
    xs = [dev(z, yh, (x + d) % 4, yl, co) for d in (1, 2, 3)]
    return core, ylp, xs


REDUCE_SCRATCH = [
    pltpu.VMEM((8, 4, 2, 16, W), F32),
    pltpu.VMEM((8, 4, 2, 16, W), BF),
    pltpu.VMEM((8, 4, 2, 16, W), BF),
    pltpu.VMEM((8, 4, 2, 16, W), BF),
    pltpu.VMEM((4, 3, 2, 16, W), BF),
    pltpu.VMEM((4, 2, 16, W), BF),
    pltpu.VMEM((8, 4, 16, W), BF),
    pltpu.VMEM((4, 16, W), BF),
    pltpu.VMEM((8, 3, 16, W), BF),
    pltpu.VMEM((4, 16, W), BF),
    pltpu.VMEM((8, 3, 16, W), BF),
    pltpu.VMEM((8, 16, W), F32),
    DMA((8,)),
    DMA((8,)),
    DMA((4, 3)),
    DMA((4, 3)),
    DMA((8,)),
    DMA((8,)),
    DMA((4,)),
    DMA((4,)),
    DMA((8, 3)),
    DMA((8, 3)),
]


class Reduce:
    def __init__(self, refs, pos, crossed):
        (self.own, self.cs, self.cl, self.s1, self.x1, self.xc, self.y1, self.y2s, self.x2s, self.y2,
         self.x2, self.acc, *self.sems) = refs
        self.pos = pos
        self.crossed = crossed
        self.core, self.ylp, self.xs = exp_peers(pos)

    def c_core(self, n):
        return put(self.cs.at[n], self.cl.at[n], self.sems[0].at[n], self.sems[1].at[n], self.core)

    def c_x1(self, i, part):
        z, yh, x, yl, co = self.pos
        way = 1 + 2 * (i % 2)
        if part == 2:
            src = self.xc.at[i]
        else:
            src = self.s1.at[2 * i, (x + (2 if part == 0 else 4 - way)) % 4]
        to = (x + (4 - way if part == 1 else way)) % 4
        return put(src, self.x1.at[i, part], self.sems[2].at[i, part], self.sems[3].at[i, part],
                   dev(z, yh, to, yl, co))

    def c_y1(self, n):
        return put(self.s1.at[n, :, (self.pos[3] + 1) % 2], self.y1.at[n], self.sems[4].at[n],
                   self.sems[5].at[n], self.ylp)

    def c_y2(self, i):
        return put(self.y2s.at[i], self.y2.at[i], self.sems[6].at[i], self.sems[7].at[i], self.ylp)

    def c_x2(self, n, part, odd):
        plus = (part == 1) == odd
        return put(self.x2s.at[n, part], self.x2.at[n, part], self.sems[8].at[n, part],
                   self.sems[9].at[n, part], self.xs[0 if plus else 2])

    def over_y(self, n, xx):
        return self.s1[n, xx, self.pos[3]].astype(F32) + self.y1[n, xx].astype(F32)

    def first(self, i):
        for j in range(2):
            n = 2 * i + j
            self.c_core(n).wait_recv()
            self.s1[n] = (self.own[n] + self.cl[n].astype(F32)).astype(BF)
            if self.crossed and j == 0:
                self.c_x1(i, 0).start()
                self.c_x1(i, 1).start()
            else:
                self.c_y1(n).start()

    def second(self, i):
        x, yl = self.pos[2], self.pos[3]
        for j in range(2):
            n = 2 * i + j
            if self.crossed and j == 0:
                self.c_x1(i, 0).wait_recv()
                near = (x + 1 + 2 * (i % 2)) % 4
                self.xc[i] = (self.s1[n, near].astype(F32) + self.x1[i, 0].astype(F32)).astype(BF)
                self.c_x1(i, 2).start()
            else:
                self.c_y1(n).wait_recv()
                for part, d in ((0, 2), (1, 1 if j else 3)):
                    self.x2s[n, part] = self.over_y(n, (x + d) % 4).astype(BF)
                    self.c_x2(n, part, j == 1).start()
                self.acc[n] = self.over_y(n, x)

    def carry(self, i):
        for j in range(2):
            n = 2 * i + j
            if self.crossed and j == 0:
                self.c_x1(i, 1).wait_recv()
                self.c_x1(i, 2).wait_recv()

                def over_x(which):
                    t = self.s1[n, self.pos[2], which].astype(F32)
                    return t + self.x1[i, 1, which].astype(F32) + self.x1[i, 2, which].astype(F32)

                self.y2s[i] = over_x((self.pos[3] + 1) % 2).astype(BF)
                self.c_y2(i).start()
                self.acc[n] = over_x(self.pos[3])
            else:
                self.c_x2(n, 0, j == 1).wait_recv()
                xx = (self.pos[2] + (3 if j else 1)) % 4
                self.x2s[n, 2] = (self.over_y(n, xx) + self.x2[n, 0].astype(F32)).astype(BF)
                self.c_x2(n, 2, j == 1).start()

    def third(self, i):
        for j in range(2):
            n = 2 * i + j
            t = self.acc[n]
            if self.crossed and j == 0:
                self.c_y2(i).wait_recv()
                t = t + self.y2[i].astype(F32)
            else:
                for part in (1, 2):
                    self.c_x2(n, part, j == 1).wait_recv()
                    t = t + self.x2[n, part].astype(F32)
            self.acc[n] = t

    def drain(self, i):
        for j in range(2):
            n = 2 * i + j
            self.c_core(n).wait_send()
            if self.crossed and j == 0:
                self.c_y2(i).wait_send()
            else:
                self.c_y1(n).wait_send()
            for d in (1, 2, 3):
                if self.crossed and j == 0:
                    self.c_x1(i, d - 1).wait_send()
                else:
                    self.c_x2(n, d - 1, j == 1).wait_send()


REDUCE_X_SCRATCH = [
    pltpu.VMEM((8, 4, 2, 16, W), F32),
    pltpu.VMEM((8, 4, 2, 16, W), BF),
    pltpu.VMEM((8, 4, 2, 16, W), BF),
    pltpu.VMEM((8, 4, 2, 16, W), BF),
    pltpu.VMEM((8, 2, 16, W), BF),
    pltpu.VMEM((8, 3, 2, 16, W), BF),
    pltpu.VMEM((8, 16, W), BF),
    pltpu.VMEM((8, 16, W), BF),
    pltpu.VMEM((8, 16, W), F32),
    DMA((8,)),
    DMA((8,)),
    DMA((8, 3)),
    DMA((8, 3)),
    DMA((8,)),
    DMA((8,)),
]


class ReduceX:
    def __init__(self, refs, pos):
        (self.own, self.cs, self.cl, self.s1, self.xc, self.xl, self.ys, self.yr, self.acc, *self.sems) = refs
        self.pos = pos
        self.core, self.ylp, self.xs = exp_peers(pos)

    def c_core(self, n):
        return put(self.cs.at[n], self.cl.at[n], self.sems[0].at[n], self.sems[1].at[n], self.core)

    def c_x(self, n, part, odd):
        x = self.pos[2]
        if part == 2:
            src = self.xc.at[n]
        else:
            src = self.s1.at[n, (x + 2) % 4 if part == 0 else (x + (1 if odd else 3)) % 4]
        plus = (part == 1) == odd
        return put(src, self.xl.at[n, part], self.sems[2].at[n, part], self.sems[3].at[n, part],
                   self.xs[0 if plus else 2])

    def c_y(self, n):
        return put(self.ys.at[n], self.yr.at[n], self.sems[4].at[n], self.sems[5].at[n], self.ylp)

    def first(self, i):
        for j in range(2):
            n = 2 * i + j
            self.c_core(n).wait_recv()
            self.s1[n] = (self.own[n] + self.cl[n].astype(F32)).astype(BF)
            self.c_x(n, 0, j == 1).start()
            self.c_x(n, 1, j == 1).start()

    def second(self, i):
        for j in range(2):
            n = 2 * i + j
            self.c_x(n, 0, j == 1).wait_recv()
            near = (self.pos[2] + (3 if j else 1)) % 4
            self.xc[n] = (self.s1[n, near].astype(F32) + self.xl[n, 0].astype(F32)).astype(BF)
            self.c_x(n, 2, j == 1).start()

    def carry(self, i):
        x, yl = self.pos[2], self.pos[3]
        for j in range(2):
            n = 2 * i + j
            self.c_x(n, 1, j == 1).wait_recv()
            self.c_x(n, 2, j == 1).wait_recv()

            def over_x(which):
                t = self.s1[n, x, which].astype(F32)
                return t + self.xl[n, 1, which].astype(F32) + self.xl[n, 2, which].astype(F32)

            self.ys[n] = over_x((yl + 1) % 2).astype(BF)
            self.c_y(n).start()
            self.acc[n] = over_x(yl)

    def third(self, i):
        for j in range(2):
            n = 2 * i + j
            self.c_y(n).wait_recv()
            self.acc[n] = self.acc[n] + self.yr[n].astype(F32)

    def drain(self, i):
        for j in range(2):
            n = 2 * i + j
            self.c_core(n).wait_send()
            self.c_y(n).wait_send()
            for part in range(3):
                self.c_x(n, part, j == 1).wait_send()


def loop(count, step):
    def body(k, carry):
        step(k)
        return carry

    lax.fori_loop(0, count, body, 0)


def when(cond):
    return pl.when(cond)


def fetch(pairs, sems):
    copies = [pltpu.make_async_copy(src, dst, sems.at[i]) for i, (src, dst) in enumerate(pairs)]
    for cp in copies:
        cp.start()
    return copies


def attend_part(scale, loads, block_order, queries, latent, w_uv, ids, weights, out, table,
                  kb, near, qs, top, scores, mid, part, some,
                  s_a, r_a, s_ay, r_ay, s_b, r_b, s_by, r_by, s_c, r_c,
                  s_tx, r_tx, s_ty, r_ty, s_tc, r_tc, s_tz, r_tz, s_th, r_th):
    pos = place()
    z, yh, x, yl, co = pos
    core, ylp, xs = exp_peers(pos)
    yp = dev(z, (yh + 1) % 2, x, yl, co)
    zs = [dev((z + d) % 4, yh, x, yl, co) for d in (1, 2, 3)]
    above, below = zs[0], zs[2]
    feat = latent.shape[0]
    heads = queries.shape[0]
    lat_width = w_uv.shape[1]
    greet([core, ylp, yp] + xs + zs)
    got_latent, got_ids, got_weights, got_queries, got_w = loads

    def c_a(p):
        plane, first, count = ((0, 0, 64), (0, 0, 64), (1, 0, 32), (3, 32, 32))[p]
        src = kb.at[(z + plane) % 4, yh, co, pl.ds(first, count)]
        return put(src, src, s_a.at[p], r_a.at[p], above if p in (0, 3) else below)

    def c_ay(dz):
        src = kb.at[(z + 4 - dz) % 4, yh, co, pl.ds(0, 64)]
        return put(src, src, s_ay.at[dz], r_ay.at[dz], yp)

    def c_b(p):
        if p < 2:
            src = kb.at[z, :, co, pl.ds(64, 64)]
        elif p == 2:
            src = kb.at[(z + 1) % 4, 0, co, pl.ds(64, 64)]
        else:
            src = kb.at[(z + 3) % 4, 1, co, pl.ds(64, 64)]
        return put(src, src, s_b.at[p], r_b.at[p], above if p in (0, 3) else below)

    own = kb.at[z, yh, co, pl.ds(64, 64)]
    c_by = put(own, own, s_by, r_by, yp)

    def c_core(dz, dy):
        src = kb.at[(z + 4 - dz) % 4, (yh + dy) % 2, co]
        return put(src, src, s_c.at[dz, dy], r_c.at[dz, dy], core)

    got_latent.wait()
    kb[z, yh, :, :, feat:] = jnp.zeros((2, 128, kb.shape[4] - feat), BF)
    kb[z, yh, :, :, :feat] = latent[...].T.reshape(2, 128, feat)
    c_a(0).start()
    c_a(1).start()
    c_by.start()
    c_ay(0).start()

    got_ids.wait()
    got_weights.wait()
    near[co, x, yl] = jnp.zeros((16, 128), BF)
    near[co, x, yl, :, :16] = jnp.concatenate([ids[...].astype(F32), weights[...]], axis=0).astype(BF)

    def t_x(d):
        src = near.at[co, x, yl]
        return put(src, src, s_tx.at[d - 1], r_tx.at[d - 1], xs[d - 1])

    def t_z(d):
        src = table.at[z, yh]
        return put(src, src, s_tz.at[d - 1], r_tz.at[d - 1], zs[d - 1])

    t_y = put(near.at[co, :, yl], near.at[co, :, yl], s_ty, r_ty, ylp)
    t_c = put(near.at[co], near.at[co], s_tc, r_tc, core)
    t_h = put(table.at[:, yh], table.at[:, yh], s_th, r_th, yp)
    for d in (1, 2, 3):
        t_x(d).start()

    def pack():
        row = lax.broadcasted_iota(jnp.int32, (128, 256), 0)
        col = lax.broadcasted_iota(jnp.int32, (128, 256), 1)
        t = jnp.zeros((16, 256), F32)
        for i in range(16):
            move = jnp.where((col - row == 16 * i) & (row < 16), 1.0, 0.0).astype(BF)
            t = t + jnp.dot(near[i // 8, i // 2 % 4, i % 2], move, preferred_element_type=F32)
        table[z, yh] = t

    def turn(h):
        qs[h] = queries[h].T

    got_queries.wait()
    loop(heads, turn)
    top[...] = jnp.full(top.shape, -jnp.inf, F32)

    def place_of(c, axis):
        shape = (1, 256) if axis else (256, 1)
        at = lax.broadcasted_iota(jnp.int32, shape, axis)
        return jnp.where(at < 128, block_order[2 * c] * 128 + at, block_order[2 * c + 1] * 128 + (at - 128))

    def attend_chunk(r):
        zz, yy = (z + 4 - r // 2) % 4, (yh + r) % 2
        hidden = jnp.where(place_of(zz * 2 + yy, 1) <= place_of(z * 2 + yh, 0), 0.0, -jnp.inf)
        keys = kb[zz, yy].reshape(256, kb.shape[4])[:, :feat]
        for h in range(heads):
            s = lax.dot_general(qs[h], keys, (((1,), (1,)), ((), ())), preferred_element_type=F32)
            s = s + hidden
            scores[r, h] = s
            top[h] = jnp.maximum(top[h], jnp.maximum(s[:, :128], s[:, 128:]))

    def weigh(h, most, chunks):
        total = jnp.zeros((256, 128), F32)
        value = jnp.zeros((256, lat_width), F32)
        for r in chunks:
            p = jnp.exp2((scores[r, h] - most) * scale)
            total = total + (p[:, :128] + p[:, 128:])
            keys = kb[(z + 4 - r // 2) % 4, (yh + r) % 2].reshape(256, kb.shape[4])[:, :lat_width]
            value = value + jnp.dot(p.astype(BF), keys, preferred_element_type=F32)
        return total, value

    early, late = (0, 1, 2, 6), (3, 7, 4, 5)

    def begin(h):
        most = jnp.max(top[h], axis=1, keepdims=True)
        mid[h] = jnp.broadcast_to(most, mid.shape[1:])
        part[h], some[h] = weigh(h, most, early)

    def finish(h):
        most = jnp.max(top[h], axis=1, keepdims=True)
        fade = jnp.exp2((mid[h, :, :1] - most) * scale)
        total, value = weigh(h, most, late)
        total = jnp.sum(total + part[h] * fade, axis=1, keepdims=True)
        context = ((value + some[h] * fade) / total).astype(BF)
        r = jnp.dot(context, w_uv[h], preferred_element_type=F32).astype(BF)
        cols = pl.ds(pl.multiple_of(h * 128, 128), 128)
        for g in range(16):
            row = (g % 2 + co + 1) % 2 * 128 + g // 2 * 16
            out[pl.ds(pl.multiple_of(row, 16), 16), cols] = r[g * 16:g * 16 + 16]

    c_by.wait_recv()
    c_b(0).start()
    c_b(1).start()
    c_ay(0).wait_recv()
    c_core(0, 1).start()
    c_a(0).wait_recv()
    c_a(3).start()
    c_ay(1).start()
    c_a(1).wait_recv()
    c_a(2).start()
    c_ay(3).start()
    attend_chunk(0)
    for d in (1, 2, 3):
        t_x(d).wait_recv()
    t_y.start()
    c_core(0, 1).wait_recv()
    attend_chunk(1)
    c_b(0).wait_recv()
    c_b(3).start()
    c_core(1, 0).start()
    c_b(1).wait_recv()
    c_b(2).start()
    c_core(3, 0).start()
    c_a(2).wait_recv()
    c_a(3).wait_recv()
    c_ay(2).start()
    t_y.wait_recv()
    t_c.start()
    c_core(1, 0).wait_recv()
    attend_chunk(2)
    c_ay(1).wait_recv()
    c_core(1, 1).start()
    c_ay(3).wait_recv()
    c_core(3, 1).start()
    c_core(3, 0).wait_recv()
    attend_chunk(6)
    t_c.wait_recv()
    pack()
    for d in (1, 2, 3):
        t_z(d).start()
    loop(heads, begin)
    c_b(2).wait_recv()
    c_b(3).wait_recv()
    c_core(2, 0).start()
    c_ay(2).wait_recv()
    c_core(2, 1).start()
    for d in (1, 2, 3):
        t_z(d).wait_recv()
    t_h.start()
    c_core(1, 1).wait_recv()
    attend_chunk(3)
    c_core(3, 1).wait_recv()
    attend_chunk(7)
    c_core(2, 0).wait_recv()
    attend_chunk(4)
    c_core(2, 1).wait_recv()
    attend_chunk(5)
    got_w.wait()
    loop(heads, finish)
    t_h.wait_recv()
    for p in range(4):
        c_a(p).wait_send()
        c_b(p).wait_send()
        c_ay(p).wait_send()
    c_by.wait_send()
    for r in range(1, 8):
        c_core(r // 2, r % 2).wait_send()
    for d in (1, 2, 3):
        t_x(d).wait_send()
        t_z(d).wait_send()
    t_y.wait_send()
    t_c.wait_send()
    t_h.wait_send()


def project_part(heads, load, last, resid, gain, state, normed, w, *reduce_refs):
    pos = place()
    red = Reduce(reduce_refs, pos, True)

    def multiply(n):
        load(n).wait()
        t = jnp.dot(heads[...], w[n], preferred_element_type=F32)
        red.cs[n] = t[:128].astype(BF).reshape(4, 2, 16, W)
        red.c_core(n).start()
        red.own[n] = t[128:].reshape(4, 2, 16, W)

    def step(k):
        @when(k < 4)
        def _():
            multiply(2 * k)
            multiply(2 * k + 1)

        @when((k >= 1) & (k < 5))
        def _():
            red.first(k - 1)

        @when((k >= 2) & (k < 6))
        def _():
            red.second(k - 2)

        @when((k >= 3) & (k < 7))
        def _():
            red.carry(k - 3)

        @when(k >= 4)
        def _():
            red.third(k - 4)

    loop(8, step)
    for cp in last:
        cp.wait()
    square = jnp.zeros((16, 1), F32)
    for n in range(8):
        t = resid[:, n * W:(n + 1) * W].astype(F32) + red.acc[n]
        state[n] = t
        square = square + jnp.sum(t * t, axis=1, keepdims=True)
    scale = lax.rsqrt(square / (8 * W) + 1e-06)
    for n in range(8):
        normed[n] = (state[n] * scale * gain[:, n * W:(n + 1) * W]).astype(BF)
    loop(4, red.drain)


ATTEND_SEMS = [
    DMA((4,)), DMA((4,)), DMA((4,)), DMA((4,)), DMA((4,)), DMA((4,)), DMA, DMA,
    DMA((4, 2)), DMA((4, 2)),
    DMA((3,)), DMA((3,)), DMA, DMA, DMA, DMA, DMA((3,)), DMA((3,)), DMA, DMA,
]


def front_kernel(scale, block_order, queries_hbm, latent_hbm, w_uv_hbm, ids_hbm, weights_hbm, w_hbm, resid_hbm,
                 gain_hbm, state, normed, table, queries, latent, w_uv, ids, weights, resid, gain, heads, w,
                 lsem, wsem, *refs):
    loads = fetch([(latent_hbm, latent), (ids_hbm, ids), (weights_hbm, weights), (queries_hbm, queries),
                   (w_uv_hbm, w_uv), (resid_hbm, resid), (gain_hbm, gain)], lsem)

    def load(n):
        return pltpu.make_async_copy(
            w_hbm.at[:, pl.ds(pl.multiple_of(n * W, W), W)], w.at[n], wsem.at[n]
        )

    loop(8, lambda n: load(n).start())
    count = 8 + len(ATTEND_SEMS)
    attend_part(scale, loads[:5], block_order, queries, latent, w_uv, ids, weights, heads, table, *refs[:count])
    project_part(heads, load, loads[5:], resid, gain, state, normed, w, *refs[count:])


def experts_kernel(normed_hbm, table_hbm, state_hbm, wg_hbm, wd_hbm, out,
                   normed, table, state, lsem, slots, weights, hits, wg, wd, wsem, xb, rows, abuf, fa, la, bbuf, bown, lb1, b2, fb, lb2, a2, la2, suma,
                   acta, actb, yrow, fin, ret, sems, *reduce_refs):
    pos = place()
    z, yh, x, yl, co = pos
    me = z * 2 + yh
    core, ylp, xs = exp_peers(pos)
    yo = (yl + 1) % 2
    yp = dev(z, (yh + 1) % 2, x, yl, co)
    zs = [dev((z + d) % 4, yh, x, yl, co) for d in (1, 2, 3)]
    red = ReduceX(reduce_refs, pos)
    (s_in, r_in, s_gy, r_gy, s_gx, r_gx, s_gc, r_gc,
     s_a1, r_a1, s_b1, r_b1, s_b2, r_b2, s_a2, r_a2, s_ay, r_ay, s_az, r_az, s_bz, r_bz, s_by, r_by,
     s_f, r_f) = sems
    na, nb = a2.shape[1], bown.shape[2]
    n1 = na - 48
    half = nb // 2
    above, below = zs[0], zs[2]

    got_normed, got_table, got_state = fetch(
        [(normed_hbm, normed), (table_hbm, table), (state_hbm, state)], lsem)
    loads = [
        pltpu.make_async_copy(wg_hbm.at[0], wg.at[0], wsem.at[0]),
        pltpu.make_async_copy(wg_hbm.at[1], wg.at[1], wsem.at[1]),
        pltpu.make_async_copy(wd_hbm, wd, wsem.at[2]),
    ]
    for cp in loads:
        cp.start()
    ctx = [dev((z + dz) % 4, (yh + dy) % 2, x, yy, co)
           for dz in range(4) for dy in range(2) for yy in (yl, yo) if dz or dy]
    greet([core, ylp] + xs + ctx)
    got_normed.wait()

    def chunk(dz, dy):
        return ((z + 4 - dz) % 4) * 2 + (yh + dy) % 2

    def c_in(dz, dy):
        zz, yy = (z + dz) % 4, (yh + dy) % 2
        r = dz * 2 + dy
        return put(normed.at[zz * 2 + yy], xb.at[me, co, x, yl], s_in.at[r], r_in.at[r],
                   dev(zz, yy, x, yl, co))

    xb[me, co, x, yl] = normed[me]

    def c_gy(dz, dy):
        zz, yy = (z + dz) % 4, (yh + dy) % 2
        return put(normed.at[zz * 2 + yy], xb.at[me, co, x, yl], s_gy.at[dz, dy], r_gy.at[dz, dy],
                   dev(zz, yy, x, yo, co))

    for dz in (2, 1, 3, 0):
        for dy in range(2):
            if dz or dy:
                c_in(dz, dy).start()
            c_gy(dz, dy).start()

    def c_gx(dz, dy, part):
        c = chunk(dz, dy)
        r = dz * 2 + dy
        src = x if part < 2 else (x + (3 if dy else 1)) % 4
        plus = part == 0 or (part == 2 and dy == 1)
        return put(xb.at[c, co, src], xb.at[c, co, src], s_gx.at[r, part], r_gx.at[r, part], xs[0 if plus else 2])

    def c_gc(dz, dy):
        c = chunk(dz, dy)
        return put(xb.at[c, co], xb.at[c, co], s_gc.at[dz, dy], r_gc.at[dz, dy], core)

    def gather1(dz):
        if dz:
            c_in(dz, 0).wait_recv()
        c_in(dz, 1).wait_recv()

    def gather2(dz):
        for dy in range(2):
            c_gy(dz, dy).wait_recv()
            c_gx(dz, dy, 0).start()
            c_gx(dz, dy, 1).start()

    def gather3(dz):
        for dy in range(2):
            c_gx(dz, dy, 0).wait_recv()
            c_gx(dz, dy, 1).wait_recv()
            c_gx(dz, dy, 2).start()

    def gather4(dz):
        for dy in range(2):
            c_gx(dz, dy, 2).wait_recv()
            c_gc(dz, dy).start()

    def c_far(g, dy):
        return put(abuf.at[g, 2, dy], fa.at[g, dy], s_a1.at[g, 0, dy], r_a1.at[g, 0, dy], above if dy else below)

    def c_below(g, dy):
        return put(abuf.at[g, 1, dy], la.at[g, 0, dy], s_a1.at[g, 1, dy], r_a1.at[g, 1, dy], below)

    def c_above(g, dy):
        return put(abuf.at[g, 3, dy], la.at[g, 1, dy], s_a1.at[g, 2, dy], r_a1.at[g, 2, dy], above)

    def c_b1(g, dz):
        return put(bbuf.at[g, dz], lb1.at[g, dz], s_b1.at[g, dz], r_b1.at[g, dz], yp)

    def part(h):
        return pl.ds(h * half, half)

    def c_bfar(g, h):
        return put(b2.at[g, 2, part(h)], fb.at[g, part(h)], s_b2.at[g, 0, h], r_b2.at[g, 0, h],
                   above if h else below)

    def c_bbelow(g, h):
        return put(b2.at[g, 1, part(h)], lb2.at[g, 0, part(h)], s_b2.at[g, 1, h], r_b2.at[g, 1, h], below)

    def c_babove(g, h):
        return put(b2.at[g, 3, part(h)], lb2.at[g, 1, part(h)], s_b2.at[g, 2, h], r_b2.at[g, 2, h], above)

    def c_a2(g):
        return put(a2.at[g], la2.at[g], s_a2.at[g], r_a2.at[g], yp)

    def c_ay(g):
        return put(acta.at[g, z, yh], acta.at[g, z, yh], s_ay.at[g], r_ay.at[g], yp)

    def c_az(g, p):
        if p < 2:
            src = acta.at[g, z]
        elif p == 2:
            src = acta.at[g, (z + 1) % 4, 0]
        else:
            src = acta.at[g, (z + 3) % 4, 1]
        return put(src, src, s_az.at[g, p], r_az.at[g, p], above if p in (0, 3) else below)

    def c_bz(g, p):
        if p < 2:
            src = actb.at[g, z, yh]
        elif p == 2:
            src = actb.at[g, (z + 1) % 4, yh, part(0)]
        else:
            src = actb.at[g, (z + 3) % 4, yh, part(1)]
        return put(src, src, s_bz.at[g, p], r_bz.at[g, p], above if p in (0, 3) else below)

    def c_by(g, dz):
        zz = (z + 4 - dz) % 4
        return put(actb.at[g, zz, yh], actb.at[g, zz, yh], s_by.at[g, dz], r_by.at[g, dz], yp)

    def find(k):
        for i in range(2):
            mine = table[k, :8, :] == (lax.axis_index("exp") * 2 + i).astype(F32)
            hits[k, i:i + 1, :] = jnp.max(jnp.where(mine, 1.0, 0.0), axis=0, keepdims=True)
            weights[k, i:i + 1, :] = jnp.sum(jnp.where(mine, table[k, 8:, :], 0.0), axis=0, keepdims=True)

    got_table.wait()
    loop(8, find)
    one, two = (lax.broadcasted_iota(jnp.int32, (256, 256), a) for a in (0, 1))
    before = jnp.where((one < two) & (one // 16 == two // 16), 1.0, 0.0).astype(BF)
    block = (lax.broadcasted_iota(jnp.int32, (2, 256), 1) // 16 * 6).astype(F32)

    def rank(k):
        r = jnp.dot(hits[k].astype(BF), before, preferred_element_type=F32)
        slots[k] = jnp.where(hits[k] > 0.5, block + r, -1.0)

    loop(8, rank)
    row_id = lax.broadcasted_iota(jnp.int32, (48, 128), 0).astype(F32)

    def chosen(c, i, g):
        tokens = slice(g * 128, g * 128 + 128)
        return row_id == slots[c, i:i + 1, tokens] - 48.0 * g, weights[c, i:i + 1, tokens]

    def gate_up(dz):
        for dy in range(2):
            c_gc(dz, dy).wait_recv()
            c = chunk(dz, dy)
            for g in range(2):
                tokens = xb[c, g].reshape(128, W)
                for i in range(2):
                    pick = chosen(c, i, g)[0].astype(BF)
                    rows[i, g, dy * 48:(dy + 1) * 48] = jnp.dot(
                        pick, tokens, preferred_element_type=F32).astype(BF)

        def cols(t):
            sl = pl.ds(pl.multiple_of(t * 512, 512), 512)
            r = jnp.dot(rows[0].reshape(192, W), wg[0, :, sl], preferred_element_type=F32)
            abuf[:, dz, :, :48, sl] = r.astype(BF).reshape(2, 2, 48, 512)
            r = jnp.dot(rows[1].reshape(192, W), wg[1, :, sl], preferred_element_type=F32)
            r = r.astype(BF).reshape(2, 2, 48, 512)
            abuf[:, dz, :, 48:, sl] = r[:, :, :n1]
            bown[:, dz, :, sl] = r[:, 0, n1:]
            bbuf[:, dz, :, sl] = r[:, 1, n1:]

        loop(4, cols)

        @when(dz == 2)
        def _():
            c_far(0, 0).start()
            c_far(0, 1).start()

        @when(dz == 1)
        def _():
            c_below(0, 1).start()

        @when(dz == 3)
        def _():
            c_above(0, 0).start()

        c_b1(0, dz).start()
        c_b1(1, dz).start()

    def carry_a(g):
        for dy, dz, c in ((0, 1, c_below), (1, 3, c_above)):
            c_far(g, dy).wait_recv()

            def cols(t):
                sl = pl.ds(pl.multiple_of(t * 512, 512), 512)
                abuf[g, dz, dy, :, sl] = (abuf[g, dz, dy, :, sl].astype(F32) + fa[g, dy, :, sl].astype(F32)).astype(BF)

            loop(4, cols)
            c(g, dy).start()

    def forward_b(g):
        def one(dz):
            c_b1(g, dz).wait_recv()
            b2[g, dz] = (bown[g, dz].astype(F32) + lb1[g, dz].astype(F32)).astype(BF)

        loop(4, one)
        c_bfar(g, 0).start()
        c_bfar(g, 1).start()
        c_bbelow(g, 1).start()
        c_babove(g, 0).start()

    def carry_b(g):
        for h, dz, c in ((0, 1, c_bbelow), (1, 3, c_babove)):
            c_bfar(g, h).wait_recv()
            b2[g, dz, part(h)] = (b2[g, dz, part(h)].astype(F32) + fb[g, part(h)].astype(F32)).astype(BF)
            c(g, h).start()

    def sum_a(g):
        for dy in range(2):
            c_below(g, dy).wait_recv()
            c_above(g, dy).wait_recv()

        def cols(t):
            sl = pl.ds(pl.multiple_of(t * 512, 512), 512)

            def total(dy):
                r = abuf[g, 0, dy, :, sl].astype(F32)
                return r + la[g, 0, dy, :, sl].astype(F32) + la[g, 1, dy, :, sl].astype(F32)

            a2[g, :, sl] = total(1).astype(BF)
            suma[g, :, sl] = total(0)

        loop(4, cols)
        c_a2(g).start()

    def activate(gate, up):
        return (gate / (1.0 + jnp.exp(-gate)) * up).astype(BF)

    def halves(t):
        return tuple(pl.ds(pl.multiple_of(t * 256 + o, 256), 256) for o in (0, wd.shape[1]))

    def act_a(g):
        c_a2(g).wait_recv()

        def cols(t):
            def total(sl):
                return suma[g, :, sl] + la2[g, :, sl].astype(F32)

            lo, hi = halves(t)
            acta[g, z, yh, :, lo] = activate(total(lo), total(hi))

        loop(4, cols)
        c_ay(g).start()

    def act_b(g):
        for h in range(2):
            c_bbelow(g, h).wait_recv()
            c_babove(g, h).wait_recv()

        def cols(t):
            def total(sl):
                r = b2[g, 0, :, sl].astype(F32)
                return r + lb2[g, 0, :, sl].astype(F32) + lb2[g, 1, :, sl].astype(F32)

            lo, hi = halves(t)
            actb[g, z, yh, :, lo] = activate(total(lo), total(hi))

        loop(4, cols)
        c_bz(g, 0).start()
        c_bz(g, 1).start()
        c_by(g, 0).start()

    def spread_a(g):
        c_ay(g).wait_recv()
        c_az(g, 0).start()
        c_az(g, 1).start()

    def pass_on(g):
        for p in range(2):
            c_bz(g, p).wait_recv()
            c_bz(g, 3 - p).start()
        c_by(g, 1).start()
        c_by(g, 3).start()
        for p in range(2):
            c_az(g, p).wait_recv()
            c_az(g, 3 - p).start()

    def pass_far(g):
        c_bz(g, 2).wait_recv()
        c_bz(g, 3).wait_recv()
        c_by(g, 2).start()

    def order(k):
        return 2 - k + 3 * (k // 2) - 2 * (k // 3)

    for dz in (2, 1, 3, 0):
        gather1(dz)
        gather2(dz)
    gather3(order(0))
    loads[0].wait()
    loads[1].wait()

    def step(k):
        @when(k < 3)
        def _():
            gather3(order(k + 1))

        gather4(order(k))
        gate_up(order(k))

    loop(4, step)

    def nearest(k):
        return k + k // 2 - 2 * (k // 3)

    def down(g, k):
        dz = nearest(k)
        zz = (z + 4 - dz) % 4

        if k == 3:
            c_az(g, 2).wait_recv()
            c_az(g, 3).wait_recv()
        c_by(g, dz).wait_recv()
        yrow[0] = jnp.dot(acta[g, zz, :, :48].reshape(96, -1), wd[0], preferred_element_type=F32).astype(BF)
        one = jnp.concatenate([acta[g, zz, :, 48:], actb[g, zz]], axis=1).reshape(96, -1)
        yrow[1] = jnp.dot(one, wd[1], preferred_element_type=F32).astype(BF)
        for dy in range(2):
            yy = (yh + dy) % 2
            c = zz * 2 + yy
            n = k * 2 + dy
            pick = jnp.concatenate([jnp.where(*chosen(c, i, g), 0.0) for i in range(2)], axis=0).astype(BF)
            sl = pl.ds(pl.multiple_of(yy * 48, 16), 48)
            t = lax.dot_general(
                pick, jnp.concatenate([yrow[0, sl], yrow[1, sl]], axis=0), (((0,), (0,)), ((), ())),
                preferred_element_type=F32).reshape(4, 2, 16, W)

            @when(co == g)
            def _():
                red.own[n] = t

            @when(co != g)
            def _():
                red.cs[n] = t.astype(BF)
                red.c_core(n).start()

    def c_f(k, dy):
        zz, yy = (z + 4 - nearest(k)) % 4, (yh + dy) % 2
        r = k * 2 + dy
        return put(fin.at[r], ret.at[me], s_f.at[r], r_f.at[r], dev(zz, yy, x, yl, co))

    def send_back(k):
        red.third(k)
        for dy in range(2):
            n = k * 2 + dy
            fin[n] = red.acc[n].astype(BF)
            if n:
                c_f(k, dy).start()

    def back(g, *stages):
        @when(co == g)
        def _():
            for stage, k in stages:
                stage(k)

    first, second, carry = red.first, red.second, red.carry
    carry_a(0)
    c_far(1, 0).start()
    c_far(1, 1).start()
    c_below(1, 1).start()
    c_above(1, 0).start()
    forward_b(0)
    sum_a(0)
    carry_b(0)
    act_a(0)
    carry_a(1)
    act_b(0)
    spread_a(0)
    forward_b(1)
    sum_a(1)
    carry_b(1)
    loads[2].wait()
    pass_on(0)
    down(0, 0)
    act_a(1)
    back(0, (first, 0))
    act_b(1)
    down(0, 1)
    spread_a(1)
    back(0, (second, 0), (first, 1))
    down(0, 2)
    back(0, (carry, 0), (second, 1), (first, 2))
    pass_far(0)
    down(0, 3)
    pass_on(1)
    down(1, 0)
    back(0, (send_back, 0), (carry, 1), (second, 2), (first, 3))
    back(1, (first, 0))
    down(1, 1)
    back(1, (second, 0), (first, 1))
    down(1, 2)
    back(1, (carry, 0), (second, 1), (first, 2))
    back(0, (send_back, 1), (carry, 2), (second, 3))
    pass_far(1)
    down(1, 3)
    back(1, (first, 3), (send_back, 0), (carry, 1), (second, 2))
    back(0, (send_back, 2), (carry, 3))
    back(1, (second, 3), (send_back, 1), (carry, 2))
    back(1, (carry, 3), (send_back, 2))
    back(1, (send_back, 3))
    back(0, (send_back, 3))
    got_state.wait()
    ret[me] = fin[0]
    for r in range(1, 8):
        c_f(r // 2, r % 2).wait_recv()
    for n in range(8):
        out[:, n * W:(n + 1) * W] = (state[n] + ret[n].astype(F32)).astype(BF)

    loop(4, red.drain)
    for r in range(1, 8):
        c_f(r // 2, r % 2).wait_send()
        c_in(r // 2, r % 2).wait_send()
    for dz in range(4):
        for dy in range(2):
            for p in range(3):
                c_gx(dz, dy, p).wait_send()
            c_gy(dz, dy).wait_send()
            c_gc(dz, dy).wait_send()
        for g in range(2):
            c_b1(g, dz).wait_send()
            c_by(g, dz).wait_send()
    for g in range(2):
        for h in range(2):
            c_far(g, h).wait_send()
            c_below(g, h).wait_send()
            c_above(g, h).wait_send()
            c_bfar(g, h).wait_send()
            c_bbelow(g, h).wait_send()
            c_babove(g, h).wait_send()
        for p in range(4):
            c_az(g, p).wait_send()
            c_bz(g, p).wait_send()
        c_a2(g).wait_send()
        c_ay(g).wait_send()


VM = pl.BlockSpec(memory_space=pltpu.VMEM)
ANY = pl.BlockSpec(memory_space=pl.ANY)


def experts(normed, table, state, w_gate_up, w_down):
    hid2 = w_gate_up.shape[2]
    hid = hid2 // 2
    na, nb = 64, 32
    sems = [
        DMA((8,)), DMA((8,)),
        DMA((4, 2)), DMA((4, 2)), DMA((8, 3)), DMA((8, 3)),
        DMA((4, 2)), DMA((4, 2)),
        DMA((2, 3, 2)), DMA((2, 3, 2)), DMA((2, 4)), DMA((2, 4)), DMA((2, 3, 2)), DMA((2, 3, 2)),
        DMA((2,)), DMA((2,)), DMA((2,)), DMA((2,)), DMA((2, 4)), DMA((2, 4)), DMA((2, 4)), DMA((2, 4)),
        DMA((2, 4)), DMA((2, 4)),
        DMA((8,)), DMA((8,)),
    ]
    return pl.pallas_call(
        experts_kernel,
        name="experts",
        out_shape=jax.ShapeDtypeStruct((16, 8 * W), BF),
        in_specs=[ANY] * 5,
        out_specs=VM,
        scratch_shapes=[
            pltpu.VMEM(normed.shape, BF),
            pltpu.VMEM(table.shape, F32),
            pltpu.VMEM(state.shape, F32),
            DMA((3,)),
            pltpu.VMEM((8, 2, 256), F32),
            pltpu.VMEM((8, 2, 256), F32),
            pltpu.VMEM((8, 2, 256), F32),
            pltpu.VMEM((2, W, hid2), BF),
            pltpu.VMEM((2, hid, W), BF),
            DMA((3,)),
            pltpu.VMEM((8, 2, 4, 2, 16, W), BF),
            pltpu.VMEM((2, 2, 96, W), BF),
            pltpu.VMEM((2, 4, 2, na, hid2), BF),
            pltpu.VMEM((2, 2, na, hid2), BF),
            pltpu.VMEM((2, 2, 2, na, hid2), BF),
            pltpu.VMEM((2, 4, nb, hid2), BF),
            pltpu.VMEM((2, 4, nb, hid2), BF),
            pltpu.VMEM((2, 4, nb, hid2), BF),
            pltpu.VMEM((2, 4, nb, hid2), BF),
            pltpu.VMEM((2, nb, hid2), BF),
            pltpu.VMEM((2, 2, nb, hid2), BF),
            pltpu.VMEM((2, na, hid2), BF),
            pltpu.VMEM((2, na, hid2), BF),
            pltpu.VMEM((2, na, hid2), F32),
            pltpu.VMEM((2, 4, 2, na, hid), BF),
            pltpu.VMEM((2, 4, 2, nb, hid), BF),
            pltpu.VMEM((2, 96, W), BF),
            pltpu.VMEM((8, 16, W), BF),
            pltpu.VMEM((8, 16, W), BF),
            tuple(sems),
        ] + REDUCE_X_SCRATCH,
        compiler_params=pltpu.CompilerParams(
            collective_id=2, has_side_effects=True, vmem_limit_bytes=62 << 20),
    )(normed, table, state, w_gate_up, w_down)


def front(block_order, queries, latent, w_uv, ids, weights, w_out, resid, gain):
    heads_dev, feat_width, query_count = queries.shape
    lat_width, value_width = w_uv.shape[1:]
    score_scale = (value_width + feat_width - lat_width) ** (-0.5)
    return pl.pallas_call(
        functools.partial(front_kernel, score_scale * 1.4426950408889634),
        name="front",
        out_shape=(
            jax.ShapeDtypeStruct((8, 16, W), F32),
            jax.ShapeDtypeStruct((8, 16, W), BF),
            jax.ShapeDtypeStruct((4, 2, 16, 256), F32),
        ),
        in_specs=[pl.BlockSpec(memory_space=pltpu.SMEM)] + [ANY] * 8,
        out_specs=(VM, VM, VM),
        scratch_shapes=[
            pltpu.VMEM(queries.shape, BF),
            pltpu.VMEM(latent.shape, BF),
            pltpu.VMEM(w_uv.shape, BF),
            pltpu.VMEM(ids.shape, jnp.int32),
            pltpu.VMEM(weights.shape, F32),
            pltpu.VMEM(resid.shape, BF),
            pltpu.VMEM(gain.shape, F32),
            pltpu.VMEM((query_count, heads_dev * value_width), BF),
            pltpu.VMEM((8, 768, W), BF),
            DMA((7,)),
            DMA((8,)),
            pltpu.VMEM((4, 2, 2, 128, (feat_width + 127) // 128 * 128), BF),
            pltpu.VMEM((2, 4, 2, 16, 128), BF),
            pltpu.VMEM((heads_dev, query_count, feat_width), BF),
            pltpu.VMEM((heads_dev, query_count, 128), F32),
            pltpu.VMEM((8, heads_dev, query_count, 256), F32),
            pltpu.VMEM((heads_dev, query_count, 128), F32),
            pltpu.VMEM((heads_dev, query_count, 128), F32),
            pltpu.VMEM((heads_dev, query_count, lat_width), F32),
        ] + ATTEND_SEMS + REDUCE_SCRATCH,
        compiler_params=pltpu.CompilerParams(
            collective_id=3, has_side_effects=True, vmem_limit_bytes=62 << 20),
    )(block_order, queries, latent, w_uv, ids, weights, w_out, resid, gain)


def body(queries, latent, block_order, w_uv, w_out, resid, norm_gain, expert_ids, route_weights, w_gate_up, w_down):
    state, normed, table = front(
        block_order, queries.transpose(1, 2, 0), latent.T, w_uv, expert_ids.T, route_weights.T,
        w_out, resid, norm_gain.reshape(1, -1))
    return experts(normed, table.reshape(8, 16, 256), state, w_gate_up, w_down)


def solution(mesh):
    return jax.shard_map(
        body,
        mesh=mesh,
        in_specs=(
            P("ctx", "exp", None),
            P("ctx", None),
            P(),
            P("exp", None, None),
            P("exp", None),
            P(("ctx", "exp"), None),
            P(),
            P(("ctx", "exp"), None),
            P(("ctx", "exp"), None),
            P("exp", "ctx", None),
            P("exp", None, "ctx"),
        ),
        out_specs=P(("ctx", "exp"), None),
        check_vma=False,
    )
```
